256 devices in a mesh: row: 8 (over y_lo, x), col: 32 (over z, y_hi, core).
Axes of the slice: x: 4, y: 4 (y_hi: 2, y_lo: 2; y = y_hi * 2 + y_lo), z: 8, core: 2. Of those that a mesh axis runs over, the one named last changes fastest.
Arguments:
- counts: int32 [2, 16384, 16384], P(None, 'row', 'col'), may hold values from 0 to 199, as said below
- row_embed: float32 [2, 16384, 256], P(None, ('row', 'col')), may hold values from -1.5 to 1.5
- col_embed: float32 [2, 16384, 256], P(None, ('col', 'row')), may hold values from -1.5 to 1.5
- row_marg: int32 [2, 16384], P(None, ('row', 'col')), may hold values from 2000 to 59999
- col_marg: int32 [2, 16384], P(None, ('col', 'row')), may hold values from 2000 to 59999
- row_accum: float32 [2, 16384, 256], P(None, ('row', 'col')), may hold values from 1000 to 100000
- col_accum: float32 [2, 16384, 256], P(None, ('col', 'row')), may hold values from 1000 to 100000
Outputs:
- new_rows: float32 [2, 16384, 256], P(None, ('row', 'col'))
- new_cols: float32 [2, 16384, 256], P(None, ('col', 'row'))
The draws below stay inside these ranges and needn't reach their ends.
Inputs may be any that keep to these rules, and one draw needn't show every extreme that they name: `counts`: about half of the cells are zero.
All inputs are finite; a program needn't handle non-finite values.
Results may differ from the reference program's by a relative error of at most 0.0075.
Values may be sent and summed in bfloat16 or wider, within the bound.
A program may use at most 64 MiB of HBM per device.

```python
import math
import jax
import jax.numpy as jnp
from jax import lax

D = 256
SHARDS = 2
RB = 2048
ROWS = 16384
COLS = 16384


def draw_counts(key, part):
    key = jax.random.fold_in(key, 11)
    first_key, second_key = jax.random.split(key)
    shape = (SHARDS, ROWS, COLS)
    present = jax.random.randint(first_key, shape, 0, 2)
    values = jax.random.randint(second_key, shape, 1, 200)
    return (present * values).astype(jnp.int32)


def with_ends(entries, stream_key, smallest, top_value):
    longest = entries.shape.index(max(entries.shape))
    spots = []
    for shift in (0, 1):
        where = [jax.random.randint(jax.random.fold_in(stream_key, axis), (), 0, length) for axis, length in enumerate(entries.shape)]
        where[longest] = (where[longest] + shift) % entries.shape[longest]
        spots.append(tuple(where))
    return entries.at[spots[0]].set(smallest).at[spots[1]].set(top_value)


def levels(stream_key, shape, cuts, least, top_value):
    def one(position, parts):
        steps = jax.random.uniform(jax.random.fold_in(jax.random.fold_in(stream_key, 6), position), (parts,), jnp.float32, least / len(cuts), top_value / len(cuts))
        return jnp.repeat(jnp.exp(steps), shape[position] // parts).reshape((-1,) + (1,) * (len(shape) - position - 1))

    gain = one(*cuts[0])
    for cut in cuts[1:]:
        gain = gain * one(*cut)
    return gain


def noise(stream_key, shape, spread, most, cuts=(), held_as=jnp.bfloat16):
    loudness = levels(stream_key, shape, cuts, -0.22, 0.18) if cuts else 1.0
    values = jax.random.normal(stream_key, shape, jnp.float32) * spread * loudness
    return jnp.minimum(jnp.maximum(values, -most), most).astype(held_as)


def setup_inputs(seed: int = 0) -> dict:
    key_of = jax.random.split(jax.random.key(seed), 8)
    counts = draw_counts(jax.random.fold_in(key_of[7], 71), 0)
    row_embed = noise(key_of[1], (SHARDS, ROWS, D), 0.25, 1.5, ((1, 256),), jnp.float32)
    col_embed = noise(key_of[2], (SHARDS, COLS, D), 0.25, 1.5, ((1, 256),), jnp.float32)
    row_marg = with_ends(jax.random.randint(key_of[3], (SHARDS, ROWS), 2000, 60000), jax.random.fold_in(key_of[3], 1), 2000, 59999).astype(jnp.int32)
    col_marg = with_ends(jax.random.randint(key_of[4], (SHARDS, COLS), 2000, 60000), jax.random.fold_in(key_of[4], 1), 2000, 59999).astype(jnp.int32)
    row_accum = jnp.clip(jnp.exp(math.log(100000.0) - 4.6051702 * jax.random.uniform(key_of[5], (SHARDS, ROWS, D), jnp.float32) ** levels(key_of[5], (SHARDS, ROWS, D), ((1, 256),), -0.2, 0.2)), 1000.0, 100000.0)
    col_accum = jnp.clip(jnp.exp(math.log(100000.0) - 4.6051702 * jax.random.uniform(key_of[6], (SHARDS, COLS, D), jnp.float32) ** levels(key_of[6], (SHARDS, COLS, D), ((1, 256),), -0.2, 0.2)), 1000.0, 100000.0)
    return dict(counts=counts, row_embed=row_embed, col_embed=col_embed, row_marg=row_marg, col_marg=col_marg, row_accum=row_accum, col_accum=col_accum)


LOG_TOTAL = 20.0
LEARN_RATE = 1.0

def cell_grads(count_block, rows_half, cols_half, row_counts, col_counts):
    scores = jnp.dot(rows_half, cols_half.T, preferred_element_type=jnp.float32)
    pmi_zero = LOG_TOTAL - jnp.log(row_counts.astype(jnp.float32))[:, None] - jnp.log(col_counts.astype(jnp.float32))[None, :]
    counts_real = count_block.astype(jnp.float32)
    pmi_full = jnp.log(jnp.maximum(counts_real, 1.0)) + pmi_zero
    confidence = 0.1 + 0.25 * jnp.sqrt(counts_real)
    return jnp.where(count_block > 0, confidence * (scores - pmi_full), jax.nn.sigmoid(scores - pmi_zero)).astype(jnp.bfloat16)

def adagrad(weights, accum, gradient):
    return weights - LEARN_RATE * gradient / jnp.sqrt(accum + gradient * gradient)

def one_shard(pieces):
    count_tile, row_embed, col_embed, row_marg, col_marg, row_accum, col_accum = pieces
    rows_half = row_embed.astype(jnp.bfloat16)
    cols_half = col_embed.astype(jnp.bfloat16)

    def advance(col_running, block_id):
        offset = (block_id * RB).astype(jnp.int32)
        block = lax.dynamic_slice_in_dim(count_tile, offset, RB, 0)
        rows_block = lax.dynamic_slice_in_dim(rows_half, offset, RB, 0)
        marg_block = lax.dynamic_slice_in_dim(row_marg, offset, RB, 0)
        grads = cell_grads(block, rows_block, cols_half, marg_block, col_marg)
        row_part = jnp.dot(grads, cols_half, preferred_element_type=jnp.float32)
        col_running = col_running + jnp.dot(grads.T, rows_block, preferred_element_type=jnp.float32)
        return (col_running, row_part)
    col_grad, row_parts = lax.scan(advance, jnp.zeros((COLS, D), jnp.float32), jnp.arange(ROWS // RB, dtype=jnp.int32))
    row_grad = row_parts.reshape(ROWS, D)
    return (adagrad(row_embed, row_accum, row_grad), adagrad(col_embed, col_accum, col_grad))

def reference(counts, row_embed, col_embed, row_marg, col_marg, row_accum, col_accum):
    new_rows, new_cols = lax.map(one_shard, (counts, row_embed, col_embed, row_marg, col_marg, row_accum, col_accum))
    return (new_rows, new_cols)
```

```python
import functools

import jax
import jax.numpy as jnp
from jax import lax
from jax.experimental import pallas as pl
from jax.experimental.pallas import tpu as pltpu
from jax.sharding import PartitionSpec as P

MESH = pl.DeviceIdType.MESH
F32 = jnp.float32
BF16 = jnp.bfloat16
NT = (((1,), (1,)), ((), ()))
NN = (((1,), (0,)), ((), ()))
TN = (((0,), (0,)), ((), ()))


def dot(a, b, dims):
    return lax.dot_general(a, b, dims, preferred_element_type=F32)


def adagrad(w, a, g):
    return w - g / jnp.sqrt(a + g * g)


def kernel(
    NZ, XN, B, D, CN,
    counts, re_h, ce_h, rm_h, cm_h, nr, nc,
    re, ce, rm, cm,
    cnt, rows, cols, colsT, RM, CM, LRB, LC, PA, PB, RP, OWN, CPT, CP,
    CS, CR, RSp, RSm, RRp, RRm, YS, YR, VR, Q1s, Q1r, Q2s, Q2r, Q3s, Q3r, VC,
    s_in, s_cnt, s_all, r_a, r_b, r_far, r_core, r_col, r_mz, s_mz, r_mo, s_mo, r_nx, s_nx, r_cr, r_rp, r_rm, r_y, r_q,
):
    H = NZ // 2
    NS = 2
    row = lax.axis_index("row")
    col = lax.axis_index("col")
    x = lax.rem(row, XN)
    yl = row // XN
    z = col // 4
    yh = lax.rem(col // 2, 2)
    c = lax.rem(col, 2)
    oc = 1 - c
    xp = lax.rem(x + 1, XN)
    xm = lax.rem(x + XN - 1, XN)
    x2 = lax.rem(x + 2, XN)
    zp = lax.rem(z + 1, NZ)
    zm = lax.rem(z + NZ - 1, NZ)
    to_core = (row, col + 1 - 2 * c)
    to_yh = (row, col + 2 - 4 * yh)
    to_zp = (row, zp * 4 + yh * 2 + c)
    to_zm = (row, zm * 4 + yh * 2 + c)
    to_yl = ((1 - yl) * XN + x, col)
    to_xp = (yl * XN + xp, col)
    to_xm = (yl * XN + xm, col)
    to_diag = (row, col + 1 - 2 * c + 2 - 4 * yh)
    to_x2 = (yl * XN + x2, col)
    r_own = yl * XN + x
    r_oth = (1 - yl) * XN + x

    def place(r):
        return 0 if r == 0 else 2 * r - 1 if r > 0 or r == -H else -2 * r

    def place_of(r):
        return place(H) if r == -H else place(r)

    def span(d):
        return (2 * d - 1, 2) if 0 < d < H else (place_of(d), 1)

    rel = [0]
    for d in range(1, H):
        rel += [d, -d]
    rel += [H]

    def to_z(r):
        return (row, lax.rem(z + r + NZ, NZ) * 4 + yh * 2 + c)

    small = []
    total = [0]

    def send(src, dst, rsem, dev, blocks):
        pltpu.make_async_remote_copy(
            src_ref=src, dst_ref=dst, send_sem=s_all, recv_sem=rsem, device_id=dev, device_id_type=MESH
        ).start()
        total[0] += blocks

    def send_small(src, dst, ssem, rsem, dev):
        copy = pltpu.make_async_remote_copy(
            src_ref=src, dst_ref=dst, send_sem=ssem, recv_sem=rsem, device_id=dev, device_id_type=MESH
        )
        copy.start()
        small.append(copy)

    def arrive(dst, rsem):
        pltpu.make_async_copy(dst, dst, rsem).wait()

    own_in = [
        pltpu.make_async_copy(src, dst, s_in.at[i])
        for i, (src, dst) in enumerate(((rm_h, rm), (cm_h, cm), (re_h, re), (ce_h, ce)))
    ]
    for copy in own_in:
        copy.start()

    def count_copy(q, r=0):
        zc = lax.rem(z + r + NZ, NZ)
        at = pl.ds(q * 4 * B, 4 * B)
        return pltpu.make_async_copy(counts.at[q // NZ, zc], cnt.at[at], s_cnt.at[q])

    for s in range(NS):
        for p in range(NZ):
            count_copy(s * NZ + p, rel[p]).start()

    for copy in own_in:
        copy.wait()
    for s in range(NS):
        rows[s, 0, yh, c] = re[s].astype(BF16)
        cols[s, r_own] = ce[s].astype(BF16)
    mine_r = jnp.concatenate([rm[0:1, :], rm[1:2, :]], axis=1).astype(F32)
    mine_c = jnp.concatenate([cm[0:1, :], cm[1:2, :]], axis=1).astype(F32)
    RM[0, yh, c] = 0.5 * (jnp.log(mine_r) - 20.0)
    CM[x, yl] = 0.5 * jnp.log(mine_c)

    barrier = pltpu.get_barrier_semaphore()
    partners = [to_core, to_yh, to_diag, to_yl, to_xp, to_xm, to_x2] + [to_z(r) for r in rel[1:]]
    for dev in partners:
        pl.semaphore_signal(barrier, inc=1, device_id=dev, device_id_type=MESH)
    pl.semaphore_wait(barrier, len(partners))

    def send_a(r, up):
        to = place_of(r - 1 if up else r + 1)
        send(rows.at[:, place(r), yh, c], rows.at[:, to, yh, c], r_a.at[to], to_zp if up else to_zm, 2)

    def step_a(d):
        for sign in (-1, 1):
            arrive(rows.at[:, place(sign * d), yh, c], r_a.at[place(sign * d)])
            if d < H - 1 or sign < 0:
                send_a(sign * d, sign < 0)

    def send_b(s, r, up):
        to = place_of(r - 1 if up else r + 1)
        ref, dst = rows.at[s, place(r), 1 - yh, c], rows.at[s, to, 1 - yh, c]
        send(ref, dst, r_b.at[s, to], to_zp if up else to_zm, 1)

    def step_b(s, d):
        for sign in (-1, 1) if d > 0 else (1,):
            arrive(rows.at[s, place(sign * d), 1 - yh, c], r_b.at[s, place(sign * d)])
            if d == 0:
                send_b(s, 0, True)
            if d < H - 1:
                send_b(s, sign * d, sign < 0)

    def far_out():
        arrive(rows.at[:, NZ - 1, yh, c], r_a.at[NZ - 1])
        send(rows.at[:, NZ - 1, yh, c], rows.at[:, NZ - 1, yh, c], r_far, to_yh, 2)

    def far_here():
        arrive(rows.at[:, NZ - 1, 1 - yh, c], r_far)

    def row_core(s, j):
        ref = rows.at[s, pl.ds(2 * j, 2), :, c]
        send(ref, ref, r_core.at[s, j], to_core, 4)

    def core_here(s, j):
        arrive(rows.at[s, pl.ds(2 * j, 2), :, oc], r_core.at[s, j])

    def send_col(r, up):
        send(cols.at[:, r], cols.at[:, r], r_col.at[r], to_xp if up else to_xm, 2)

    def col_here(r):
        arrive(cols.at[:, r], r_col.at[r])

    def margs_out():
        me = RM.at[0, yh, c]
        for i, dev in enumerate((to_core, to_yh, to_diag)):
            send_small(me, me, s_mo.at[i], r_mo.at[i], dev)
        send_small(CM.at[x, yl], CM.at[x, yl], s_nx.at[3], r_nx.at[3], to_yl)

    def margs_x():
        arrive(CM.at[x, 1 - yl], r_nx.at[3])
        for i, dev in enumerate((to_xp, to_xm, to_x2)):
            send_small(CM.at[x], CM.at[x], s_nx.at[i], r_nx.at[i], dev)

    def margs_z():
        arrive(RM.at[0, yh, oc], r_mo.at[0])
        arrive(RM.at[0, 1 - yh, c], r_mo.at[1])
        arrive(RM.at[0, 1 - yh, oc], r_mo.at[2])
        for p in range(1, NZ):
            to = place_of(-rel[p])
            send_small(RM.at[0], RM.at[to], s_mz.at[p], r_mz.at[to], to_z(rel[p]))

    def preps(lo, hi):
        def chunk(q, carry):
            count_copy(q).wait()

            def part(i, carry):
                at = pl.ds(pl.multiple_of(i * 32, 32), 32)
                n = cnt[pl.ds(pl.multiple_of(q * 4 * B + i * 32, 32), 32), :].astype(F32)
                m = jnp.maximum(n, 1.0)
                conf = jnp.where(n > 0, 0.4 + m * lax.rsqrt(m), 0.0)
                PA[q, at, :] = conf
                PB[q, at, :] = 0.5 * conf * jnp.log(m)
                return carry

            return lax.fori_loop(0, 4 * B // 32, part, carry)

        lax.fori_loop(lo, hi, chunk, 0)

    def halves(s, a, b):
        return jnp.concatenate([a[:, s * B : (s + 1) * B], b[:, s * B : (s + 1) * B]], axis=1)

    def col_lines():
        for s in range(NS):
            for j in range(CN // 128):
                a, b = divmod(2 * j, XN), divmod(2 * j + 1, XN)
                LC[s, :, j * 128 : (j + 1) * 128] = halves(s, CM[a[1], a[0]], CM[b[1], b[0]])

    def lift(p):
        for y in range(2):
            for k in range(2):
                wide = jnp.broadcast_to(RM[p, y, k], (128, 2 * B)).T
                for s in range(NS):
                    LRB[s, p, (y * 2 + k) * B : (y * 2 + k + 1) * B, :] = wide[s * B : (s + 1) * B]

    def unit(s, p, k):
        left = rows[s, p].reshape(4 * B, D)
        lr = LRB[s, p]
        t = dot(left, colsT[s], NN) + jnp.concatenate([lr] * (CN // 128), axis=1) + LC[s]
        conf = PA[s * NZ + p]
        g = jnp.where(conf > 0, conf * t - PB[s * NZ + p], jnp.tanh(t) + 1.0).astype(BF16)
        RP[k] = dot(g, cols[s].reshape(CN, D), NN).reshape(2, 2, B, D)
        OWN[s, p] = RP[k, :, c]
        CS[s, p] = RP[k, :, oc].astype(BF16)
        return dot(left.T, g, NN)

    def sums_here(s, j):
        arrive(CR.at[s, pl.ds(2 * j, 2)], r_cr.at[s, j])

    def chip_sum(s, r):
        return OWN[s, place(r)] + CR[s, place(r)].astype(F32)

    def ring(s, d):
        if d > 0:
            sums_here(s, d - 1)
        if d == H:
            v = chip_sum(s, H)
            RSp[s, H - 1, 0] = v[0].astype(BF16)
            send(RSp.at[s, H - 1, 0], RRp.at[s, H - 1, 0], r_rp.at[s, H - 1], to_zp, 1)
            RSm[s, H - 1, 1] = v[1].astype(BF16)
            send(RSm.at[s, H - 1, 1], RRm.at[s, H - 1, 1], r_rm.at[s, H - 1], to_zm, 1)
        elif d > 0:
            for up in (True, False):
                RS, RR, rr, dev = (RSp, RRp, r_rp, to_zp) if up else (RSm, RRm, r_rm, to_zm)
                v = chip_sum(s, d if up else -d)
                if d == H - 1:
                    half = 0 if up else 1
                    arrive(RR.at[s, d, half], rr.at[s, d])
                    RS[s, d - 1, half] = (v[half] + RR[s, d, half].astype(F32)).astype(BF16)
                    RS[s, d - 1, 1 - half] = v[1 - half].astype(BF16)
                else:
                    arrive(RR.at[s, d], rr.at[s, d])
                    RS[s, d - 1] = (v + RR[s, d].astype(F32)).astype(BF16)
                send(RS.at[s, d - 1], RR.at[s, d - 1], rr.at[s, d - 1], dev, 2)
        else:
            v = chip_sum(s, 0)
            arrive(RRp.at[s, 0], r_rp.at[s, 0])
            arrive(RRm.at[s, 0], r_rm.at[s, 0])
            VR[s] = v + RRp[s, 0].astype(F32) + RRm[s, 0].astype(F32)
            YS[s] = VR[s, 1 - yh].astype(BF16)
            send(YS.at[s], YR.at[s], r_y.at[s], to_yh, 1)

    def rows_out(s):
        arrive(YR.at[s], r_y.at[s])
        nr[s] = 0.5 * (VR[s, yh] + YR[s].astype(F32))

    def col_far(s):
        CP[s] = CPT[s].T.reshape(2 * XN, B, D)
        Q1s[s, 0] = CP[s, yl * XN + x2].astype(BF16)
        send(Q1s.at[s, 0], Q1r.at[s, 0], r_q.at[s, 0], to_xp, 1)
        Q1s[s, 1] = CP[s, (1 - yl) * XN + x2].astype(BF16)
        send(Q1s.at[s, 1], Q1r.at[s, 1], r_q.at[s, 1], to_xm, 1)

    def col_near(s):
        arrive(Q1r.at[s, 0], r_q.at[s, 0])
        Q2s[s, 0, 0] = (CP[s, yl * XN + xp] + Q1r[s, 0].astype(F32)).astype(BF16)
        Q2s[s, 0, 1] = CP[s, (1 - yl) * XN + xp].astype(BF16)
        send(Q2s.at[s, 0], Q2r.at[s, 0], r_q.at[s, 2], to_xp, 2)
        arrive(Q1r.at[s, 1], r_q.at[s, 1])
        Q2s[s, 1, 0] = CP[s, yl * XN + xm].astype(BF16)
        Q2s[s, 1, 1] = (CP[s, (1 - yl) * XN + xm] + Q1r[s, 1].astype(F32)).astype(BF16)
        send(Q2s.at[s, 1], Q2r.at[s, 1], r_q.at[s, 3], to_xm, 2)

    def col_own(s):
        arrive(Q2r.at[s, 0], r_q.at[s, 2])
        arrive(Q2r.at[s, 1], r_q.at[s, 3])
        Q3s[s] = (CP[s, r_oth] + Q2r[s, 0, 1].astype(F32) + Q2r[s, 1, 1].astype(F32)).astype(BF16)
        send(Q3s.at[s], Q3r.at[s], r_q.at[s, 4], to_yl, 1)
        VC[s] = CP[s, r_own] + Q2r[s, 0, 0].astype(F32) + Q2r[s, 1, 0].astype(F32)

    def cols_out(s):
        arrive(Q3r.at[s], r_q.at[s, 4])
        nc[s] = 0.5 * (VC[s] + Q3r[s].astype(F32))

    send(rows.at[0, 0, yh, c], rows.at[0, 0, yh, c], r_b.at[0, 0], to_yh, 1)
    send_a(0, True)
    send_a(0, False)
    send(rows.at[1, 0, yh, c], rows.at[1, 0, yh, c], r_b.at[1, 0], to_yh, 1)
    send(cols.at[:, r_own], cols.at[:, r_own], r_col.at[r_own], to_yl, 2)
    send_col(r_own, True)
    send_col(r_own, False)
    margs_out()
    preps(0, 2)
    step_a(1)
    col_here(r_oth)
    send_col(r_oth, True)
    send_col(r_oth, False)
    step_b(0, 0)
    step_b(1, 0)
    margs_x()
    margs_z()
    preps(2, 5)
    step_a(2)
    col_here(yl * XN + xp)
    send_col(yl * XN + xp, False)
    col_here((1 - yl) * XN + xm)
    send_col((1 - yl) * XN + xm, True)
    step_b(0, 1)
    row_core(0, 0)
    preps(5, 8)
    step_b(1, 1)
    step_a(3)
    row_core(1, 0)
    preps(8, 11)
    for i, r in enumerate((xm, xp, x2)):
        arrive(CM.at[r], r_nx.at[i])
    col_lines()
    step_b(0, 2)
    row_core(0, 1)
    col_here((1 - yl) * XN + xp)
    col_here(yl * XN + xm)
    col_here(yl * XN + x2)
    col_here((1 - yl) * XN + x2)
    for s in range(NS):
        colsT[s] = (cols[s].reshape(CN, D).astype(F32) * 0.5).T.astype(BF16)
        CPT[s] = jnp.zeros_like(CPT[s])
    step_b(1, 2)
    row_core(1, 1)
    preps(11, 2 * NZ)

    def before(i):
        if i < H:
            for q in range(max(1, 2 * i), 2 * i + 2):
                arrive(RM.at[q], r_mz.at[q])
            core_here(0, i)
        if i == 1:
            far_out()
            step_b(0, 3)
            row_core(0, 2)
            step_b(1, 3)
            row_core(1, 2)
        if i == 2:
            far_here()
            row_core(0, 3)
            row_core(1, 3)
        if i == H:
            col_far(0)
            ring(0, H)
        if i == H + 1:
            ring(0, 3)
            ring(1, H)
        if i == H + 2:
            col_near(0)
            ring(0, 2)
            ring(1, 3)
        if i == H + 3:
            col_own(0)
            ring(0, 1)
            ring(1, 2)
        if i >= H:
            core_here(1, 2 * H - 1 - i)

    def step(i, carry):
        for k in range(2 * H):
            pl.when(i == k)(functools.partial(before, k))
        s = i // H
        j = i * (1 - s) + (2 * H - 1 - i) * s
        p = 2 * j

        @pl.when(i < H)
        def _():
            lift(p)
            lift(p + 1)

        CPT[s] += unit(s, p, 0) + unit(s, p + 1, 1)
        part = pl.ds(p, 2)
        send(CS.at[s, part], CR.at[s, part], r_cr.at[s, j], to_core, 4 * 2 * H)
        return carry

    lax.fori_loop(0, 2 * H, step, 0)
    col_far(1)
    ring(0, 0)
    ring(1, 1)
    cols_out(0)
    col_near(1)
    for copy in small:
        copy.wait_send()
    rows_out(0)
    ring(1, 0)
    col_own(1)
    rows_out(1)
    cols_out(1)
    n = total[0] * B * D * 2 // (CN * 4)
    arrive(cnt.at[pl.ds(0, n)], s_all)


def local(counts, re, ce, rm, cm, ra, ca, *, NZ, XN):
    S, B, D = re.shape
    CB = counts.shape[2]
    H = NZ // 2
    R = 2 * XN
    counts = counts.reshape(S, NZ, 4 * B, CB)
    vmem = pl.BlockSpec(memory_space=pltpu.VMEM)
    sem = pltpu.SemaphoreType.DMA
    v = pltpu.VMEM
    scratch = [
        v((S, B, D), F32),
        v((S, B, D), F32),
        v((S, B), jnp.int32),
        v((S, B), jnp.int32),
        v((S * NZ * 4 * B, CB), jnp.int32),
        v((S, NZ, 2, 2, B, D), BF16),
        v((S, R, B, D), BF16),
        v((S, D, CB), BF16),
        v((NZ, 2, 2, 1, 2 * B), F32),
        v((XN, 2, 1, 2 * B), F32),
        v((S, NZ, 4 * B, 128), F32),
        v((S, 1, CB), F32),
        v((S * NZ, 4 * B, CB), F32),
        v((S * NZ, 4 * B, CB), F32),
        v((2, 2, 2, B, D), F32),
        v((S, NZ, 2, B, D), F32),
        v((S, D, CB), F32),
        v((S, R, B, D), F32),
        v((S, NZ, 2, B, D), BF16),
        v((S, NZ, 2, B, D), BF16),
        v((S, H, 2, B, D), BF16),
        v((S, H, 2, B, D), BF16),
        v((S, H, 2, B, D), BF16),
        v((S, H, 2, B, D), BF16),
        v((S, B, D), BF16),
        v((S, B, D), BF16),
        v((S, 2, B, D), F32),
        v((S, 2, B, D), BF16),
        v((S, 2, B, D), BF16),
        v((S, 2, 2, B, D), BF16),
        v((S, 2, 2, B, D), BF16),
        v((S, B, D), BF16),
        v((S, B, D), BF16),
        v((S, B, D), F32),
        sem((4,)),
        sem((S * NZ,)),
        sem(()),
        sem((NZ,)),
        sem((S, NZ)),
        sem(()),
        sem((S, H)),
        sem((R,)),
        sem((NZ,)),
        sem((NZ,)),
        sem((3,)),
        sem((3,)),
        sem((4,)),
        sem((4,)),
        sem((S, H)),
        sem((S, H)),
        sem((S, H)),
        sem((S,)),
        sem((S, 5)),
    ]
    gr, gc = pl.pallas_call(
        functools.partial(kernel, NZ, XN, B, D, CB),
        out_shape=(jax.ShapeDtypeStruct((S, B, D), F32), jax.ShapeDtypeStruct((S, B, D), F32)),
        in_specs=[pl.BlockSpec(memory_space=pltpu.HBM)] * 5,
        out_specs=(vmem, vmem),
        scratch_shapes=scratch,
        compiler_params=pltpu.CompilerParams(
            collective_id=0, has_side_effects=True, vmem_limit_bytes=60 * 1024 * 1024
        ),
    )(counts, re, ce, rm, cm)
    return adagrad(re, ra, gr), adagrad(ce, ca, gc)


def solution(mesh):
    return jax.shard_map(
        functools.partial(local, NZ=mesh.shape["col"] // 4, XN=mesh.shape["row"] // 2),
        mesh=mesh,
        in_specs=(
            P(None, "row", "col"),
            P(None, ("row", "col"), None),
            P(None, ("col", "row"), None),
            P(None, ("row", "col")),
            P(None, ("col", "row")),
            P(None, ("row", "col"), None),
            P(None, ("col", "row"), None),
        ),
        out_specs=(P(None, ("row", "col"), None), P(None, ("col", "row"), None)),
        check_vma=False,
    )
```

```python
import functools

import jax
import jax.numpy as jnp
from jax import lax
from jax.experimental import pallas as pl
from jax.experimental.pallas import tpu as pltpu
from jax.sharding import PartitionSpec as P

MESH = pl.DeviceIdType.MESH
F32 = jnp.float32
BF16 = jnp.bfloat16
NT = (((1,), (1,)), ((), ()))
NN = (((1,), (0,)), ((), ()))
TN = (((0,), (0,)), ((), ()))


def dot(a, b, dims):
    return lax.dot_general(a, b, dims, preferred_element_type=F32)


def adagrad(w, a, g):
    return w - g / jnp.sqrt(a + g * g)


def kernel(
    NZ, XN, B, D, CN,
    counts, re_h, ce_h, rm_h, cm_h, nr, nc,
    re, ce, rm, cm,
    cnt, rows, cols, colsT, RM, CM, LRB, LC, PA, PB, RP, OWN, CPT, CP,
    CS, CR, RSp, RSm, RRp, RRm, YS, YR, VR, Q1s, Q1r, Q2s, Q2r, Q3s, Q3r, VC, gr, gc,
    s_in, s_cnt, s_all, s_out, r_row, r_core, r_col, r_mz, s_mz, r_mo, s_mo, r_nx, s_nx, r_cr, r_rp, r_rm, r_y, r_q,
):
    H = NZ // 2
    NS = 2
    row = lax.axis_index("row")
    col = lax.axis_index("col")
    x = lax.rem(row, XN)
    yl = row // XN
    z = col // 4
    yh = lax.rem(col // 2, 2)
    c = lax.rem(col, 2)
    oc = 1 - c
    xp = lax.rem(x + 1, XN)
    xm = lax.rem(x + XN - 1, XN)
    x2 = lax.rem(x + 2, XN)
    zp = lax.rem(z + 1, NZ)
    zm = lax.rem(z + NZ - 1, NZ)
    to_core = (row, col + 1 - 2 * c)
    to_yh = (row, col + 2 - 4 * yh)
    to_zp = (row, zp * 4 + yh * 2 + c)
    to_zm = (row, zm * 4 + yh * 2 + c)
    to_yl = ((1 - yl) * XN + x, col)
    to_xp = (yl * XN + xp, col)
    to_xm = (yl * XN + xm, col)
    to_diag = (row, col + 1 - 2 * c + 2 - 4 * yh)
    to_x2 = (yl * XN + x2, col)
    r_own = yl * XN + x
    r_oth = (1 - yl) * XN + x

    def place(r):
        return 0 if r == 0 else 2 * r - 1 if r > 0 or r == -H else -2 * r

    def place_of(r):
        return place(H) if r == -H else place(r)

    def span(d):
        return (2 * d - 1, 2) if 0 < d < H else (place_of(d), 1)

    rel = [0]
    for d in range(1, H):
        rel += [d, -d]
    rel += [H]

    def to_z(r):
        return (row, lax.rem(z + r + NZ, NZ) * 4 + yh * 2 + c)

    small = []
    total = [0]

    def send(src, dst, rsem, dev, blocks):
        pltpu.make_async_remote_copy(
            src_ref=src, dst_ref=dst, send_sem=s_all, recv_sem=rsem, device_id=dev, device_id_type=MESH
        ).start()
        total[0] += blocks

    def send_small(src, dst, ssem, rsem, dev):
        copy = pltpu.make_async_remote_copy(
            src_ref=src, dst_ref=dst, send_sem=ssem, recv_sem=rsem, device_id=dev, device_id_type=MESH
        )
        copy.start()
        small.append(copy)

    def arrive(dst, rsem):
        pltpu.make_async_copy(dst, dst, rsem).wait()

    own_in = [
        pltpu.make_async_copy(src, dst, s_in.at[i])
        for i, (src, dst) in enumerate(((rm_h, rm), (cm_h, cm), (re_h, re), (ce_h, ce)))
    ]
    for copy in own_in:
        copy.start()

    barrier = pltpu.get_barrier_semaphore()
    partners = [to_core, to_yh, to_diag, to_yl, to_xp, to_xm, to_x2] + [to_z(r) for r in rel[1:]]
    for dev in partners:
        pl.semaphore_signal(barrier, inc=1, device_id=dev, device_id_type=MESH)

    def count_copy(q):
        p = lax.rem(q, NZ)
        d = (p + 1) // 2
        zc = lax.rem(z + NZ + d * (2 * lax.rem(p, 2) - 1), NZ)
        at = pl.ds(pl.multiple_of(q * 4 * B, 4 * B), 4 * B)
        return pltpu.make_async_copy(counts.at[q // NZ, zc], cnt.at[at], s_cnt.at[q])

    AHEAD = 3
    for q in range(AHEAD):
        count_copy(q).start()

    for copy in own_in:
        copy.wait()
    for s in range(NS):
        rows[s, 0, yh, c] = re[s].astype(BF16)
        cols[s, r_own] = ce[s].astype(BF16)
    mine_r = jnp.concatenate([rm[0:1, :], rm[1:2, :]], axis=1).astype(F32)
    mine_c = jnp.concatenate([cm[0:1, :], cm[1:2, :]], axis=1).astype(F32)
    RM[0, yh, c] = 0.5 * (jnp.log(mine_r) - 20.0)
    CM[x, yl] = 0.5 * jnp.log(mine_c)

    pl.semaphore_wait(barrier, len(partners))

    def row_block(s, p, y):
        return rows.at[s, p, 1 - yh if y else yh, c]

    def send_row(s, y, r, up):
        to = place_of(r - 1 if up else r + 1)
        send(row_block(s, place(r), y), row_block(s, to, y), r_row.at[s, to, y], to_zp if up else to_zm, 1)

    def row_here(s, y, r):
        arrive(row_block(s, place_of(r), y), r_row.at[s, place_of(r), y])

    def row_step(s, y, d):
        for sign in (-1, 1):
            row_here(s, y, sign * d)
            if d < H - 1 or (y == 0 and sign < 0):
                send_row(s, y, sign * d, sign < 0)

    def row_y(s):
        row_here(s, 1, 0)
        send_row(s, 1, 0, True)
        send_row(s, 1, 0, False)

    def far_out(s):
        row_here(s, 0, H)
        ref = row_block(s, NZ - 1, 0)
        send(ref, ref, r_row.at[s, NZ - 1, 1], to_yh, 1)

    def far_here(s):
        row_here(s, 1, H)

    def row_core(s, j):
        ref = rows.at[s, pl.ds(2 * j, 2), :, c]
        send(ref, ref, r_core.at[s, j], to_core, 4)

    def core_here(s, j):
        arrive(rows.at[s, pl.ds(2 * j, 2), :, oc], r_core.at[s, j])

    def send_col(r, up):
        send(cols.at[:, r], cols.at[:, r], r_col.at[r], to_xp if up else to_xm, 2)

    def col_here(r):
        arrive(cols.at[:, r], r_col.at[r])

    def margs_out():
        me = RM.at[0, yh, c]
        for i, dev in enumerate((to_core, to_yh, to_diag)):
            send_small(me, me, s_mo.at[i], r_mo.at[i], dev)
        send_small(CM.at[x, yl], CM.at[x, yl], s_nx.at[3], r_nx.at[3], to_yl)

    def margs_x():
        arrive(CM.at[x, 1 - yl], r_nx.at[3])
        for i, dev in enumerate((to_xp, to_xm, to_x2)):
            send_small(CM.at[x], CM.at[x], s_nx.at[i], r_nx.at[i], dev)

    def margs_z():
        arrive(RM.at[0, yh, oc], r_mo.at[0])
        arrive(RM.at[0, 1 - yh, c], r_mo.at[1])
        arrive(RM.at[0, 1 - yh, oc], r_mo.at[2])
        for p in range(1, NZ):
            to = place_of(-rel[p])
            send_small(RM.at[0], RM.at[to], s_mz.at[p], r_mz.at[to], to_z(rel[p]))

    def preps(lo, hi):
        def chunk(q, carry):
            @pl.when(q < NZ)
            def _():
                count_copy(q + NZ).start()

            @pl.when(q + AHEAD < NZ)
            def _():
                count_copy(q + AHEAD).start()

            count_copy(q).wait()

            def part(i, carry):
                at = pl.ds(pl.multiple_of(i * 32, 32), 32)
                n = cnt[pl.ds(pl.multiple_of(q * 4 * B + i * 32, 32), 32), :].astype(F32)
                m = jnp.maximum(n, 1.0)
                conf = jnp.where(n > 0, 0.4 + m * lax.rsqrt(m), 0.0)
                PA[q, at, :] = conf
                PB[q, at, :] = 0.5 * conf * jnp.log(m)
                return carry

            return lax.fori_loop(0, 4 * B // 32, part, carry)

        lax.fori_loop(lo, hi, chunk, 0)

    def halves(s, a, b):
        return jnp.concatenate([a[:, s * B : (s + 1) * B], b[:, s * B : (s + 1) * B]], axis=1)

    def col_lines():
        for s in range(NS):
            for j in range(CN // 128):
                a, b = divmod(2 * j, XN), divmod(2 * j + 1, XN)
                LC[s, :, j * 128 : (j + 1) * 128] = halves(s, CM[a[1], a[0]], CM[b[1], b[0]])

    def lift():
        lines = [RM[p, y, k] for p in range(NZ) for y in range(2) for k in range(2)]
        wide = jnp.concatenate(lines, axis=0).T
        for i in range(4 * NZ):
            p, b = divmod(i, 4)
            for s in range(NS):
                column = wide[s * B : (s + 1) * B, i : i + 1]
                LRB[s, p, b * B : (b + 1) * B, :] = jnp.broadcast_to(column, (B, 128))

    def unit(s, p, k):
        left = rows[s, p].reshape(4 * B, D)
        lr = LRB[s, p]
        t = dot(left, colsT[s], NN) + jnp.concatenate([lr] * (CN // 128), axis=1) + LC[s]
        conf = PA[s * NZ + p]
        g = jnp.where(conf > 0, conf * t - PB[s * NZ + p], jnp.tanh(t) + 1.0).astype(BF16)
        RP[k] = dot(g, cols[s].reshape(CN, D), NN).reshape(2, 2, B, D)
        OWN[s, p] = RP[k, :, c]
        CS[s, p] = RP[k, :, oc].astype(BF16)
        return dot(left.T, g, NN)

    def sums_here(s, j):
        arrive(CR.at[s, pl.ds(2 * j, 2)], r_cr.at[s, j])

    def chip_sum(s, r):
        return OWN[s, place(r)] + CR[s, place(r)].astype(F32)

    def ring(s, d):
        if d > 0:
            sums_here(s, d - 1)
        if d == H:
            v = chip_sum(s, H)
            RSp[s, H - 1, 0] = v[0].astype(BF16)
            send(RSp.at[s, H - 1, 0], RRp.at[s, H - 1, 0], r_rp.at[s, H - 1], to_zp, 1)
            RSm[s, H - 1, 1] = v[1].astype(BF16)
            send(RSm.at[s, H - 1, 1], RRm.at[s, H - 1, 1], r_rm.at[s, H - 1], to_zm, 1)
        elif d > 0:
            for up in (True, False):
                RS, RR, rr, dev = (RSp, RRp, r_rp, to_zp) if up else (RSm, RRm, r_rm, to_zm)
                v = chip_sum(s, d if up else -d)
                if d == H - 1:
                    half = 0 if up else 1
                    arrive(RR.at[s, d, half], rr.at[s, d])
                    RS[s, d - 1, half] = (v[half] + RR[s, d, half].astype(F32)).astype(BF16)
                    RS[s, d - 1, 1 - half] = v[1 - half].astype(BF16)
                else:
                    arrive(RR.at[s, d], rr.at[s, d])
                    RS[s, d - 1] = (v + RR[s, d].astype(F32)).astype(BF16)
                send(RS.at[s, d - 1], RR.at[s, d - 1], rr.at[s, d - 1], dev, 2)
        else:
            v = chip_sum(s, 0)
            arrive(RRp.at[s, 0], r_rp.at[s, 0])
            arrive(RRm.at[s, 0], r_rm.at[s, 0])
            VR[s] = v + RRp[s, 0].astype(F32) + RRm[s, 0].astype(F32)
            YS[s] = VR[s, 1 - yh].astype(BF16)
            send(YS.at[s], YR.at[s], r_y.at[s], to_yh, 1)

    def out_copy(k, s):
        src, dst = ((gr, nr), (gc, nc))[k]
        return pltpu.make_async_copy(src.at[s], dst.at[s], s_out.at[k, s])

    def rows_out(s):
        arrive(YR.at[s], r_y.at[s])
        gr[s] = 0.5 * (VR[s, yh] + YR[s].astype(F32))
        out_copy(0, s).start()

    def col_far(s):
        CP[s] = CPT[s].T.reshape(2 * XN, B, D)
        Q1s[s, 0] = CP[s, yl * XN + x2].astype(BF16)
        send(Q1s.at[s, 0], Q1r.at[s, 0], r_q.at[s, 0], to_xp, 1)
        Q1s[s, 1] = CP[s, (1 - yl) * XN + x2].astype(BF16)
        send(Q1s.at[s, 1], Q1r.at[s, 1], r_q.at[s, 1], to_xm, 1)

    def col_near(s):
        arrive(Q1r.at[s, 0], r_q.at[s, 0])
        Q2s[s, 0, 0] = (CP[s, yl * XN + xp] + Q1r[s, 0].astype(F32)).astype(BF16)
        Q2s[s, 0, 1] = CP[s, (1 - yl) * XN + xp].astype(BF16)
        send(Q2s.at[s, 0], Q2r.at[s, 0], r_q.at[s, 2], to_xp, 2)
        arrive(Q1r.at[s, 1], r_q.at[s, 1])
        Q2s[s, 1, 0] = CP[s, yl * XN + xm].astype(BF16)
        Q2s[s, 1, 1] = (CP[s, (1 - yl) * XN + xm] + Q1r[s, 1].astype(F32)).astype(BF16)
        send(Q2s.at[s, 1], Q2r.at[s, 1], r_q.at[s, 3], to_xm, 2)

    def col_own(s):
        arrive(Q2r.at[s, 0], r_q.at[s, 2])
        arrive(Q2r.at[s, 1], r_q.at[s, 3])
        Q3s[s] = (CP[s, r_oth] + Q2r[s, 0, 1].astype(F32) + Q2r[s, 1, 1].astype(F32)).astype(BF16)
        send(Q3s.at[s], Q3r.at[s], r_q.at[s, 4], to_yl, 1)
        VC[s] = CP[s, r_own] + Q2r[s, 0, 0].astype(F32) + Q2r[s, 1, 0].astype(F32)

    def cols_out(s):
        arrive(Q3r.at[s], r_q.at[s, 4])
        gc[s] = 0.5 * (VC[s] + Q3r[s].astype(F32))
        out_copy(1, s).start()

    for s in range(NS):
        send(row_block(s, 0, 0), row_block(s, 0, 0), r_row.at[s, 0, 1], to_yh, 1)
        send_row(s, 0, 0, True)
        send_row(s, 0, 0, False)
        if s == 0:
            send(cols.at[:, r_own], cols.at[:, r_own], r_col.at[r_own], to_yl, 2)
            send_col(r_own, True)
            send_col(r_own, False)
            margs_out()
    preps(0, 1)
    row_step(0, 0, 1)
    col_here(r_oth)
    send_col(r_oth, True)
    send_col(r_oth, False)
    row_step(1, 0, 1)
    row_y(0)
    margs_x()
    preps(1, 2)
    row_step(0, 0, 2)
    row_y(1)
    margs_z()
    row_step(1, 0, 2)
    col_here(yl * XN + xp)
    send_col(yl * XN + xp, False)
    col_here((1 - yl) * XN + xm)
    send_col((1 - yl) * XN + xm, True)
    preps(2, 4)
    row_step(0, 1, 1)
    row_core(0, 0)
    row_step(0, 0, 3)
    preps(4, 5)
    row_step(1, 0, 3)
    row_step(1, 1, 1)
    row_core(1, 0)
    preps(5, 7)
    row_step(0, 1, 2)
    row_core(0, 1)
    far_out(0)
    preps(7, 8)
    for p in range(1, NZ):
        arrive(RM.at[p], r_mz.at[p])
    lift()
    for i, r in enumerate((xm, xp, x2)):
        arrive(CM.at[r], r_nx.at[i])
    col_lines()
    row_step(1, 1, 2)
    row_core(1, 1)
    col_here((1 - yl) * XN + xp)
    col_here(yl * XN + xm)
    col_here(yl * XN + x2)
    col_here((1 - yl) * XN + x2)

    def turn(s):
        colsT[s] = (cols[s].reshape(CN, D) * 0.5).T
        CPT[s] = jnp.zeros_like(CPT[s])

    turn(0)

    def before(i):
        if i < H:
            if i == 1:
                row_step(0, 1, 3)
                row_core(0, 2)
                far_out(1)
            if i == 2:
                far_here(0)
                row_core(0, 3)
                row_step(1, 1, 3)
                row_core(1, 2)
            if i == 3:
                far_here(1)
                row_core(1, 3)
            core_here(0, i)
            return
        if i == H:
            turn(1)
        preps(2 * NZ - 2 * (i - H) - 2, 2 * NZ - 2 * (i - H))
        core_here(1, 2 * H - 1 - i)
        if i == H:
            col_far(0)
            ring(0, H)
        if i == H + 1:
            ring(0, 3)
            ring(1, H)
        if i == H + 2:
            col_near(0)
            ring(0, 2)
            ring(1, 3)
        if i == H + 3:
            col_own(0)
            ring(0, 1)
            ring(1, 2)

    def step(i, carry):
        for k in range(2 * H):
            pl.when(i == k)(functools.partial(before, k))
        s = i // H
        j = i * (1 - s) + (2 * H - 1 - i) * s
        p = 2 * j
        CPT[s] += unit(s, p, 0) + unit(s, p + 1, 1)
        part = pl.ds(p, 2)
        send(CS.at[s, part], CR.at[s, part], r_cr.at[s, j], to_core, 4 * 2 * H)
        return carry

    lax.fori_loop(0, 2 * H, step, 0)
    col_far(1)
    ring(0, 0)
    ring(1, 1)
    cols_out(0)
    col_near(1)
    for copy in small:
        copy.wait_send()
    rows_out(0)
    ring(1, 0)
    col_own(1)
    cols_out(1)
    rows_out(1)
    for k in range(2):
        for s in range(NS):
            out_copy(k, s).wait()
    n = total[0] * B * D * 2 // (CN * 4)
    arrive(cnt.at[pl.ds(0, n)], s_all)


def local(counts, re, ce, rm, cm, ra, ca, *, NZ, XN):
    S, B, D = re.shape
    CB = counts.shape[2]
    H = NZ // 2
    R = 2 * XN
    counts = counts.reshape(S, NZ, 4 * B, CB)
    sem = pltpu.SemaphoreType.DMA
    v = pltpu.VMEM
    scratch = [
        v((S, B, D), F32),
        v((S, B, D), F32),
        v((S, B), jnp.int32),
        v((S, B), jnp.int32),
        v((S * NZ * 4 * B, CB), jnp.int32),
        v((S, NZ, 2, 2, B, D), BF16),
        v((S, R, B, D), BF16),
        v((S, D, CB), BF16),
        v((NZ, 2, 2, 1, 2 * B), F32),
        v((XN, 2, 1, 2 * B), F32),
        v((S, NZ, 4 * B, 128), F32),
        v((S, 1, CB), F32),
        v((S * NZ, 4 * B, CB), F32),
        v((S * NZ, 4 * B, CB), F32),
        v((2, 2, 2, B, D), F32),
        v((S, NZ, 2, B, D), F32),
        v((S, D, CB), F32),
        v((S, R, B, D), F32),
        v((S, NZ, 2, B, D), BF16),
        v((S, NZ, 2, B, D), BF16),
        v((S, H, 2, B, D), BF16),
        v((S, H, 2, B, D), BF16),
        v((S, H, 2, B, D), BF16),
        v((S, H, 2, B, D), BF16),
        v((S, B, D), BF16),
        v((S, B, D), BF16),
        v((S, 2, B, D), F32),
        v((S, 2, B, D), BF16),
        v((S, 2, B, D), BF16),
        v((S, 2, 2, B, D), BF16),
        v((S, 2, 2, B, D), BF16),
        v((S, B, D), BF16),
        v((S, B, D), BF16),
        v((S, B, D), F32),
        v((S, B, D), F32),
        v((S, B, D), F32),
        sem((4,)),
        sem((S * NZ,)),
        sem(()),
        sem((2, S)),
        sem((S, NZ, 2)),
        sem((S, H)),
        sem((R,)),
        sem((NZ,)),
        sem((NZ,)),
        sem((3,)),
        sem((3,)),
        sem((4,)),
        sem((4,)),
        sem((S, H)),
        sem((S, H)),
        sem((S, H)),
        sem((S,)),
        sem((S, 5)),
    ]
    gr, gc = pl.pallas_call(
        functools.partial(kernel, NZ, XN, B, D, CB),
        out_shape=(jax.ShapeDtypeStruct((S, B, D), F32), jax.ShapeDtypeStruct((S, B, D), F32)),
        in_specs=[pl.BlockSpec(memory_space=pltpu.HBM)] * 5,
        out_specs=(pl.BlockSpec(memory_space=pltpu.HBM),) * 2,
        scratch_shapes=scratch,
        compiler_params=pltpu.CompilerParams(
            collective_id=0, has_side_effects=True, vmem_limit_bytes=60 * 1024 * 1024
        ),
    )(counts, re, ce, rm, cm)
    return adagrad(re, ra, gr), adagrad(ce, ca, gc)


def solution(mesh):
    return jax.shard_map(
        functools.partial(local, NZ=mesh.shape["col"] // 4, XN=mesh.shape["row"] // 2),
        mesh=mesh,
        in_specs=(
            P(None, "row", "col"),
            P(None, ("row", "col"), None),
            P(None, ("col", "row"), None),
            P(None, ("row", "col")),
            P(None, ("col", "row")),
            P(None, ("row", "col"), None),
            P(None, ("col", "row"), None),
        ),
        out_specs=(P(None, ("row", "col"), None), P(None, ("col", "row"), None)),
        check_vma=False,
    )
```

```python
import functools

import jax
import jax.numpy as jnp
from jax import lax
from jax.experimental import pallas as pl
from jax.experimental.pallas import tpu as pltpu
from jax.sharding import PartitionSpec as P

MESH = pl.DeviceIdType.MESH
F32 = jnp.float32
BF16 = jnp.bfloat16
NT = (((1,), (1,)), ((), ()))
NN = (((1,), (0,)), ((), ()))
TN = (((0,), (0,)), ((), ()))


def dot(a, b, dims):
    return lax.dot_general(a, b, dims, preferred_element_type=F32)


def adagrad(w, a, g):
    return w - g / jnp.sqrt(a + g * g)


def kernel(
    NZ, XN, B, D, CN,
    counts, re_h, ce_h, rm_h, cm_h, nr, nc,
    re, ce, rm, cm,
    cnt, rows, cols, colsT, RM, CM, LRB, LC, PA, PB, RP, OWN, CPT, CP,
    CS, CR, RSp, RSm, RRp, RRm, YS, YR, VR, Q1s, Q1r, Q2s, Q2r, Q3s, Q3r, VC, gr, gc,
    s_in, s_cnt, s_all, s_out, r_row, r_core, r_col, r_mz, s_mz, r_mo, s_mo, r_nx, s_nx, r_cr, r_rp, r_rm, r_y, r_q,
):
    H = NZ // 2
    NS = 2
    row = lax.axis_index("row")
    col = lax.axis_index("col")
    x = lax.rem(row, XN)
    yl = row // XN
    z = col // 4
    yh = lax.rem(col // 2, 2)
    c = lax.rem(col, 2)
    oc = 1 - c
    xp = lax.rem(x + 1, XN)
    xm = lax.rem(x + XN - 1, XN)
    x2 = lax.rem(x + 2, XN)
    zp = lax.rem(z + 1, NZ)
    zm = lax.rem(z + NZ - 1, NZ)
    to_core = (row, col + 1 - 2 * c)
    to_yh = (row, col + 2 - 4 * yh)
    to_zp = (row, zp * 4 + yh * 2 + c)
    to_zm = (row, zm * 4 + yh * 2 + c)
    to_yl = ((1 - yl) * XN + x, col)
    to_xp = (yl * XN + xp, col)
    to_xm = (yl * XN + xm, col)
    to_diag = (row, col + 1 - 2 * c + 2 - 4 * yh)
    to_x2 = (yl * XN + x2, col)
    r_own = yl * XN + x
    r_oth = (1 - yl) * XN + x

    def place(r):
        return 0 if r == 0 else 2 * r - 1 if r > 0 or r == -H else -2 * r

    def place_of(r):
        return place(H) if r == -H else place(r)

    def span(d):
        return (2 * d - 1, 2) if 0 < d < H else (place_of(d), 1)

    rel = [0]
    for d in range(1, H):
        rel += [d, -d]
    rel += [H]

    def to_z(r):
        return (row, lax.rem(z + r + NZ, NZ) * 4 + yh * 2 + c)

    small = []
    total = [0]

    def send(src, dst, rsem, dev, blocks):
        pltpu.make_async_remote_copy(
            src_ref=src, dst_ref=dst, send_sem=s_all, recv_sem=rsem, device_id=dev, device_id_type=MESH
        ).start()
        total[0] += blocks

    def send_small(src, dst, ssem, rsem, dev):
        copy = pltpu.make_async_remote_copy(
            src_ref=src, dst_ref=dst, send_sem=ssem, recv_sem=rsem, device_id=dev, device_id_type=MESH
        )
        copy.start()
        small.append(copy)

    def arrive(dst, rsem):
        pltpu.make_async_copy(dst, dst, rsem).wait()

    own_in = [
        pltpu.make_async_copy(src, dst, s_in.at[i])
        for i, (src, dst) in enumerate(((rm_h, rm), (cm_h, cm), (re_h, re), (ce_h, ce)))
    ]
    for copy in own_in:
        copy.start()

    barrier = pltpu.get_barrier_semaphore()
    partners = [to_core, to_yh, to_diag, to_yl, to_xp, to_xm, to_x2] + [to_z(r) for r in rel[1:]]
    for dev in partners:
        pl.semaphore_signal(barrier, inc=1, device_id=dev, device_id_type=MESH)

    def in_turn(u):
        return lax.rem(u // 2, 2) * NZ + u // 4 * 2 + lax.rem(u, 2)

    def count_copy(u):
        q = in_turn(u)
        p = lax.rem(q, NZ)
        d = (p + 1) // 2
        zc = lax.rem(z + NZ + d * (2 * lax.rem(p, 2) - 1), NZ)
        at = pl.ds(pl.multiple_of(q * 4 * B, 4 * B), 4 * B)
        return pltpu.make_async_copy(counts.at[q // NZ, zc], cnt.at[at], s_cnt.at[q])

    AHEAD = 3
    for u in range(AHEAD):
        count_copy(u).start()

    for copy in own_in:
        copy.wait()
    for s in range(NS):
        rows[s, 0, yh, c] = re[s].astype(BF16)
        cols[s, r_own] = ce[s].astype(BF16)
    mine_r = jnp.concatenate([rm[0:1, :], rm[1:2, :]], axis=1).astype(F32)
    mine_c = jnp.concatenate([cm[0:1, :], cm[1:2, :]], axis=1).astype(F32)
    RM[0, yh, c] = 0.5 * (jnp.log(mine_r) - 20.0)
    CM[x, yl] = 0.5 * jnp.log(mine_c)

    pl.semaphore_wait(barrier, len(partners))

    def row_block(s, p, y):
        return rows.at[s, p, 1 - yh if y else yh, c]

    def send_row(s, y, r, up):
        to = place_of(r - 1 if up else r + 1)
        send(row_block(s, place(r), y), row_block(s, to, y), r_row.at[s, to, y], to_zp if up else to_zm, 1)

    def row_here(s, y, r):
        arrive(row_block(s, place_of(r), y), r_row.at[s, place_of(r), y])

    def row_step(s, y, d):
        for sign in (-1, 1):
            row_here(s, y, sign * d)
            if d < H - 1 or (y == 0 and sign < 0):
                send_row(s, y, sign * d, sign < 0)

    def row_y(s):
        row_here(s, 1, 0)
        send_row(s, 1, 0, True)
        send_row(s, 1, 0, False)

    def far_out(s):
        row_here(s, 0, H)
        ref = row_block(s, NZ - 1, 0)
        send(ref, ref, r_row.at[s, NZ - 1, 1], to_yh, 1)

    def far_here(s):
        row_here(s, 1, H)

    def row_core(s, j):
        ref = rows.at[s, pl.ds(2 * j, 2), :, c]
        send(ref, ref, r_core.at[s, j], to_core, 4)

    def core_here(s, j):
        arrive(rows.at[s, pl.ds(2 * j, 2), :, oc], r_core.at[s, j])

    def send_col(r, up):
        send(cols.at[:, r], cols.at[:, r], r_col.at[r], to_xp if up else to_xm, 2)

    def col_here(r):
        arrive(cols.at[:, r], r_col.at[r])

    def margs_out():
        me = RM.at[0, yh, c]
        for i, dev in enumerate((to_core, to_yh, to_diag)):
            send_small(me, me, s_mo.at[i], r_mo.at[i], dev)
        send_small(CM.at[x, yl], CM.at[x, yl], s_nx.at[3], r_nx.at[3], to_yl)

    def margs_x():
        arrive(CM.at[x, 1 - yl], r_nx.at[3])
        for i, dev in enumerate((to_xp, to_xm, to_x2)):
            send_small(CM.at[x], CM.at[x], s_nx.at[i], r_nx.at[i], dev)

    def margs_z():
        arrive(RM.at[0, yh, oc], r_mo.at[0])
        arrive(RM.at[0, 1 - yh, c], r_mo.at[1])
        arrive(RM.at[0, 1 - yh, oc], r_mo.at[2])
        for p in range(1, NZ):
            to = place_of(-rel[p])
            send_small(RM.at[0], RM.at[to], s_mz.at[p], r_mz.at[to], to_z(rel[p]))

    def preps(lo, hi):
        def chunk(u, carry):
            @pl.when(u + AHEAD < NS * NZ)
            def _():
                count_copy(u + AHEAD).start()

            count_copy(u).wait()
            q = in_turn(u)

            def part(i, carry):
                at = pl.ds(pl.multiple_of(i * 32, 32), 32)
                n = cnt[pl.ds(pl.multiple_of(q * 4 * B + i * 32, 32), 32), :].astype(F32)
                m = jnp.maximum(n, 1.0)
                conf = jnp.where(n > 0, 0.4 + m * lax.rsqrt(m), 0.0)
                PA[q, at, :] = conf
                PB[q, at, :] = 0.5 * conf * jnp.log(m)
                return carry

            return lax.fori_loop(0, 4 * B // 32, part, carry)

        lax.fori_loop(lo, hi, chunk, 0)

    def halves(s, a, b):
        return jnp.concatenate([a[:, s * B : (s + 1) * B], b[:, s * B : (s + 1) * B]], axis=1)

    def col_lines():
        for s in range(NS):
            for j in range(CN // 128):
                a, b = divmod(2 * j, XN), divmod(2 * j + 1, XN)
                LC[s, :, j * 128 : (j + 1) * 128] = halves(s, CM[a[1], a[0]], CM[b[1], b[0]])

    def lift():
        lines = [RM[p, y, k] for p in range(NZ) for y in range(2) for k in range(2)]
        wide = jnp.concatenate(lines, axis=0).T
        for i in range(4 * NZ):
            p, b = divmod(i, 4)
            for s in range(NS):
                column = wide[s * B : (s + 1) * B, i : i + 1]
                LRB[s, p, b * B : (b + 1) * B, :] = jnp.broadcast_to(column, (B, 128))

    def unit(s, p, k):
        left = rows[s, p].reshape(4 * B, D)
        lr = LRB[s, p]
        t = dot(left, colsT[s], NN) + jnp.concatenate([lr] * (CN // 128), axis=1) + LC[s]
        conf = PA[s * NZ + p]
        g = jnp.where(conf > 0, conf * t - PB[s * NZ + p], jnp.tanh(t) + 1.0).astype(BF16)
        RP[k] = dot(g, cols[s].reshape(CN, D), NN).reshape(2, 2, B, D)
        OWN[s, p] = RP[k, :, c]
        CS[s, p] = RP[k, :, oc].astype(BF16)
        return dot(left.T, g, NN)

    def sums_here(s, j):
        arrive(CR.at[s, pl.ds(2 * j, 2)], r_cr.at[s, j])

    def chip_sum(s, r):
        return OWN[s, place(r)] + CR[s, place(r)].astype(F32)

    def ring(s, d):
        if d > 0:
            sums_here(s, d - 1)
        if d == H:
            v = chip_sum(s, H)
            RSp[s, H - 1, 0] = v[0].astype(BF16)
            send(RSp.at[s, H - 1, 0], RRp.at[s, H - 1, 0], r_rp.at[s, H - 1], to_zp, 1)
            RSm[s, H - 1, 1] = v[1].astype(BF16)
            send(RSm.at[s, H - 1, 1], RRm.at[s, H - 1, 1], r_rm.at[s, H - 1], to_zm, 1)
        elif d > 0:
            for up in (True, False):
                RS, RR, rr, dev = (RSp, RRp, r_rp, to_zp) if up else (RSm, RRm, r_rm, to_zm)
                v = chip_sum(s, d if up else -d)
                if d == H - 1:
                    half = 0 if up else 1
                    arrive(RR.at[s, d, half], rr.at[s, d])
                    RS[s, d - 1, half] = (v[half] + RR[s, d, half].astype(F32)).astype(BF16)
                    RS[s, d - 1, 1 - half] = v[1 - half].astype(BF16)
                else:
                    arrive(RR.at[s, d], rr.at[s, d])
                    RS[s, d - 1] = (v + RR[s, d].astype(F32)).astype(BF16)
                send(RS.at[s, d - 1], RR.at[s, d - 1], rr.at[s, d - 1], dev, 2)
        else:
            v = chip_sum(s, 0)
            arrive(RRp.at[s, 0], r_rp.at[s, 0])
            arrive(RRm.at[s, 0], r_rm.at[s, 0])
            VR[s] = v + RRp[s, 0].astype(F32) + RRm[s, 0].astype(F32)
            YS[s] = VR[s, 1 - yh].astype(BF16)
            send(YS.at[s], YR.at[s], r_y.at[s], to_yh, 1)

    def out_copy(k, s):
        src, dst = ((gr, nr), (gc, nc))[k]
        return pltpu.make_async_copy(src.at[s], dst.at[s], s_out.at[k, s])

    def rows_out(s):
        arrive(YR.at[s], r_y.at[s])
        gr[s] = 0.5 * (VR[s, yh] + YR[s].astype(F32))
        out_copy(0, s).start()

    def col_far(s):
        CP[s] = CPT[s].T.reshape(2 * XN, B, D)
        Q1s[s, 0] = CP[s, yl * XN + x2].astype(BF16)
        send(Q1s.at[s, 0], Q1r.at[s, 0], r_q.at[s, 0], to_xp, 1)
        Q1s[s, 1] = CP[s, (1 - yl) * XN + x2].astype(BF16)
        send(Q1s.at[s, 1], Q1r.at[s, 1], r_q.at[s, 1], to_xm, 1)

    def col_near(s):
        arrive(Q1r.at[s, 0], r_q.at[s, 0])
        Q2s[s, 0, 0] = (CP[s, yl * XN + xp] + Q1r[s, 0].astype(F32)).astype(BF16)
        Q2s[s, 0, 1] = CP[s, (1 - yl) * XN + xp].astype(BF16)
        send(Q2s.at[s, 0], Q2r.at[s, 0], r_q.at[s, 2], to_xp, 2)
        arrive(Q1r.at[s, 1], r_q.at[s, 1])
        Q2s[s, 1, 0] = CP[s, yl * XN + xm].astype(BF16)
        Q2s[s, 1, 1] = (CP[s, (1 - yl) * XN + xm] + Q1r[s, 1].astype(F32)).astype(BF16)
        send(Q2s.at[s, 1], Q2r.at[s, 1], r_q.at[s, 3], to_xm, 2)

    def col_own(s):
        arrive(Q2r.at[s, 0], r_q.at[s, 2])
        arrive(Q2r.at[s, 1], r_q.at[s, 3])
        Q3s[s] = (CP[s, r_oth] + Q2r[s, 0, 1].astype(F32) + Q2r[s, 1, 1].astype(F32)).astype(BF16)
        send(Q3s.at[s], Q3r.at[s], r_q.at[s, 4], to_yl, 1)
        VC[s] = CP[s, r_own] + Q2r[s, 0, 0].astype(F32) + Q2r[s, 1, 0].astype(F32)

    def cols_out(s):
        arrive(Q3r.at[s], r_q.at[s, 4])
        gc[s] = 0.5 * (VC[s] + Q3r[s].astype(F32))
        out_copy(1, s).start()

    for s in range(NS):
        send(row_block(s, 0, 0), row_block(s, 0, 0), r_row.at[s, 0, 1], to_yh, 1)
        send_row(s, 0, 0, True)
        send_row(s, 0, 0, False)
        if s == 0:
            send(cols.at[:, r_own], cols.at[:, r_own], r_col.at[r_own], to_yl, 2)
            send_col(r_own, True)
            send_col(r_own, False)
            margs_out()
    preps(0, 1)
    row_step(0, 0, 1)
    col_here(r_oth)
    send_col(r_oth, True)
    send_col(r_oth, False)
    row_step(1, 0, 1)
    row_y(0)
    margs_x()
    preps(1, 2)
    row_step(0, 0, 2)
    row_y(1)
    margs_z()
    row_step(1, 0, 2)
    col_here(yl * XN + xp)
    send_col(yl * XN + xp, False)
    col_here((1 - yl) * XN + xm)
    send_col((1 - yl) * XN + xm, True)
    preps(2, 4)
    row_step(0, 1, 1)
    row_core(0, 0)
    row_step(0, 0, 3)
    preps(4, 5)
    row_step(1, 0, 3)
    row_step(1, 1, 1)
    row_core(1, 0)
    preps(5, 8)
    row_step(0, 1, 2)
    row_core(0, 1)
    far_out(0)
    preps(8, 10)
    for p in range(1, NZ):
        arrive(RM.at[p], r_mz.at[p])
    lift()
    for i, r in enumerate((xm, xp, x2)):
        arrive(CM.at[r], r_nx.at[i])
    col_lines()
    row_step(1, 1, 2)
    row_core(1, 1)
    col_here((1 - yl) * XN + xp)
    col_here(yl * XN + xm)
    col_here(yl * XN + x2)
    col_here((1 - yl) * XN + x2)

    def turn(s):
        colsT[s] = (cols[s].reshape(CN, D) * 0.5).T
        CPT[s] = jnp.zeros_like(CPT[s])

    turn(0)
    turn(1)

    def before(i):
        if i == 1:
            row_step(0, 1, 3)
            row_core(0, 2)
            far_out(1)
        if i == 2:
            preps(10, 12)
        if i == 3:
            far_here(0)
            row_core(0, 3)
            row_step(1, 1, 3)
            row_core(1, 2)
            preps(12, 14)
        if i == 4:
            far_here(1)
            row_core(1, 3)
        if i == 5:
            preps(14, 16)
        core_here(i % 2, i // 2)

    def step(i, carry):
        for k in range(2 * H):
            pl.when(i == k)(functools.partial(before, k))
        s = lax.rem(i, 2)
        j = i // 2
        p = 2 * j
        CPT[s] += unit(s, p, 0) + unit(s, p + 1, 1)
        part = pl.ds(p, 2)
        send(CS.at[s, part], CR.at[s, part], r_cr.at[s, j], to_core, 4 * 2 * H)
        return carry

    lax.fori_loop(0, 2 * H, step, 0)
    ring(0, H)
    col_far(0)
    ring(1, H)
    col_far(1)
    ring(0, 3)
    ring(1, 3)
    col_near(0)
    col_near(1)
    ring(0, 2)
    ring(1, 2)
    col_own(0)
    col_own(1)
    ring(0, 1)
    ring(1, 1)
    cols_out(0)
    cols_out(1)
    for copy in small:
        copy.wait_send()
    ring(0, 0)
    ring(1, 0)
    rows_out(0)
    rows_out(1)
    for k in range(2):
        for s in range(NS):
            out_copy(k, s).wait()
    n = total[0] * B * D * 2 // (CN * 4)
    arrive(cnt.at[pl.ds(0, n)], s_all)


def local(counts, re, ce, rm, cm, ra, ca, *, NZ, XN):
    S, B, D = re.shape
    CB = counts.shape[2]
    H = NZ // 2
    R = 2 * XN
    counts = counts.reshape(S, NZ, 4 * B, CB)
    sem = pltpu.SemaphoreType.DMA
    v = pltpu.VMEM
    scratch = [
        v((S, B, D), F32),
        v((S, B, D), F32),
        v((S, B), jnp.int32),
        v((S, B), jnp.int32),
        v((S * NZ * 4 * B, CB), jnp.int32),
        v((S, NZ, 2, 2, B, D), BF16),
        v((S, R, B, D), BF16),
        v((S, D, CB), BF16),
        v((NZ, 2, 2, 1, 2 * B), F32),
        v((XN, 2, 1, 2 * B), F32),
        v((S, NZ, 4 * B, 128), F32),
        v((S, 1, CB), F32),
        v((S * NZ, 4 * B, CB), F32),
        v((S * NZ, 4 * B, CB), F32),
        v((2, 2, 2, B, D), F32),
        v((S, NZ, 2, B, D), F32),
        v((S, D, CB), F32),
        v((S, R, B, D), F32),
        v((S, NZ, 2, B, D), BF16),
        v((S, NZ, 2, B, D), BF16),
        v((S, H, 2, B, D), BF16),
        v((S, H, 2, B, D), BF16),
        v((S, H, 2, B, D), BF16),
        v((S, H, 2, B, D), BF16),
        v((S, B, D), BF16),
        v((S, B, D), BF16),
        v((S, 2, B, D), F32),
        v((S, 2, B, D), BF16),
        v((S, 2, B, D), BF16),
        v((S, 2, 2, B, D), BF16),
        v((S, 2, 2, B, D), BF16),
        v((S, B, D), BF16),
        v((S, B, D), BF16),
        v((S, B, D), F32),
        v((S, B, D), F32),
        v((S, B, D), F32),
        sem((4,)),
        sem((S * NZ,)),
        sem(()),
        sem((2, S)),
        sem((S, NZ, 2)),
        sem((S, H)),
        sem((R,)),
        sem((NZ,)),
        sem((NZ,)),
        sem((3,)),
        sem((3,)),
        sem((4,)),
        sem((4,)),
        sem((S, H)),
        sem((S, H)),
        sem((S, H)),
        sem((S,)),
        sem((S, 5)),
    ]
    gr, gc = pl.pallas_call(
        functools.partial(kernel, NZ, XN, B, D, CB),
        out_shape=(jax.ShapeDtypeStruct((S, B, D), F32), jax.ShapeDtypeStruct((S, B, D), F32)),
        in_specs=[pl.BlockSpec(memory_space=pltpu.HBM)] * 5,
        out_specs=(pl.BlockSpec(memory_space=pltpu.HBM),) * 2,
        scratch_shapes=scratch,
        compiler_params=pltpu.CompilerParams(
            collective_id=0, has_side_effects=True, vmem_limit_bytes=60 * 1024 * 1024
        ),
    )(counts, re, ce, rm, cm)
    return adagrad(re, ra, gr), adagrad(ce, ca, gc)


def solution(mesh):
    return jax.shard_map(
        functools.partial(local, NZ=mesh.shape["col"] // 4, XN=mesh.shape["row"] // 2),
        mesh=mesh,
        in_specs=(
            P(None, "row", "col"),
            P(None, ("row", "col"), None),
            P(None, ("col", "row"), None),
            P(None, ("row", "col")),
            P(None, ("col", "row")),
            P(None, ("row", "col"), None),
            P(None, ("col", "row"), None),
        ),
        out_specs=(P(None, ("row", "col"), None), P(None, ("col", "row"), None)),
        check_vma=False,
    )
```

```python
import functools

import jax
import jax.numpy as jnp
from jax import lax
from jax.experimental import pallas as pl
from jax.experimental.pallas import tpu as pltpu
from jax.sharding import PartitionSpec as P

MESH = pl.DeviceIdType.MESH
F32 = jnp.float32
BF16 = jnp.bfloat16
NT = (((1,), (1,)), ((), ()))
NN = (((1,), (0,)), ((), ()))
TN = (((0,), (0,)), ((), ()))


def dot(a, b, dims):
    return lax.dot_general(a, b, dims, preferred_element_type=F32)


def adagrad(w, a, g):
    return w - g / jnp.sqrt(a + g * g)


def kernel(
    NZ, XN, B, D, CN,
    counts, re_h, ce_h, rm_h, cm_h, nr, nc,
    re, ce, rm, cm,
    cnt, rows, cols, colsT, colsC, LRB, LC, PA, PB, RP, OWN, CPT, CP,
    CS, CR, RSp, RSm, RRp, RRm, YS, YR, VR, Q1s, Q1r, Q2s, Q2r, Q3s, Q3r, VC, gr, gc,
    s_in, s_cnt, s_all, s_out, r_row, r_core, r_col, r_cr, r_rp, r_rm, r_y, r_q,
):
    H = NZ // 2
    NS = 2
    row = lax.axis_index("row")
    col = lax.axis_index("col")
    x = lax.rem(row, XN)
    yl = row // XN
    z = col // 4
    yh = lax.rem(col // 2, 2)
    c = lax.rem(col, 2)
    oc = 1 - c
    xp = lax.rem(x + 1, XN)
    xm = lax.rem(x + XN - 1, XN)
    x2 = lax.rem(x + 2, XN)
    zp = lax.rem(z + 1, NZ)
    zm = lax.rem(z + NZ - 1, NZ)
    to_core = (row, col + 1 - 2 * c)
    to_yh = (row, col + 2 - 4 * yh)
    to_zp = (row, zp * 4 + yh * 2 + c)
    to_zm = (row, zm * 4 + yh * 2 + c)
    to_yl = ((1 - yl) * XN + x, col)
    to_xp = (yl * XN + xp, col)
    to_xm = (yl * XN + xm, col)
    r_own = yl * XN + x
    r_oth = (1 - yl) * XN + x

    def place(r):
        return 0 if r == 0 else 2 * r - 1 if r > 0 or r == -H else -2 * r

    def place_of(r):
        return place(H) if r == -H else place(r)

    def span(d):
        return (2 * d - 1, 2) if 0 < d < H else (place_of(d), 1)

    rel = [0]
    for d in range(1, H):
        rel += [d, -d]
    rel += [H]

    total = [0]
    summed = [0]

    def send(src, dst, rsem, dev, blocks, sums=0):
        pltpu.make_async_remote_copy(
            src_ref=src, dst_ref=dst, send_sem=s_all, recv_sem=rsem, device_id=dev, device_id_type=MESH
        ).start()
        total[0] += blocks
        summed[0] += sums

    def arrive(dst, rsem):
        pltpu.make_async_copy(dst, dst, rsem).wait()

    own_in = [
        pltpu.make_async_copy(src, dst, s_in.at[i])
        for i, (src, dst) in enumerate(((rm_h, rm), (cm_h, cm), (re_h, re), (ce_h, ce)))
    ]
    for copy in own_in:
        copy.start()

    barrier = pltpu.get_barrier_semaphore()
    partners = [to_core, to_yh, to_zp, to_zm, to_yl, to_xp, to_xm]
    for dev in partners:
        pl.semaphore_signal(barrier, inc=1, device_id=dev, device_id_type=MESH)

    def in_turn(u):
        return lax.rem(u // 2, 2) * NZ + u // 4 * 2 + lax.rem(u, 2)

    def count_copy(u):
        q = in_turn(u)
        p = lax.rem(q, NZ)
        d = (p + 1) // 2
        zc = lax.rem(z + NZ + d * (2 * lax.rem(p, 2) - 1), NZ)
        at = pl.ds(pl.multiple_of(q * 4 * B, 4 * B), 4 * B)
        return pltpu.make_async_copy(counts.at[q // NZ, zc], cnt.at[at], s_cnt.at[q])

    AHEAD = 3
    for u in range(AHEAD):
        count_copy(u).start()

    for copy in own_in:
        copy.wait()

    def own_block(embed, margs, shift):
        line = jnp.concatenate([margs[0:1, :], margs[1:2, :]], axis=1).astype(F32)
        line = 0.5 * (jnp.log(line) - shift)
        hi = line.astype(BF16).astype(F32)
        mid = (line - hi).astype(BF16).astype(F32)
        upper = jnp.concatenate([hi, mid], axis=1)
        lower = jnp.concatenate([line - hi - mid, jnp.zeros_like(line)], axis=1)
        which = lax.broadcasted_iota(jnp.int32, (16, 4 * B), 0)
        tail = jnp.where(which == 0, upper, jnp.where(which == 1, lower, 0.0)).astype(BF16)
        return embed[0].astype(BF16), embed[1].astype(BF16), tail

    for ref, parts in ((rows.at[0, yh, c], own_block(re, rm, 20.0)), (cols.at[r_own], own_block(ce, cm, 0.0))):
        ref[0:B] = parts[0]
        ref[B : 2 * B] = parts[1]
        ref[2 * B :] = parts[2]

    def line_of(tail):
        tail = tail.astype(F32)
        return tail[0:1, : 2 * B] + tail[0:1, 2 * B :] + tail[1:2, : 2 * B]

    pl.semaphore_wait(barrier, len(partners))

    def row_block(p, y):
        return rows.at[p, 1 - yh if y else yh, c]

    def send_row(y, r, up):
        to = place_of(r - 1 if up else r + 1)
        send(row_block(place(r), y), row_block(to, y), r_row.at[to, y], to_zp if up else to_zm, 1)

    def row_here(y, r):
        arrive(row_block(place_of(r), y), r_row.at[place_of(r), y])

    def row_step(y, d):
        for sign in (-1, 1):
            row_here(y, sign * d)
            if d < H - 1 or (y == 0 and sign < 0):
                send_row(y, sign * d, sign < 0)

    def far_out():
        row_here(0, H)
        send(row_block(NZ - 1, 0), row_block(NZ - 1, 0), r_row.at[NZ - 1, 1], to_yh, 1)

    def row_core(j):
        ref = rows.at[pl.ds(2 * j, 2), :, c]
        send(ref, ref, r_core.at[j], to_core, 4)

    def core_here(j):
        arrive(rows.at[pl.ds(2 * j, 2), :, oc], r_core.at[j])

    def send_col(r, up):
        send(cols.at[r], cols.at[r], r_col.at[r], to_xp if up else to_xm, 1)

    def col_here(r):
        arrive(cols.at[r], r_col.at[r])

    def preps(lo, hi):
        def chunk(u, carry):
            @pl.when(u + AHEAD < NS * NZ)
            def _():
                count_copy(u + AHEAD).start()

            count_copy(u).wait()
            q = in_turn(u)

            def part(i, carry):
                at = pl.ds(pl.multiple_of(i * 128, 128), 128)
                n = cnt[pl.ds(pl.multiple_of(q * 4 * B + i * 128, 128), 128), :].astype(F32)
                m = jnp.maximum(n, 1.0)
                conf = jnp.where(n > 0, 0.4 + m * lax.rsqrt(m), 0.0)
                PA[q, at, :] = conf
                PB[q, at, :] = 0.5 * conf * jnp.log(m)
                return carry

            return lax.fori_loop(0, 4 * B // 128, part, carry)

        lax.fori_loop(lo, hi, chunk, 0)

    def halves(s, a, b):
        return jnp.concatenate([a[:, s * B : (s + 1) * B], b[:, s * B : (s + 1) * B]], axis=1)

    def col_lines():
        lines = [line_of(cols[r, 2 * B :]) for r in range(2 * XN)]
        for s in range(NS):
            for j in range(CN // 128):
                LC[s, :, j * 128 : (j + 1) * 128] = halves(s, lines[2 * j], lines[2 * j + 1])

    def lift(p):
        lines = [line_of(rows[p + q, y, k, 2 * B :]) for q in range(2) for y in range(2) for k in range(2)]
        wide = jnp.concatenate(lines, axis=0).T
        for i in range(8):
            for s in range(NS):
                column = wide[s * B : (s + 1) * B, i : i + 1]
                LRB[s, p + i // 4, i % 4 * B : (i % 4 + 1) * B, :] = jnp.broadcast_to(column, (B, 128))

    def turn(s):
        own = cols[:, s * B : (s + 1) * B, :].reshape(CN, D)
        colsC[s] = own
        colsT[s] = (own * 0.5).T
        CPT[s] = jnp.zeros_like(CPT[s])

    def unit(s, p):
        pair = pl.ds(p, 2)
        left = rows[pair, :, :, pl.ds(pl.multiple_of(s * B, B), B), :].reshape(8 * B, D)
        lr = LRB[s, pair].reshape(8 * B, 128)
        t = dot(left, colsT[s], NN) + jnp.concatenate([lr] * (CN // 128), axis=1) + LC[s]
        conf = PA[pl.ds(s * NZ + p, 2)].reshape(8 * B, CN)
        plain = PB[pl.ds(s * NZ + p, 2)].reshape(8 * B, CN)
        g = jnp.where(conf > 0, conf * t - plain, jnp.tanh(t) + 1.0).astype(BF16)
        RP[...] = dot(g, colsC[s], NN).reshape(2, 2, 2, B, D)
        OWN[s, pair] = RP[:, :, c]
        CS[s, pair] = RP[:, :, oc].astype(BF16)
        CPT[s] += dot(left.T, g, NN)

    def sums_here(s, j):
        arrive(CR.at[s, pl.ds(2 * j, 2)], r_cr.at[s, j])

    def chip_sum(s, r):
        return OWN[s, place(r)] + CR[s, place(r)].astype(F32)

    def ring(s, d):
        if d > 0:
            sums_here(s, d - 1)
        if d == H:
            v = chip_sum(s, H)
            RSp[s, H - 1, 0] = v[0].astype(BF16)
            send(RSp.at[s, H - 1, 0], RRp.at[s, H - 1, 0], r_rp.at[s, H - 1], to_zp, 0, 1)
            RSm[s, H - 1, 1] = v[1].astype(BF16)
            send(RSm.at[s, H - 1, 1], RRm.at[s, H - 1, 1], r_rm.at[s, H - 1], to_zm, 0, 1)
        elif d > 0:
            for up in (True, False):
                RS, RR, rr, dev = (RSp, RRp, r_rp, to_zp) if up else (RSm, RRm, r_rm, to_zm)
                v = chip_sum(s, d if up else -d)
                if d == H - 1:
                    half = 0 if up else 1
                    arrive(RR.at[s, d, half], rr.at[s, d])
                    RS[s, d - 1, half] = (v[half] + RR[s, d, half].astype(F32)).astype(BF16)
                    RS[s, d - 1, 1 - half] = v[1 - half].astype(BF16)
                else:
                    arrive(RR.at[s, d], rr.at[s, d])
                    RS[s, d - 1] = (v + RR[s, d].astype(F32)).astype(BF16)
                send(RS.at[s, d - 1], RR.at[s, d - 1], rr.at[s, d - 1], dev, 0, 2)
        else:
            v = chip_sum(s, 0)
            arrive(RRp.at[s, 0], r_rp.at[s, 0])
            arrive(RRm.at[s, 0], r_rm.at[s, 0])
            VR[s] = v + RRp[s, 0].astype(F32) + RRm[s, 0].astype(F32)
            YS[s] = VR[s, 1 - yh].astype(BF16)
            send(YS.at[s], YR.at[s], r_y.at[s], to_yh, 0, 1)

    def out_copy(k, s):
        src, dst = ((gr, nr), (gc, nc))[k]
        return pltpu.make_async_copy(src.at[s], dst.at[s], s_out.at[k, s])

    def rows_out(s):
        arrive(YR.at[s], r_y.at[s])
        gr[s] = 0.5 * (VR[s, yh] + YR[s].astype(F32))
        out_copy(0, s).start()

    def col_far(s):
        CP[s] = CPT[s].T.reshape(2 * XN, B, D)
        Q1s[s, 0] = CP[s, yl * XN + x2].astype(BF16)
        send(Q1s.at[s, 0], Q1r.at[s, 0], r_q.at[s, 0], to_xp, 0, 1)
        Q1s[s, 1] = CP[s, (1 - yl) * XN + x2].astype(BF16)
        send(Q1s.at[s, 1], Q1r.at[s, 1], r_q.at[s, 1], to_xm, 0, 1)

    def col_near(s):
        arrive(Q1r.at[s, 0], r_q.at[s, 0])
        Q2s[s, 0, 0] = (CP[s, yl * XN + xp] + Q1r[s, 0].astype(F32)).astype(BF16)
        Q2s[s, 0, 1] = CP[s, (1 - yl) * XN + xp].astype(BF16)
        send(Q2s.at[s, 0], Q2r.at[s, 0], r_q.at[s, 2], to_xp, 0, 2)
        arrive(Q1r.at[s, 1], r_q.at[s, 1])
        Q2s[s, 1, 0] = CP[s, yl * XN + xm].astype(BF16)
        Q2s[s, 1, 1] = (CP[s, (1 - yl) * XN + xm] + Q1r[s, 1].astype(F32)).astype(BF16)
        send(Q2s.at[s, 1], Q2r.at[s, 1], r_q.at[s, 3], to_xm, 0, 2)

    def col_own(s):
        arrive(Q2r.at[s, 0], r_q.at[s, 2])
        arrive(Q2r.at[s, 1], r_q.at[s, 3])
        Q3s[s] = (CP[s, r_oth] + Q2r[s, 0, 1].astype(F32) + Q2r[s, 1, 1].astype(F32)).astype(BF16)
        send(Q3s.at[s], Q3r.at[s], r_q.at[s, 4], to_yl, 0, 1)
        VC[s] = CP[s, r_own] + Q2r[s, 0, 0].astype(F32) + Q2r[s, 1, 0].astype(F32)

    def cols_out(s):
        arrive(Q3r.at[s], r_q.at[s, 4])
        gc[s] = 0.5 * (VC[s] + Q3r[s].astype(F32))
        out_copy(1, s).start()

    send(row_block(0, 0), row_block(0, 0), r_row.at[0, 1], to_yh, 1)
    send_row(0, 0, True)
    send_row(0, 0, False)
    send(cols.at[r_own], cols.at[r_own], r_col.at[r_own], to_yl, 1)
    send_col(r_own, True)
    send_col(r_own, False)
    preps(0, 3)
    row_step(0, 1)
    col_here(r_oth)
    send_col(r_oth, True)
    send_col(r_oth, False)
    preps(3, 6)
    row_here(1, 0)
    send_row(1, 0, True)
    send_row(1, 0, False)
    preps(6, 8)
    row_step(0, 2)
    col_here(yl * XN + xp)
    send_col(yl * XN + xp, False)
    col_here((1 - yl) * XN + xm)
    send_col((1 - yl) * XN + xm, True)
    preps(8, 11)
    row_step(1, 1)
    row_core(0)
    preps(11, 13)
    row_step(0, 3)
    col_here((1 - yl) * XN + xp)
    col_here(yl * XN + xm)
    col_here(yl * XN + x2)
    col_here((1 - yl) * XN + x2)
    col_lines()
    turn(0)
    turn(1)

    def before(i):
        if i == 1:
            row_step(1, 2)
            row_core(1)
        if i == 2:
            far_out()
            preps(13, 15)
        if i == 3:
            row_step(1, 3)
            row_core(2)
        if i == 4:
            preps(15, 16)
        if i == 5:
            row_here(1, H)
            row_core(3)
        if i % 2 == 0:
            core_here(i // 2)
            lift(i)

    def step(i, carry):
        for k in range(2 * H):
            pl.when(i == k)(functools.partial(before, k))
        s = lax.rem(i, 2)
        j = i // 2
        p = 2 * j
        unit(s, p)
        part = pl.ds(p, 2)
        send(CS.at[s, part], CR.at[s, part], r_cr.at[s, j], to_core, 0)
        return carry

    lax.fori_loop(0, 2 * H, step, 0)
    ring(0, H)
    col_far(0)
    ring(1, H)
    col_far(1)
    ring(0, 3)
    ring(1, 3)
    col_near(0)
    col_near(1)
    ring(0, 2)
    ring(1, 2)
    col_own(0)
    col_own(1)
    ring(0, 1)
    ring(1, 1)
    cols_out(0)
    cols_out(1)
    ring(0, 0)
    ring(1, 0)
    rows_out(0)
    rows_out(1)
    for k in range(2):
        for s in range(NS):
            out_copy(k, s).wait()
    whole = B * D * 2 // (CN * 4)
    gathered = whole * 2 + 16 * D * 2 // (CN * 4)
    arrive(cnt.at[pl.ds(0, total[0] * gathered + (summed[0] + 8 * 2 * H // 2) * whole)], s_all)


def local(counts, re, ce, rm, cm, ra, ca, *, NZ, XN):
    S, B, D = re.shape
    CB = counts.shape[2]
    H = NZ // 2
    R = 2 * XN
    counts = counts.reshape(S, NZ, 4 * B, CB)
    sem = pltpu.SemaphoreType.DMA
    v = pltpu.VMEM
    scratch = [
        v((S, B, D), F32),
        v((S, B, D), F32),
        v((S, B), jnp.int32),
        v((S, B), jnp.int32),
        v((S * NZ * 4 * B, CB), jnp.int32),
        v((NZ, 2, 2, 2 * B + 16, D), BF16),
        v((R, 2 * B + 16, D), BF16),
        v((S, D, CB), BF16),
        v((S, CB, D), BF16),
        v((S, NZ, 4 * B, 128), F32),
        v((S, 1, CB), F32),
        v((S * NZ, 4 * B, CB), F32),
        v((S * NZ, 4 * B, CB), F32),
        v((2, 2, 2, B, D), F32),
        v((S, NZ, 2, B, D), F32),
        v((S, D, CB), F32),
        v((S, R, B, D), F32),
        v((S, NZ, 2, B, D), BF16),
        v((S, NZ, 2, B, D), BF16),
        v((S, H, 2, B, D), BF16),
        v((S, H, 2, B, D), BF16),
        v((S, H, 2, B, D), BF16),
        v((S, H, 2, B, D), BF16),
        v((S, B, D), BF16),
        v((S, B, D), BF16),
        v((S, 2, B, D), F32),
        v((S, 2, B, D), BF16),
        v((S, 2, B, D), BF16),
        v((S, 2, 2, B, D), BF16),
        v((S, 2, 2, B, D), BF16),
        v((S, B, D), BF16),
        v((S, B, D), BF16),
        v((S, B, D), F32),
        v((S, B, D), F32),
        v((S, B, D), F32),
        sem((4,)),
        sem((S * NZ,)),
        sem(()),
        sem((2, S)),
        sem((NZ, 2)),
        sem((H,)),
        sem((R,)),
        sem((S, H)),
        sem((S, H)),
        sem((S, H)),
        sem((S,)),
        sem((S, 5)),
    ]
    gr, gc = pl.pallas_call(
        functools.partial(kernel, NZ, XN, B, D, CB),
        out_shape=(jax.ShapeDtypeStruct((S, B, D), F32), jax.ShapeDtypeStruct((S, B, D), F32)),
        in_specs=[pl.BlockSpec(memory_space=pltpu.HBM)] * 5,
        out_specs=(pl.BlockSpec(memory_space=pltpu.HBM),) * 2,
        scratch_shapes=scratch,
        compiler_params=pltpu.CompilerParams(
            collective_id=0, has_side_effects=True, vmem_limit_bytes=60 * 1024 * 1024
        ),
    )(counts, re, ce, rm, cm)
    return adagrad(re, ra, gr), adagrad(ce, ca, gc)


def solution(mesh):
    return jax.shard_map(
        functools.partial(local, NZ=mesh.shape["col"] // 4, XN=mesh.shape["row"] // 2),
        mesh=mesh,
        in_specs=(
            P(None, "row", "col"),
            P(None, ("row", "col"), None),
            P(None, ("col", "row"), None),
            P(None, ("row", "col")),
            P(None, ("col", "row")),
            P(None, ("row", "col"), None),
            P(None, ("col", "row"), None),
        ),
        out_specs=(P(None, ("row", "col"), None), P(None, ("col", "row"), None)),
        check_vma=False,
    )
```

```python
import functools

import jax
import jax.numpy as jnp
from jax import lax
from jax.experimental import pallas as pl
from jax.experimental.pallas import tpu as pltpu
from jax.sharding import PartitionSpec as P

MESH = pl.DeviceIdType.MESH
F32 = jnp.float32
BF16 = jnp.bfloat16
NT = (((1,), (1,)), ((), ()))
NN = (((1,), (0,)), ((), ()))
TN = (((0,), (0,)), ((), ()))


def dot(a, b, dims):
    return lax.dot_general(a, b, dims, preferred_element_type=F32)


def adagrad(w, a, g):
    return w - g / jnp.sqrt(a + g * g)


def kernel(
    NZ, XN, B, D, CN,
    counts, re_h, ce_h, rm_h, cm_h, nr, nc,
    re, ce, rm, cm,
    cnt, rows, cols, colsT, colsC, LRB, LC, PA, PB, RP, CPT, CP,
    CS, CR, RSp, RSm, RRp, RRm, YS, YR, VR, Q1s, Q1r, Q2s, Q2r, Q3s, Q3r, VC, gr, gc,
    s_in, s_cnt, s_all, s_out, r_row, r_core, r_col, r_cr, r_rp, r_rm, r_y, r_q,
):
    H = NZ // 2
    NS = 2
    row = lax.axis_index("row")
    col = lax.axis_index("col")
    x = lax.rem(row, XN)
    yl = row // XN
    z = col // 4
    yh = lax.rem(col // 2, 2)
    c = lax.rem(col, 2)
    oc = 1 - c
    xp = lax.rem(x + 1, XN)
    xm = lax.rem(x + XN - 1, XN)
    x2 = lax.rem(x + 2, XN)
    zp = lax.rem(z + 1, NZ)
    zm = lax.rem(z + NZ - 1, NZ)
    to_core = (row, col + 1 - 2 * c)
    to_yh = (row, col + 2 - 4 * yh)
    to_zp = (row, zp * 4 + yh * 2 + c)
    to_zm = (row, zm * 4 + yh * 2 + c)
    to_yl = ((1 - yl) * XN + x, col)
    to_xp = (yl * XN + xp, col)
    to_xm = (yl * XN + xm, col)
    r_own = yl * XN + x
    r_oth = (1 - yl) * XN + x

    def place(r):
        return 0 if r == 0 else 2 * r - 1 if r > 0 or r == -H else -2 * r

    def place_of(r):
        return place(H) if r == -H else place(r)

    def span(d):
        return (2 * d - 1, 2) if 0 < d < H else (place_of(d), 1)

    rel = [0]
    for d in range(1, H):
        rel += [d, -d]
    rel += [H]

    total = [0]
    summed = [0]

    def send(src, dst, rsem, dev, blocks, sums=0):
        pltpu.make_async_remote_copy(
            src_ref=src, dst_ref=dst, send_sem=s_all, recv_sem=rsem, device_id=dev, device_id_type=MESH
        ).start()
        total[0] += blocks
        summed[0] += sums

    def arrive(dst, rsem):
        pltpu.make_async_copy(dst, dst, rsem).wait()

    own_in = [
        pltpu.make_async_copy(src, dst, s_in.at[i])
        for i, (src, dst) in enumerate(((rm_h, rm), (cm_h, cm), (re_h, re), (ce_h, ce)))
    ]
    for copy in own_in:
        copy.start()

    barrier = pltpu.get_barrier_semaphore()
    partners = [to_core, to_yh, to_zp, to_zm, to_yl, to_xp, to_xm]
    for dev in partners:
        pl.semaphore_signal(barrier, inc=1, device_id=dev, device_id_type=MESH)

    def turn_of(i):
        first, second, late = (i + 7) // 8, (i + 6) // 8, (i + 3) // 8
        return late + first - second, (1 - late) * (i - first) + late * (8 - i)

    def in_turn(u):
        s, j = turn_of(u // 2)
        return s * NZ + 2 * j + lax.rem(u, 2)

    def count_copy(u):
        q = in_turn(u)
        p = lax.rem(q, NZ)
        d = (p + 1) // 2
        zc = lax.rem(z + NZ + d * (2 * lax.rem(p, 2) - 1), NZ)
        at = pl.ds(pl.multiple_of(q * 4 * B, 4 * B), 4 * B)
        return pltpu.make_async_copy(counts.at[q // NZ, zc], cnt.at[at], s_cnt.at[q])

    AHEAD = 3
    for u in range(AHEAD):
        count_copy(u).start()

    for copy in own_in:
        copy.wait()

    def own_block(embed, margs, shift):
        line = jnp.concatenate([margs[0:1, :], margs[1:2, :]], axis=1).astype(F32)
        line = 0.5 * (jnp.log(line) - shift)
        hi = line.astype(BF16).astype(F32)
        mid = (line - hi).astype(BF16).astype(F32)
        upper = jnp.concatenate([hi, mid], axis=1)
        lower = jnp.concatenate([line - hi - mid, jnp.zeros_like(line)], axis=1)
        which = lax.broadcasted_iota(jnp.int32, (16, 4 * B), 0)
        tail = jnp.where(which == 0, upper, jnp.where(which == 1, lower, 0.0)).astype(BF16)
        return embed[0].astype(BF16), embed[1].astype(BF16), tail

    for ref, parts in ((rows.at[0, yh, c], own_block(re, rm, 20.0)), (cols.at[r_own], own_block(ce, cm, 0.0))):
        ref[0:B] = parts[0]
        ref[B : 2 * B] = parts[1]
        ref[2 * B :] = parts[2]

    def line_of(tail):
        tail = tail.astype(F32)
        return tail[0:1, : 2 * B] + tail[0:1, 2 * B :] + tail[1:2, : 2 * B]

    pl.semaphore_wait(barrier, len(partners))

    def row_block(p, y):
        return rows.at[p, 1 - yh if y else yh, c]

    def send_row(y, r, up):
        to = place_of(r - 1 if up else r + 1)
        send(row_block(place(r), y), row_block(to, y), r_row.at[to, y], to_zp if up else to_zm, 1)

    def row_here(y, r):
        arrive(row_block(place_of(r), y), r_row.at[place_of(r), y])

    def row_step(y, d):
        for sign in (-1, 1):
            row_here(y, sign * d)
            if d < H - 1 or (y == 0 and sign < 0):
                send_row(y, sign * d, sign < 0)

    def far_out():
        row_here(0, H)
        send(row_block(NZ - 1, 0), row_block(NZ - 1, 0), r_row.at[NZ - 1, 1], to_yh, 1)

    def row_core(j):
        ref = rows.at[pl.ds(2 * j, 2), :, c]
        send(ref, ref, r_core.at[j], to_core, 4)

    def core_here(j):
        arrive(rows.at[pl.ds(2 * j, 2), :, oc], r_core.at[j])

    def send_col(r, up):
        send(cols.at[r], cols.at[r], r_col.at[r], to_xp if up else to_xm, 1)

    def col_here(r):
        arrive(cols.at[r], r_col.at[r])

    def preps(lo, hi):
        def chunk(u, carry):
            @pl.when(u + AHEAD < NS * NZ)
            def _():
                count_copy(u + AHEAD).start()

            count_copy(u).wait()
            q = in_turn(u)

            def part(i, carry):
                at = pl.ds(pl.multiple_of(i * 128, 128), 128)
                n = cnt[pl.ds(pl.multiple_of(q * 4 * B + i * 128, 128), 128), :].astype(F32)
                m = jnp.maximum(n, 1.0)
                conf = jnp.where(n > 0, 0.4 + m * lax.rsqrt(m), 0.0)
                PA[q, at, :] = conf
                PB[q, at, :] = 0.5 * conf * jnp.log(m)
                return carry

            return lax.fori_loop(0, 4 * B // 128, part, carry)

        lax.fori_loop(lo, hi, chunk, 0)

    def halves(s, a, b):
        return jnp.concatenate([a[:, s * B : (s + 1) * B], b[:, s * B : (s + 1) * B]], axis=1)

    def col_lines():
        lines = [line_of(cols[r, 2 * B :]) for r in range(2 * XN)]
        for s in range(NS):
            for j in range(CN // 128):
                LC[s, :, j * 128 : (j + 1) * 128] = halves(s, lines[2 * j], lines[2 * j + 1])

    def lift(p):
        lines = [line_of(rows[p + q, y, k, 2 * B :]) for q in range(2) for y in range(2) for k in range(2)]
        wide = jnp.concatenate(lines, axis=0).T
        for i in range(8):
            for s in range(NS):
                column = wide[s * B : (s + 1) * B, i : i + 1]
                LRB[s, p + i // 4, i % 4 * B : (i % 4 + 1) * B, :] = jnp.broadcast_to(column, (B, 128))

    def turn(s):
        own = cols[:, s * B : (s + 1) * B, :].reshape(CN, D)
        colsC[s] = own
        colsT[s] = (own * 0.5).T
        CPT[s] = jnp.zeros_like(CPT[s])

    def unit(s, p):
        pair = pl.ds(p, 2)
        left = rows[pair, :, :, pl.ds(pl.multiple_of(s * B, B), B), :].reshape(8 * B, D)
        lr = LRB[s, pair].reshape(8 * B, 128)
        t = dot(left, colsT[s], NN) + jnp.concatenate([lr] * (CN // 128), axis=1) + LC[s]
        conf = PA[pl.ds(s * NZ + p, 2)].reshape(8 * B, CN)
        plain = PB[pl.ds(s * NZ + p, 2)].reshape(8 * B, CN)
        g = jnp.where(conf > 0, conf * t - plain, jnp.tanh(t) + 1.0).astype(BF16)
        RP[s, pair] = dot(g, colsC[s], NN).reshape(2, 2, 2, B, D)
        CS[s, pair] = RP[s, pair, :, oc].astype(BF16)
        CPT[s] += dot(left.T, g, NN)

    def sums_here(s, j):
        arrive(CR.at[s, pl.ds(2 * j, 2)], r_cr.at[s, j])

    def chip_sum(s, r):
        return RP[s, place(r), :, c] + CR[s, place(r)].astype(F32)

    def ring(s, d):
        if d > 0:
            sums_here(s, d - 1)
        if d == H:
            v = chip_sum(s, H)
            RSp[s, H - 1, 0] = v[0].astype(BF16)
            send(RSp.at[s, H - 1, 0], RRp.at[s, H - 1, 0], r_rp.at[s, H - 1], to_zp, 0, 1)
            RSm[s, H - 1, 1] = v[1].astype(BF16)
            send(RSm.at[s, H - 1, 1], RRm.at[s, H - 1, 1], r_rm.at[s, H - 1], to_zm, 0, 1)
        elif d > 0:
            for up in (True, False):
                RS, RR, rr, dev = (RSp, RRp, r_rp, to_zp) if up else (RSm, RRm, r_rm, to_zm)
                v = chip_sum(s, d if up else -d)
                if d == H - 1:
                    half = 0 if up else 1
                    arrive(RR.at[s, d, half], rr.at[s, d])
                    RS[s, d - 1, half] = (v[half] + RR[s, d, half].astype(F32)).astype(BF16)
                    RS[s, d - 1, 1 - half] = v[1 - half].astype(BF16)
                else:
                    arrive(RR.at[s, d], rr.at[s, d])
                    RS[s, d - 1] = (v + RR[s, d].astype(F32)).astype(BF16)
                send(RS.at[s, d - 1], RR.at[s, d - 1], rr.at[s, d - 1], dev, 0, 2)
        else:
            v = chip_sum(s, 0)
            arrive(RRp.at[s, 0], r_rp.at[s, 0])
            arrive(RRm.at[s, 0], r_rm.at[s, 0])
            VR[s] = v + RRp[s, 0].astype(F32) + RRm[s, 0].astype(F32)
            YS[s] = VR[s, 1 - yh].astype(BF16)
            send(YS.at[s], YR.at[s], r_y.at[s], to_yh, 0, 1)

    def out_copy(k, s):
        src, dst = ((gr, nr), (gc, nc))[k]
        return pltpu.make_async_copy(src.at[s], dst.at[s], s_out.at[k, s])

    def rows_out(s):
        arrive(YR.at[s], r_y.at[s])
        gr[s] = 0.5 * (VR[s, yh] + YR[s].astype(F32))
        out_copy(0, s).start()

    def col_far(s):
        CP[s] = CPT[s].T.reshape(2 * XN, B, D)
        Q1s[s, 0] = CP[s, yl * XN + x2].astype(BF16)
        send(Q1s.at[s, 0], Q1r.at[s, 0], r_q.at[s, 0], to_xp, 0, 1)
        Q1s[s, 1] = CP[s, (1 - yl) * XN + x2].astype(BF16)
        send(Q1s.at[s, 1], Q1r.at[s, 1], r_q.at[s, 1], to_xm, 0, 1)

    def col_near(s):
        arrive(Q1r.at[s, 0], r_q.at[s, 0])
        Q2s[s, 0, 0] = (CP[s, yl * XN + xp] + Q1r[s, 0].astype(F32)).astype(BF16)
        Q2s[s, 0, 1] = CP[s, (1 - yl) * XN + xp].astype(BF16)
        send(Q2s.at[s, 0], Q2r.at[s, 0], r_q.at[s, 2], to_xp, 0, 2)
        arrive(Q1r.at[s, 1], r_q.at[s, 1])
        Q2s[s, 1, 0] = CP[s, yl * XN + xm].astype(BF16)
        Q2s[s, 1, 1] = (CP[s, (1 - yl) * XN + xm] + Q1r[s, 1].astype(F32)).astype(BF16)
        send(Q2s.at[s, 1], Q2r.at[s, 1], r_q.at[s, 3], to_xm, 0, 2)

    def col_own(s):
        arrive(Q2r.at[s, 0], r_q.at[s, 2])
        arrive(Q2r.at[s, 1], r_q.at[s, 3])
        Q3s[s] = (CP[s, r_oth] + Q2r[s, 0, 1].astype(F32) + Q2r[s, 1, 1].astype(F32)).astype(BF16)
        send(Q3s.at[s], Q3r.at[s], r_q.at[s, 4], to_yl, 0, 1)
        VC[s] = CP[s, r_own] + Q2r[s, 0, 0].astype(F32) + Q2r[s, 1, 0].astype(F32)

    def cols_out(s):
        arrive(Q3r.at[s], r_q.at[s, 4])
        gc[s] = 0.5 * (VC[s] + Q3r[s].astype(F32))
        out_copy(1, s).start()

    send(row_block(0, 0), row_block(0, 0), r_row.at[0, 1], to_yh, 1)
    send_row(0, 0, True)
    send_row(0, 0, False)
    send(cols.at[r_own], cols.at[r_own], r_col.at[r_own], to_yl, 1)
    send_col(r_own, True)
    send_col(r_own, False)
    preps(0, 3)
    row_step(0, 1)
    col_here(r_oth)
    send_col(r_oth, True)
    send_col(r_oth, False)
    preps(3, 6)
    row_here(1, 0)
    send_row(1, 0, True)
    send_row(1, 0, False)
    preps(6, 8)
    row_step(0, 2)
    col_here(yl * XN + xp)
    send_col(yl * XN + xp, False)
    col_here((1 - yl) * XN + xm)
    send_col((1 - yl) * XN + xm, True)
    preps(8, 9)
    row_step(1, 1)
    row_core(0)
    preps(9, 10)
    row_step(0, 3)
    col_here((1 - yl) * XN + xp)
    col_here(yl * XN + xm)
    col_here(yl * XN + x2)
    col_here((1 - yl) * XN + x2)
    col_lines()
    turn(0)
    turn(1)

    def before(i):
        if i == 0:
            core_here(0)
            lift(0)
        if i == 1:
            row_step(1, 2)
            row_core(1)
        if i == 2:
            far_out()
            core_here(1)
            lift(2)
        if i == 3:
            row_step(1, 3)
            row_core(2)
            preps(10, 12)
            core_here(2)
            lift(4)
        if i == 4:
            row_here(1, H)
            row_core(3)
            preps(12, 14)
            core_here(3)
            lift(6)
        if i == 6:
            ring(0, H)
            col_far(0)
            preps(14, 16)
        if i == 7:
            ring(1, H)
            ring(0, 3)

    def step(i, carry):
        for k in range(2 * H):
            pl.when(i == k)(functools.partial(before, k))
        s, j = turn_of(i)
        p = 2 * j
        unit(s, p)
        part = pl.ds(p, 2)
        send(CS.at[s, part], CR.at[s, part], r_cr.at[s, j], to_core, 0)
        return carry

    lax.fori_loop(0, 2 * H, step, 0)
    ring(1, 3)
    col_near(0)
    ring(0, 2)
    col_far(1)
    ring(1, 2)
    col_own(0)
    ring(0, 1)
    col_near(1)
    ring(1, 1)
    cols_out(0)
    ring(0, 0)
    col_own(1)
    ring(1, 0)
    rows_out(0)
    cols_out(1)
    rows_out(1)
    for k in range(2):
        for s in range(NS):
            out_copy(k, s).wait()
    whole = B * D * 2 // (CN * 4)
    gathered = whole * 2 + 16 * D * 2 // (CN * 4)
    arrive(cnt.at[pl.ds(0, total[0] * gathered + (summed[0] + 8 * 2 * H // 2) * whole)], s_all)


def local(counts, re, ce, rm, cm, ra, ca, *, NZ, XN):
    S, B, D = re.shape
    CB = counts.shape[2]
    H = NZ // 2
    R = 2 * XN
    counts = counts.reshape(S, NZ, 4 * B, CB)
    sem = pltpu.SemaphoreType.DMA
    v = pltpu.VMEM
    scratch = [
        v((S, B, D), F32),
        v((S, B, D), F32),
        v((S, B), jnp.int32),
        v((S, B), jnp.int32),
        v((S * NZ * 4 * B, CB), jnp.int32),
        v((NZ, 2, 2, 2 * B + 16, D), BF16),
        v((R, 2 * B + 16, D), BF16),
        v((S, D, CB), BF16),
        v((S, CB, D), BF16),
        v((S, NZ, 4 * B, 128), F32),
        v((S, 1, CB), F32),
        v((S * NZ, 4 * B, CB), F32),
        v((S * NZ, 4 * B, CB), F32),
        v((S, NZ, 2, 2, B, D), F32),
        v((S, D, CB), F32),
        v((S, R, B, D), F32),
        v((S, NZ, 2, B, D), BF16),
        v((S, NZ, 2, B, D), BF16),
        v((S, H, 2, B, D), BF16),
        v((S, H, 2, B, D), BF16),
        v((S, H, 2, B, D), BF16),
        v((S, H, 2, B, D), BF16),
        v((S, B, D), BF16),
        v((S, B, D), BF16),
        v((S, 2, B, D), F32),
        v((S, 2, B, D), BF16),
        v((S, 2, B, D), BF16),
        v((S, 2, 2, B, D), BF16),
        v((S, 2, 2, B, D), BF16),
        v((S, B, D), BF16),
        v((S, B, D), BF16),
        v((S, B, D), F32),
        v((S, B, D), F32),
        v((S, B, D), F32),
        sem((4,)),
        sem((S * NZ,)),
        sem(()),
        sem((2, S)),
        sem((NZ, 2)),
        sem((H,)),
        sem((R,)),
        sem((S, H)),
        sem((S, H)),
        sem((S, H)),
        sem((S,)),
        sem((S, 5)),
    ]
    gr, gc = pl.pallas_call(
        functools.partial(kernel, NZ, XN, B, D, CB),
        out_shape=(jax.ShapeDtypeStruct((S, B, D), F32), jax.ShapeDtypeStruct((S, B, D), F32)),
        in_specs=[pl.BlockSpec(memory_space=pltpu.HBM)] * 5,
        out_specs=(pl.BlockSpec(memory_space=pltpu.HBM),) * 2,
        scratch_shapes=scratch,
        compiler_params=pltpu.CompilerParams(
            collective_id=0, has_side_effects=True, vmem_limit_bytes=60 * 1024 * 1024
        ),
    )(counts, re, ce, rm, cm)
    return adagrad(re, ra, gr), adagrad(ce, ca, gc)


def solution(mesh):
    return jax.shard_map(
        functools.partial(local, NZ=mesh.shape["col"] // 4, XN=mesh.shape["row"] // 2),
        mesh=mesh,
        in_specs=(
            P(None, "row", "col"),
            P(None, ("row", "col"), None),
            P(None, ("col", "row"), None),
            P(None, ("row", "col")),
            P(None, ("col", "row")),
            P(None, ("row", "col"), None),
            P(None, ("col", "row"), None),
        ),
        out_specs=(P(None, ("row", "col"), None), P(None, ("col", "row"), None)),
        check_vma=False,
    )
```

```python
import functools

import jax
import jax.numpy as jnp
from jax import lax
from jax.experimental import pallas as pl
from jax.experimental.pallas import tpu as pltpu
from jax.sharding import PartitionSpec as P

MESH = pl.DeviceIdType.MESH
F32 = jnp.float32
BF16 = jnp.bfloat16
NT = (((1,), (1,)), ((), ()))
NN = (((1,), (0,)), ((), ()))
TN = (((0,), (0,)), ((), ()))


def dot(a, b, dims):
    return lax.dot_general(a, b, dims, preferred_element_type=F32)


def adagrad(w, a, g):
    return w - g / jnp.sqrt(a + g * g)


def kernel(
    NZ, XN, B, D, CN,
    counts, re_h, ce_h, rm_h, cm_h, nr, nc,
    re, ce, rm, cm,
    cnt, rows, cols, colsT, colsC, LRB, LC, PA, PB, RP, CPT, CP,
    CS, CR, RSp, RSm, RRp, RRm, YS, YR, VR, Q1s, Q1r, Q2s, Q2r, Q3s, Q3r, VC, gr, gc,
    s_in, s_cnt, s_all, s_out, r_row, r_core, r_col, r_cr, r_rp, r_rm, r_y, r_q,
):
    H = NZ // 2
    NS = 2
    row = lax.axis_index("row")
    col = lax.axis_index("col")
    x = lax.rem(row, XN)
    yl = row // XN
    z = col // 4
    yh = lax.rem(col // 2, 2)
    c = lax.rem(col, 2)
    oc = 1 - c
    xp = lax.rem(x + 1, XN)
    xm = lax.rem(x + XN - 1, XN)
    x2 = lax.rem(x + 2, XN)
    zp = lax.rem(z + 1, NZ)
    zm = lax.rem(z + NZ - 1, NZ)
    to_core = (row, col + 1 - 2 * c)
    to_yh = (row, col + 2 - 4 * yh)
    to_zp = (row, zp * 4 + yh * 2 + c)
    to_zm = (row, zm * 4 + yh * 2 + c)
    to_yl = ((1 - yl) * XN + x, col)
    to_xp = (yl * XN + xp, col)
    to_xm = (yl * XN + xm, col)
    r_own = yl * XN + x
    r_oth = (1 - yl) * XN + x

    def place(r):
        return 0 if r == 0 else 2 * r - 1 if r > 0 or r == -H else -2 * r

    def place_of(r):
        return place(H) if r == -H else place(r)

    def span(d):
        return (2 * d - 1, 2) if 0 < d < H else (place_of(d), 1)

    rel = [0]
    for d in range(1, H):
        rel += [d, -d]
    rel += [H]

    total = [0]

    def send(src, dst, rsem, dev, kind, count=1):
        pltpu.make_async_remote_copy(
            src_ref=src, dst_ref=dst, send_sem=s_all, recv_sem=rsem, device_id=dev, device_id_type=MESH
        ).start()
        total[0] += count * (B + 16 if kind == 0 else B)

    def arrive(dst, rsem):
        pltpu.make_async_copy(dst, dst, rsem).wait()

    own_in = [
        pltpu.make_async_copy(src, dst, s_in.at[i])
        for i, (src, dst) in enumerate(((rm_h, rm), (cm_h, cm), (re_h, re), (ce_h, ce)))
    ]
    for copy in own_in:
        copy.start()

    barrier = pltpu.get_barrier_semaphore()
    partners = [to_core, to_yh, to_zp, to_zm, to_yl, to_xp, to_xm]
    for dev in partners:
        pl.semaphore_signal(barrier, inc=1, device_id=dev, device_id_type=MESH)

    def turn_of(i):
        first, second, late = (i + 7) // 8, (i + 6) // 8, (i + 3) // 8
        return late + first - second, (1 - late) * (i - first) + late * (8 - i)

    def in_turn(u):
        s, j = turn_of(u // 2)
        return s * NZ + 2 * j + lax.rem(u, 2)

    def count_copy(u):
        q = in_turn(u)
        p = lax.rem(q, NZ)
        d = (p + 1) // 2
        zc = lax.rem(z + NZ + d * (2 * lax.rem(p, 2) - 1), NZ)
        at = pl.ds(pl.multiple_of(q * 4 * B, 4 * B), 4 * B)
        return pltpu.make_async_copy(counts.at[q // NZ, zc], cnt.at[at], s_cnt.at[q])

    AHEAD = 3
    for u in range(AHEAD):
        count_copy(u).start()

    for copy in own_in:
        copy.wait()

    def own_block(embed, margs, shift):
        line = jnp.concatenate([margs[0:1, :], margs[1:2, :]], axis=1).astype(F32)
        line = 0.5 * (jnp.log(line) - shift)
        hi = line.astype(BF16).astype(F32)
        mid = (line - hi).astype(BF16).astype(F32)
        upper = jnp.concatenate([hi, mid], axis=1)
        lower = jnp.concatenate([line - hi - mid, jnp.zeros_like(line)], axis=1)
        which = lax.broadcasted_iota(jnp.int32, (16, 4 * B), 0)
        tail = jnp.where(which == 0, upper, jnp.where(which == 1, lower, 0.0)).astype(BF16)
        return embed[0].astype(BF16), embed[1].astype(BF16), tail

    for ref, parts in ((rows.at[0, yh, c], own_block(re, rm, 20.0)), (cols.at[r_own], own_block(ce, cm, 0.0))):
        ref[0:B] = parts[0]
        ref[B : B + 16] = parts[2]
        ref[B + 16 :] = parts[1]

    def line_of(tail):
        tail = tail.astype(F32)
        return tail[0:1, : 2 * B] + tail[0:1, 2 * B :] + tail[1:2, : 2 * B]

    pl.semaphore_wait(barrier, len(partners))

    def part(s):
        return pl.ds(0, B + 16) if s == 0 else pl.ds(B + 16, B)

    def row_block(s, p, y):
        return rows.at[p, 1 - yh if y else yh, c, part(s)]

    def send_row(s, y, r, up):
        to = place_of(r - 1 if up else r + 1)
        send(row_block(s, place(r), y), row_block(s, to, y), r_row.at[s, to, y], to_zp if up else to_zm, s)

    def row_here(s, y, r):
        arrive(row_block(s, place_of(r), y), r_row.at[s, place_of(r), y])

    def row_step(s, y, d):
        for sign in (-1, 1):
            row_here(s, y, sign * d)
            if d < H - 1 or (y == 0 and sign < 0):
                send_row(s, y, sign * d, sign < 0)

    def row_y(s):
        row_here(s, 1, 0)
        send_row(s, 1, 0, True)
        send_row(s, 1, 0, False)

    def far_out(s):
        row_here(s, 0, H)
        send(row_block(s, NZ - 1, 0), row_block(s, NZ - 1, 0), r_row.at[s, NZ - 1, 1], to_yh, s)

    def row_core(s, j):
        ref = rows.at[pl.ds(2 * j, 2), :, c, part(s)]
        send(ref, ref, r_core.at[s, j], to_core, s, 4)

    def core_here(s, j):
        arrive(rows.at[pl.ds(2 * j, 2), :, oc, part(s)], r_core.at[s, j])

    def col_block(s, r):
        return cols.at[r, part(s)]

    def send_col(s, r, up):
        send(col_block(s, r), col_block(s, r), r_col.at[s, r], to_xp if up else to_xm, s)

    def col_here(s, r):
        arrive(col_block(s, r), r_col.at[s, r])

    def col_y(s):
        col_here(s, r_oth)
        send_col(s, r_oth, True)
        send_col(s, r_oth, False)

    def col_x(s):
        col_here(s, yl * XN + xp)
        send_col(s, yl * XN + xp, False)
        col_here(s, (1 - yl) * XN + xm)
        send_col(s, (1 - yl) * XN + xm, True)

    def all_cols(s):
        col_here(s, (1 - yl) * XN + xp)
        col_here(s, yl * XN + xm)
        col_here(s, yl * XN + x2)
        col_here(s, (1 - yl) * XN + x2)

    def preps(lo, hi):
        def chunk(u, carry):
            @pl.when(u + AHEAD < NS * NZ)
            def _():
                count_copy(u + AHEAD).start()

            count_copy(u).wait()
            q = in_turn(u)

            def part(i, carry):
                at = pl.ds(pl.multiple_of(i * 128, 128), 128)
                n = cnt[pl.ds(pl.multiple_of(q * 4 * B + i * 128, 128), 128), :].astype(F32)
                m = jnp.maximum(n, 1.0)
                conf = jnp.where(n > 0, 0.4 + m * lax.rsqrt(m), 0.0)
                PA[q, at, :] = conf
                PB[q, at, :] = 0.5 * conf * jnp.log(m)
                return carry

            return lax.fori_loop(0, 4 * B // 128, part, carry)

        lax.fori_loop(lo, hi, chunk, 0)

    def halves(s, a, b):
        return jnp.concatenate([a[:, s * B : (s + 1) * B], b[:, s * B : (s + 1) * B]], axis=1)

    def col_lines():
        lines = [line_of(cols[r, B : B + 16]) for r in range(2 * XN)]
        for s in range(NS):
            for j in range(CN // 128):
                LC[s, :, j * 128 : (j + 1) * 128] = halves(s, lines[2 * j], lines[2 * j + 1])

    def lift(p):
        lines = [line_of(rows[p + q, y, k, B : B + 16]) for q in range(2) for y in range(2) for k in range(2)]
        wide = jnp.concatenate(lines, axis=0).T
        for i in range(8):
            for s in range(NS):
                column = wide[s * B : (s + 1) * B, i : i + 1]
                LRB[s, p + i // 4, i % 4 * B : (i % 4 + 1) * B, :] = jnp.broadcast_to(column, (B, 128))

    def turn(s):
        own = cols[:, s * (B + 16) : s * (B + 16) + B, :].reshape(CN, D)
        colsC[s] = own
        colsT[s] = (own * 0.5).T
        CPT[s] = jnp.zeros_like(CPT[s])

    def unit(s, p):
        pair = pl.ds(p, 2)
        left = rows[pair, :, :, pl.ds(pl.multiple_of(s * (B + 16), 16), B), :].reshape(8 * B, D)
        lr = LRB[s, pair].reshape(8 * B, 128)
        t = dot(left, colsT[s], NN) + jnp.concatenate([lr] * (CN // 128), axis=1) + LC[s]
        conf = PA[pl.ds(s * NZ + p, 2)].reshape(8 * B, CN)
        plain = PB[pl.ds(s * NZ + p, 2)].reshape(8 * B, CN)
        g = jnp.where(conf > 0, conf * t - plain, jnp.tanh(t) + 1.0).astype(BF16)
        RP[s, pair] = dot(g, colsC[s], NN).reshape(2, 2, 2, B, D)
        CS[s, pair] = RP[s, pair, :, oc].astype(BF16)
        CPT[s] += dot(left.T, g, NN)

    def sums_here(s, j):
        arrive(CR.at[s, pl.ds(2 * j, 2)], r_cr.at[s, j])

    def chip_sum(s, r):
        return RP[s, place(r), :, c] + CR[s, place(r)].astype(F32)

    def ring(s, d):
        if d > 0:
            sums_here(s, d - 1)
        if d == H:
            v = chip_sum(s, H)
            RSp[s, H - 1, 0] = v[0].astype(BF16)
            send(RSp.at[s, H - 1, 0], RRp.at[s, H - 1, 0], r_rp.at[s, H - 1], to_zp, 1, 1)
            RSm[s, H - 1, 1] = v[1].astype(BF16)
            send(RSm.at[s, H - 1, 1], RRm.at[s, H - 1, 1], r_rm.at[s, H - 1], to_zm, 1, 1)
        elif d > 0:
            for up in (True, False):
                RS, RR, rr, dev = (RSp, RRp, r_rp, to_zp) if up else (RSm, RRm, r_rm, to_zm)
                v = chip_sum(s, d if up else -d)
                if d == H - 1:
                    half = 0 if up else 1
                    arrive(RR.at[s, d, half], rr.at[s, d])
                    RS[s, d - 1, half] = (v[half] + RR[s, d, half].astype(F32)).astype(BF16)
                    RS[s, d - 1, 1 - half] = v[1 - half].astype(BF16)
                else:
                    arrive(RR.at[s, d], rr.at[s, d])
                    RS[s, d - 1] = (v + RR[s, d].astype(F32)).astype(BF16)
                send(RS.at[s, d - 1], RR.at[s, d - 1], rr.at[s, d - 1], dev, 1, 2)
        else:
            v = chip_sum(s, 0)
            arrive(RRp.at[s, 0], r_rp.at[s, 0])
            arrive(RRm.at[s, 0], r_rm.at[s, 0])
            VR[s] = v + RRp[s, 0].astype(F32) + RRm[s, 0].astype(F32)
            YS[s] = VR[s, 1 - yh].astype(BF16)
            send(YS.at[s], YR.at[s], r_y.at[s], to_yh, 1, 1)

    def out_copy(k, s):
        src, dst = ((gr, nr), (gc, nc))[k]
        return pltpu.make_async_copy(src.at[s], dst.at[s], s_out.at[k, s])

    def rows_out(s):
        arrive(YR.at[s], r_y.at[s])
        gr[s] = 0.5 * (VR[s, yh] + YR[s].astype(F32))
        out_copy(0, s).start()

    def col_far(s):
        CP[s] = CPT[s].T.reshape(2 * XN, B, D)
        Q1s[s, 0] = CP[s, yl * XN + x2].astype(BF16)
        send(Q1s.at[s, 0], Q1r.at[s, 0], r_q.at[s, 0], to_xp, 1, 1)
        Q1s[s, 1] = CP[s, (1 - yl) * XN + x2].astype(BF16)
        send(Q1s.at[s, 1], Q1r.at[s, 1], r_q.at[s, 1], to_xm, 1, 1)

    def col_near(s):
        arrive(Q1r.at[s, 0], r_q.at[s, 0])
        Q2s[s, 0, 0] = (CP[s, yl * XN + xp] + Q1r[s, 0].astype(F32)).astype(BF16)
        Q2s[s, 0, 1] = CP[s, (1 - yl) * XN + xp].astype(BF16)
        send(Q2s.at[s, 0], Q2r.at[s, 0], r_q.at[s, 2], to_xp, 1, 2)
        arrive(Q1r.at[s, 1], r_q.at[s, 1])
        Q2s[s, 1, 0] = CP[s, yl * XN + xm].astype(BF16)
        Q2s[s, 1, 1] = (CP[s, (1 - yl) * XN + xm] + Q1r[s, 1].astype(F32)).astype(BF16)
        send(Q2s.at[s, 1], Q2r.at[s, 1], r_q.at[s, 3], to_xm, 1, 2)

    def col_own(s):
        arrive(Q2r.at[s, 0], r_q.at[s, 2])
        arrive(Q2r.at[s, 1], r_q.at[s, 3])
        Q3s[s] = (CP[s, r_oth] + Q2r[s, 0, 1].astype(F32) + Q2r[s, 1, 1].astype(F32)).astype(BF16)
        send(Q3s.at[s], Q3r.at[s], r_q.at[s, 4], to_yl, 1, 1)
        VC[s] = CP[s, r_own] + Q2r[s, 0, 0].astype(F32) + Q2r[s, 1, 0].astype(F32)

    def cols_out(s):
        arrive(Q3r.at[s], r_q.at[s, 4])
        gc[s] = 0.5 * (VC[s] + Q3r[s].astype(F32))
        out_copy(1, s).start()

    for s in range(NS):
        send(row_block(s, 0, 0), row_block(s, 0, 0), r_row.at[s, 0, 1], to_yh, s)
        send_row(s, 0, 0, True)
        send_row(s, 0, 0, False)
        send(col_block(s, r_own), col_block(s, r_own), r_col.at[s, r_own], to_yl, s)
        send_col(s, r_own, True)
        send_col(s, r_own, False)
    preps(0, 1)
    row_step(0, 0, 1)
    col_y(0)
    row_y(0)
    row_step(1, 0, 1)
    preps(1, 2)
    row_step(0, 0, 2)
    col_x(0)
    row_y(1)
    col_y(1)
    row_step(1, 0, 2)
    preps(2, 3)
    row_step(0, 1, 1)
    row_core(0, 0)
    col_x(1)
    row_step(0, 0, 3)
    preps(3, 4)
    row_step(1, 1, 1)
    row_core(1, 0)
    row_step(1, 0, 3)
    preps(4, 5)
    all_cols(0)
    col_lines()
    turn(0)
    row_step(0, 1, 2)
    row_core(0, 1)
    preps(5, 6)

    def before(i):
        if i == 0:
            core_here(0, 0)
            lift(0)
        if i == 1:
            far_out(0)
            row_step(1, 1, 2)
            row_core(1, 1)
            all_cols(1)
            turn(1)
            core_here(1, 0)
        if i == 2:
            row_step(0, 1, 3)
            row_core(0, 2)
            far_out(1)
            core_here(0, 1)
            lift(2)
        if i == 3:
            row_step(1, 1, 3)
            row_core(1, 2)
            row_here(0, 1, H)
            row_core(0, 3)
            preps(6, 8)
            core_here(0, 2)
            lift(4)
        if i == 4:
            row_here(1, 1, H)
            row_core(1, 3)
            preps(8, 10)
            core_here(0, 3)
            lift(6)
        if i == 5:
            preps(10, 12)
            core_here(1, 3)
        if i == 6:
            ring(0, H)
            preps(12, 14)
            core_here(1, 2)
        if i == 7:
            ring(1, H)
            col_far(0)
            preps(14, 16)
            ring(0, 3)
            core_here(1, 1)

    def step(i, carry):
        for k in range(2 * H):
            pl.when(i == k)(functools.partial(before, k))
        s, j = turn_of(i)
        p = 2 * j
        unit(s, p)
        part = pl.ds(p, 2)
        send(CS.at[s, part], CR.at[s, part], r_cr.at[s, j], to_core, 1, 4 * 2 * H)
        return carry

    lax.fori_loop(0, 2 * H, step, 0)
    ring(1, 3)
    col_near(0)
    ring(0, 2)
    col_far(1)
    ring(1, 2)
    col_own(0)
    ring(0, 1)
    col_near(1)
    ring(1, 1)
    cols_out(0)
    ring(0, 0)
    col_own(1)
    ring(1, 0)
    rows_out(0)
    cols_out(1)
    rows_out(1)
    for k in range(2):
        for s in range(NS):
            out_copy(k, s).wait()
    arrive(cnt.at[pl.ds(0, total[0] * D * 2 // (CN * 4))], s_all)


def local(counts, re, ce, rm, cm, ra, ca, *, NZ, XN):
    S, B, D = re.shape
    CB = counts.shape[2]
    H = NZ // 2
    R = 2 * XN
    counts = counts.reshape(S, NZ, 4 * B, CB)
    sem = pltpu.SemaphoreType.DMA
    v = pltpu.VMEM
    scratch = [
        v((S, B, D), F32),
        v((S, B, D), F32),
        v((S, B), jnp.int32),
        v((S, B), jnp.int32),
        v((S * NZ * 4 * B, CB), jnp.int32),
        v((NZ, 2, 2, 2 * B + 16, D), BF16),
        v((R, 2 * B + 16, D), BF16),
        v((S, D, CB), BF16),
        v((S, CB, D), BF16),
        v((S, NZ, 4 * B, 128), F32),
        v((S, 1, CB), F32),
        v((S * NZ, 4 * B, CB), F32),
        v((S * NZ, 4 * B, CB), F32),
        v((S, NZ, 2, 2, B, D), F32),
        v((S, D, CB), F32),
        v((S, R, B, D), F32),
        v((S, NZ, 2, B, D), BF16),
        v((S, NZ, 2, B, D), BF16),
        v((S, H, 2, B, D), BF16),
        v((S, H, 2, B, D), BF16),
        v((S, H, 2, B, D), BF16),
        v((S, H, 2, B, D), BF16),
        v((S, B, D), BF16),
        v((S, B, D), BF16),
        v((S, 2, B, D), F32),
        v((S, 2, B, D), BF16),
        v((S, 2, B, D), BF16),
        v((S, 2, 2, B, D), BF16),
        v((S, 2, 2, B, D), BF16),
        v((S, B, D), BF16),
        v((S, B, D), BF16),
        v((S, B, D), F32),
        v((S, B, D), F32),
        v((S, B, D), F32),
        sem((4,)),
        sem((S * NZ,)),
        sem(()),
        sem((2, S)),
        sem((S, NZ, 2)),
        sem((S, H)),
        sem((S, R)),
        sem((S, H)),
        sem((S, H)),
        sem((S, H)),
        sem((S,)),
        sem((S, 5)),
    ]
    gr, gc = pl.pallas_call(
        functools.partial(kernel, NZ, XN, B, D, CB),
        out_shape=(jax.ShapeDtypeStruct((S, B, D), F32), jax.ShapeDtypeStruct((S, B, D), F32)),
        in_specs=[pl.BlockSpec(memory_space=pltpu.HBM)] * 5,
        out_specs=(pl.BlockSpec(memory_space=pltpu.HBM),) * 2,
        scratch_shapes=scratch,
        compiler_params=pltpu.CompilerParams(
            collective_id=0, has_side_effects=True, vmem_limit_bytes=60 * 1024 * 1024
        ),
    )(counts, re, ce, rm, cm)
    return adagrad(re, ra, gr), adagrad(ce, ca, gc)


def solution(mesh):
    return jax.shard_map(
        functools.partial(local, NZ=mesh.shape["col"] // 4, XN=mesh.shape["row"] // 2),
        mesh=mesh,
        in_specs=(
            P(None, "row", "col"),
            P(None, ("row", "col"), None),
            P(None, ("col", "row"), None),
            P(None, ("row", "col")),
            P(None, ("col", "row")),
            P(None, ("row", "col"), None),
            P(None, ("col", "row"), None),
        ),
        out_specs=(P(None, ("row", "col"), None), P(None, ("col", "row"), None)),
        check_vma=False,
    )
```

```python
import functools

import jax
import jax.numpy as jnp
from jax import lax
from jax.experimental import pallas as pl
from jax.experimental.pallas import tpu as pltpu
from jax.sharding import PartitionSpec as P

MESH = pl.DeviceIdType.MESH
F32 = jnp.float32
BF16 = jnp.bfloat16
NT = (((1,), (1,)), ((), ()))
NN = (((1,), (0,)), ((), ()))
TN = (((0,), (0,)), ((), ()))


def dot(a, b, dims):
    return lax.dot_general(a, b, dims, preferred_element_type=F32)


def update(g, a):
    return g / jnp.sqrt(a + g * g)


def kernel(
    NZ, XN, B, D, CN,
    counts, re_h, ce_h, rm_h, cm_h, ra_h, ca_h, nr, nc,
    re, ce, rm, cm, ra, ca,
    cnt, rows, cols, colsT, colsC, LRB, LC, PA, PB, RP, CPT, CP,
    CS, CR, RSp, RSm, RRp, RRm, YS, YR, VR, Q1s, Q1r, Q2s, Q2r, Q3s, Q3r, VC, gr, gc,
    s_in, s_cnt, s_all, s_out, r_row, r_core, r_col, r_cr, r_rp, r_rm, r_y, r_q,
):
    H = NZ // 2
    NS = 2
    row = lax.axis_index("row")
    col = lax.axis_index("col")
    x = lax.rem(row, XN)
    yl = row // XN
    z = col // 4
    yh = lax.rem(col // 2, 2)
    c = lax.rem(col, 2)
    oc = 1 - c
    xp = lax.rem(x + 1, XN)
    xm = lax.rem(x + XN - 1, XN)
    x2 = lax.rem(x + 2, XN)
    zp = lax.rem(z + 1, NZ)
    zm = lax.rem(z + NZ - 1, NZ)
    to_core = (row, col + 1 - 2 * c)
    to_yh = (row, col + 2 - 4 * yh)
    to_zp = (row, zp * 4 + yh * 2 + c)
    to_zm = (row, zm * 4 + yh * 2 + c)
    to_yl = ((1 - yl) * XN + x, col)
    to_xp = (yl * XN + xp, col)
    to_xm = (yl * XN + xm, col)
    r_own = yl * XN + x
    r_oth = (1 - yl) * XN + x

    def place(r):
        return 0 if r == 0 else 2 * r - 1 if r > 0 or r == -H else -2 * r

    def place_of(r):
        return place(H) if r == -H else place(r)

    def span(d):
        return (2 * d - 1, 2) if 0 < d < H else (place_of(d), 1)

    rel = [0]
    for d in range(1, H):
        rel += [d, -d]
    rel += [H]

    total = [0]

    def send(src, dst, rsem, dev, kind, count=1):
        pltpu.make_async_remote_copy(
            src_ref=src, dst_ref=dst, send_sem=s_all, recv_sem=rsem, device_id=dev, device_id_type=MESH
        ).start()
        total[0] += count * (B + 16 if kind == 0 else B)

    def arrive(dst, rsem):
        pltpu.make_async_copy(dst, dst, rsem).wait()

    own_in = [
        pltpu.make_async_copy(src, dst, s_in.at[i])
        for i, (src, dst) in enumerate(((rm_h, rm), (cm_h, cm), (re_h, re), (ce_h, ce), (ra_h, ra), (ca_h, ca)))
    ]
    for copy in own_in:
        copy.start()

    barrier = pltpu.get_barrier_semaphore()
    partners = [to_core, to_yh, to_zp, to_zm, to_yl, to_xp, to_xm]
    for dev in partners:
        pl.semaphore_signal(barrier, inc=1, device_id=dev, device_id_type=MESH)

    def turn_of(i):
        first, second, late = (i + 7) // 8, (i + 6) // 8, (i + 3) // 8
        return late + first - second, (1 - late) * (i - first) + late * (8 - i)

    def in_turn(u):
        s, j = turn_of(u // 2)
        return s * NZ + 2 * j + lax.rem(u, 2)

    def count_copy(u):
        q = in_turn(u)
        p = lax.rem(q, NZ)
        d = (p + 1) // 2
        zc = lax.rem(z + NZ + d * (2 * lax.rem(p, 2) - 1), NZ)
        at = pl.ds(pl.multiple_of(q * 4 * B, 4 * B), 4 * B)
        return pltpu.make_async_copy(counts.at[q // NZ, zc], cnt.at[at], s_cnt.at[q])

    AHEAD = 3
    for u in range(AHEAD):
        count_copy(u).start()

    for copy in own_in[:4]:
        copy.wait()

    def own_block(embed, margs, shift):
        line = jnp.concatenate([margs[0:1, :], margs[1:2, :]], axis=1).astype(F32)
        line = 0.5 * (jnp.log(line) - shift)
        hi = line.astype(BF16).astype(F32)
        mid = (line - hi).astype(BF16).astype(F32)
        upper = jnp.concatenate([hi, mid], axis=1)
        lower = jnp.concatenate([line - hi - mid, jnp.zeros_like(line)], axis=1)
        which = lax.broadcasted_iota(jnp.int32, (16, 4 * B), 0)
        tail = jnp.where(which == 0, upper, jnp.where(which == 1, lower, 0.0)).astype(BF16)
        return embed[0].astype(BF16), embed[1].astype(BF16), tail

    for ref, parts in ((rows.at[0, yh, c], own_block(re, rm, 20.0)), (cols.at[yl, x], own_block(ce, cm, 0.0))):
        ref[0:B] = parts[0]
        ref[B : B + 16] = parts[2]
        ref[B + 16 :] = parts[1]

    def line_of(tail):
        tail = tail.astype(F32)
        return tail[0:1, : 2 * B] + tail[0:1, 2 * B :] + tail[1:2, : 2 * B]

    pl.semaphore_wait(barrier, len(partners))

    def part(s):
        return pl.ds(0, B + 16) if s == 0 else pl.ds(B + 16, B)

    def row_block(s, p, y):
        return rows.at[p, 1 - yh if y else yh, c, part(s)]

    def send_row(s, y, r, up):
        to = place_of(r - 1 if up else r + 1)
        send(row_block(s, place(r), y), row_block(s, to, y), r_row.at[s, to, y], to_zp if up else to_zm, s)

    def row_here(s, y, r):
        arrive(row_block(s, place_of(r), y), r_row.at[s, place_of(r), y])

    def row_step(s, y, d):
        for sign in (-1, 1):
            row_here(s, y, sign * d)
            if d < H - 1 or (y == 0 and sign < 0):
                send_row(s, y, sign * d, sign < 0)

    def row_y(s):
        row_here(s, 1, 0)
        send_row(s, 1, 0, True)
        send_row(s, 1, 0, False)

    def far_out(s):
        row_here(s, 0, H)
        send(row_block(s, NZ - 1, 0), row_block(s, NZ - 1, 0), r_row.at[s, NZ - 1, 1], to_yh, s)

    def row_core(s, j):
        ref = rows.at[pl.ds(2 * j, 2), :, c, part(s)]
        send(ref, ref, r_core.at[s, j], to_core, s, 4)

    def core_here(s, j):
        arrive(rows.at[pl.ds(2 * j, 2), :, oc, part(s)], r_core.at[s, j])

    def col_block(s, y, at):
        return cols.at[y, at, part(s)]

    def col_pair(s, at):
        return cols.at[:, at, part(s)]

    def col_y(s):
        arrive(col_block(s, 1 - yl, x), r_col.at[s, 0])
        send(col_pair(s, x), col_pair(s, x), r_col.at[s, 1], to_xp, s, 2)
        send(col_pair(s, x), col_pair(s, x), r_col.at[s, 2], to_xm, s, 2)

    def col_x(s):
        arrive(col_pair(s, xp), r_col.at[s, 2])
        send(col_block(s, yl, xp), col_block(s, yl, xp), r_col.at[s, 3], to_xm, s)
        arrive(col_pair(s, xm), r_col.at[s, 1])
        send(col_block(s, 1 - yl, xm), col_block(s, 1 - yl, xm), r_col.at[s, 4], to_xp, s)

    def all_cols(s):
        arrive(col_block(s, yl, x2), r_col.at[s, 3])
        arrive(col_block(s, 1 - yl, x2), r_col.at[s, 4])

    def preps(lo, hi):
        def chunk(u, carry):
            @pl.when(u + AHEAD < NS * NZ)
            def _():
                count_copy(u + AHEAD).start()

            count_copy(u).wait()
            q = in_turn(u)

            def part(i, carry):
                at = pl.ds(pl.multiple_of(i * 128, 128), 128)
                n = cnt[pl.ds(pl.multiple_of(q * 4 * B + i * 128, 128), 128), :].astype(F32)
                m = jnp.maximum(n, 1.0)
                conf = jnp.where(n > 0, 0.4 + m * lax.rsqrt(m), 0.0)
                PA[q, at, :] = conf
                PB[q, at, :] = 0.5 * conf * jnp.log(m)
                return carry

            return lax.fori_loop(0, 4 * B // 128, part, carry)

        lax.fori_loop(lo, hi, chunk, 0)

    def halves(s, a, b):
        return jnp.concatenate([a[:, s * B : (s + 1) * B], b[:, s * B : (s + 1) * B]], axis=1)

    def col_lines():
        lines = [line_of(cols[r // XN, r % XN, B : B + 16]) for r in range(2 * XN)]
        for s in range(NS):
            for j in range(CN // 128):
                LC[s, :, j * 128 : (j + 1) * 128] = halves(s, lines[2 * j], lines[2 * j + 1])

    def lift(p):
        lines = [line_of(rows[p + q, y, k, B : B + 16]) for q in range(2) for y in range(2) for k in range(2)]
        wide = jnp.concatenate(lines, axis=0).T
        for i in range(8):
            for s in range(NS):
                column = wide[s * B : (s + 1) * B, i : i + 1]
                LRB[s, p + i // 4, i % 4 * B : (i % 4 + 1) * B, :] = jnp.broadcast_to(column, (B, 128))

    def turn(s):
        own = cols[:, :, s * (B + 16) : s * (B + 16) + B, :].reshape(CN, D)
        colsC[s] = own
        colsT[s] = (own * 0.5).T
        CPT[s] = jnp.zeros_like(CPT[s])

    def unit(s, p):
        pair = pl.ds(p, 2)
        left = rows[pair, :, :, pl.ds(pl.multiple_of(s * (B + 16), 16), B), :].reshape(8 * B, D)
        lr = LRB[s, pair].reshape(8 * B, 128)
        t = dot(left, colsT[s], NN) + jnp.concatenate([lr] * (CN // 128), axis=1) + LC[s]
        conf = PA[pl.ds(s * NZ + p, 2)].reshape(8 * B, CN)
        plain = PB[pl.ds(s * NZ + p, 2)].reshape(8 * B, CN)
        g = jnp.where(conf > 0, conf * t - plain, jnp.tanh(t) + 1.0).astype(BF16)
        RP[s, pair] = dot(g, colsC[s], NN).reshape(2, 2, 2, B, D)
        CS[s, pair] = RP[s, pair, :, oc].astype(BF16)
        CPT[s] += dot(left.T, g, NN)

    def sums_here(s, j):
        arrive(CR.at[s, pl.ds(2 * j, 2)], r_cr.at[s, j])

    def chip_sum(s, r):
        return RP[s, place(r), :, c] + CR[s, place(r)].astype(F32)

    def half_sum(s, r, y):
        return RP[s, place(r), y, c] + CR[s, place(r), y].astype(F32)

    halves_in_turn = (1 - yh, yh)

    def ring(s, d):
        if d > 0:
            sums_here(s, d - 1)
        lanes_of = ((RSp, RRp, r_rp, to_zp, 1), (RSm, RRm, r_rm, to_zm, -1))
        if d == H:
            v = chip_sum(s, H)
            for half, (RS, RR, rr, dev, _) in enumerate(lanes_of):
                RS[s, H - 1, half] = v[half].astype(BF16)
                send(RS.at[s, H - 1, half], RR.at[s, H - 1, half], rr.at[s, H - 1, 0], dev, 1, 1)
        elif d == H - 1:
            for half, (RS, RR, rr, dev, sign) in enumerate(lanes_of):
                v = chip_sum(s, sign * d)
                arrive(RR.at[s, d, half], rr.at[s, d, 0])
                RS[s, d - 1, half] = (v[half] + RR[s, d, half].astype(F32)).astype(BF16)
                RS[s, d - 1, 1 - half] = v[1 - half].astype(BF16)
                send(RS.at[s, d - 1], RR.at[s, d - 1], rr.at[s, d - 1, 0], dev, 1, 2)
        elif d > 0 and s == 0:
            for RS, RR, rr, dev, sign in lanes_of:
                v = chip_sum(s, sign * d)
                arrive(RR.at[s, d], rr.at[s, d, 0])
                RS[s, d - 1] = (v + RR[s, d].astype(F32)).astype(BF16)
                send(RS.at[s, d - 1], RR.at[s, d - 1], rr.at[s, d - 1, 0], dev, 1, 2)
        elif d > 0:
            for k, y in enumerate(halves_in_turn):
                for RS, RR, rr, dev, sign in lanes_of:
                    if d < H - 2:
                        arrive(RR.at[s, d, y], rr.at[s, d, k])
                    elif k == 0:
                        arrive(RR.at[s, d], rr.at[s, d, 0])
                    RS[s, d - 1, y] = (half_sum(s, sign * d, y) + RR[s, d, y].astype(F32)).astype(BF16)
                    send(RS.at[s, d - 1, y], RR.at[s, d - 1, y], rr.at[s, d - 1, k], dev, 1, 1)
        else:
            for k, y in enumerate(halves_in_turn):
                for _, RR, rr, _, _ in lanes_of:
                    if s == 1:
                        arrive(RR.at[s, 0, y], rr.at[s, 0, k])
                    elif k == 0:
                        arrive(RR.at[s, 0], rr.at[s, 0, 0])
                v = half_sum(s, 0, y) + RRp[s, 0, y].astype(F32) + RRm[s, 0, y].astype(F32)
                if k == 0:
                    YS[s] = v.astype(BF16)
                    send(YS.at[s], YR.at[s], r_y.at[s], to_yh, 1, 1)
                else:
                    VR[s] = v

    def out_copy(k, s):
        src, dst = ((gr, nr), (gc, nc))[k]
        return pltpu.make_async_copy(src.at[s], dst.at[s], s_out.at[k, s])

    def rows_out(s):
        arrive(YR.at[s], r_y.at[s])
        gr[s] = update(0.5 * (VR[s] + YR[s].astype(F32)), ra[s])
        out_copy(0, s).start()

    def col_far(s):
        CP[s] = CPT[s].T.reshape(2 * XN, B, D)
        Q1s[s, 0] = CP[s, yl * XN + x2].astype(BF16)
        send(Q1s.at[s, 0], Q1r.at[s, 0], r_q.at[s, 0], to_xp, 1, 1)
        Q1s[s, 1] = CP[s, (1 - yl) * XN + x2].astype(BF16)
        send(Q1s.at[s, 1], Q1r.at[s, 1], r_q.at[s, 1], to_xm, 1, 1)

    def col_near(s):
        arrive(Q1r.at[s, 0], r_q.at[s, 0])
        Q2s[s, 0, 0] = (CP[s, yl * XN + xp] + Q1r[s, 0].astype(F32)).astype(BF16)
        Q2s[s, 0, 1] = CP[s, (1 - yl) * XN + xp].astype(BF16)
        send(Q2s.at[s, 0], Q2r.at[s, 0], r_q.at[s, 2], to_xp, 1, 2)
        arrive(Q1r.at[s, 1], r_q.at[s, 1])
        Q2s[s, 1, 0] = CP[s, yl * XN + xm].astype(BF16)
        Q2s[s, 1, 1] = (CP[s, (1 - yl) * XN + xm] + Q1r[s, 1].astype(F32)).astype(BF16)
        send(Q2s.at[s, 1], Q2r.at[s, 1], r_q.at[s, 3], to_xm, 1, 2)

    def col_own(s):
        arrive(Q2r.at[s, 0], r_q.at[s, 2])
        arrive(Q2r.at[s, 1], r_q.at[s, 3])
        Q3s[s] = (CP[s, r_oth] + Q2r[s, 0, 1].astype(F32) + Q2r[s, 1, 1].astype(F32)).astype(BF16)
        send(Q3s.at[s], Q3r.at[s], r_q.at[s, 4], to_yl, 1, 1)
        VC[s] = CP[s, r_own] + Q2r[s, 0, 0].astype(F32) + Q2r[s, 1, 0].astype(F32)

    def cols_out(s):
        arrive(Q3r.at[s], r_q.at[s, 4])
        gc[s] = update(0.5 * (VC[s] + Q3r[s].astype(F32)), ca[s])
        out_copy(1, s).start()

    for s in range(NS):
        send(col_block(s, yl, x), col_block(s, yl, x), r_col.at[s, 0], to_yl, s)
        send(row_block(s, 0, 0), row_block(s, 0, 0), r_row.at[s, 0, 1], to_yh, s)
        send_row(s, 0, 0, True)
        send_row(s, 0, 0, False)
    preps(0, 1)
    col_y(0)
    row_step(0, 0, 1)
    row_y(0)
    row_step(1, 0, 1)
    col_y(1)
    preps(1, 2)
    row_step(0, 0, 2)
    col_x(0)
    row_y(1)
    row_step(1, 0, 2)
    preps(2, 3)
    row_step(0, 1, 1)
    row_core(0, 0)
    col_x(1)
    row_step(0, 0, 3)
    preps(3, 4)
    row_step(1, 1, 1)
    row_core(1, 0)
    row_step(1, 0, 3)
    preps(4, 5)
    all_cols(0)
    col_lines()
    turn(0)
    row_step(0, 1, 2)
    row_core(0, 1)
    preps(5, 6)

    def before(i):
        if i == 0:
            core_here(0, 0)
            lift(0)
        if i == 1:
            far_out(0)
            row_step(1, 1, 2)
            row_core(1, 1)
            all_cols(1)
            turn(1)
            core_here(1, 0)
        if i == 2:
            row_step(0, 1, 3)
            row_core(0, 2)
            far_out(1)
            core_here(0, 1)
            lift(2)
        if i == 3:
            row_step(1, 1, 3)
            row_core(1, 2)
            row_here(0, 1, H)
            row_core(0, 3)
            preps(6, 8)
            core_here(0, 2)
            lift(4)
        if i == 4:
            row_here(1, 1, H)
            row_core(1, 3)
            preps(8, 10)
            core_here(0, 3)
            lift(6)
        if i == 5:
            preps(10, 12)
            core_here(1, 3)
        if i == 6:
            ring(0, H)
            preps(12, 14)
            core_here(1, 2)
        if i == 7:
            ring(1, H)
            col_far(0)
            preps(14, 16)
            ring(0, 3)
            core_here(1, 1)

    def step(i, carry):
        for k in range(2 * H):
            pl.when(i == k)(functools.partial(before, k))
        s, j = turn_of(i)
        p = 2 * j
        unit(s, p)
        part = pl.ds(p, 2)
        send(CS.at[s, part], CR.at[s, part], r_cr.at[s, j], to_core, 1, 4 * 2 * H)
        return carry

    lax.fori_loop(0, 2 * H, step, 0)
    for copy in own_in[4:]:
        copy.wait()
    ring(1, 3)
    col_near(0)
    ring(0, 2)
    col_far(1)
    ring(1, 2)
    col_own(0)
    ring(0, 1)
    col_near(1)
    ring(1, 1)
    cols_out(0)
    ring(0, 0)
    col_own(1)
    ring(1, 0)
    rows_out(0)
    cols_out(1)
    rows_out(1)
    for k in range(2):
        for s in range(NS):
            out_copy(k, s).wait()
    arrive(cnt.at[pl.ds(0, total[0] * D * 2 // (CN * 4))], s_all)


def local(counts, re, ce, rm, cm, ra, ca, *, NZ, XN):
    S, B, D = re.shape
    CB = counts.shape[2]
    H = NZ // 2
    R = 2 * XN
    counts = counts.reshape(S, NZ, 4 * B, CB)
    sem = pltpu.SemaphoreType.DMA
    v = pltpu.VMEM
    scratch = [
        v((S, B, D), F32),
        v((S, B, D), F32),
        v((S, B), jnp.int32),
        v((S, B), jnp.int32),
        v((S, B, D), F32),
        v((S, B, D), F32),
        v((S * NZ * 4 * B, CB), jnp.int32),
        v((NZ, 2, 2, 2 * B + 16, D), BF16),
        v((2, XN, 2 * B + 16, D), BF16),
        v((S, D, CB), BF16),
        v((S, CB, D), BF16),
        v((S, NZ, 4 * B, 128), F32),
        v((S, 1, CB), F32),
        v((S * NZ, 4 * B, CB), F32),
        v((S * NZ, 4 * B, CB), F32),
        v((S, NZ, 2, 2, B, D), F32),
        v((S, D, CB), F32),
        v((S, R, B, D), F32),
        v((S, NZ, 2, B, D), BF16),
        v((S, NZ, 2, B, D), BF16),
        v((S, H, 2, B, D), BF16),
        v((S, H, 2, B, D), BF16),
        v((S, H, 2, B, D), BF16),
        v((S, H, 2, B, D), BF16),
        v((S, B, D), BF16),
        v((S, B, D), BF16),
        v((S, B, D), F32),
        v((S, 2, B, D), BF16),
        v((S, 2, B, D), BF16),
        v((S, 2, 2, B, D), BF16),
        v((S, 2, 2, B, D), BF16),
        v((S, B, D), BF16),
        v((S, B, D), BF16),
        v((S, B, D), F32),
        v((S, B, D), F32),
        v((S, B, D), F32),
        sem((6,)),
        sem((S * NZ,)),
        sem(()),
        sem((2, S)),
        sem((S, NZ, 2)),
        sem((S, H)),
        sem((S, 5)),
        sem((S, H)),
        sem((S, H, 2)),
        sem((S, H, 2)),
        sem((S,)),
        sem((S, 5)),
    ]
    gr, gc = pl.pallas_call(
        functools.partial(kernel, NZ, XN, B, D, CB),
        out_shape=(jax.ShapeDtypeStruct((S, B, D), F32), jax.ShapeDtypeStruct((S, B, D), F32)),
        in_specs=[pl.BlockSpec(memory_space=pltpu.HBM)] * 7,
        out_specs=(pl.BlockSpec(memory_space=pltpu.HBM),) * 2,
        scratch_shapes=scratch,
        compiler_params=pltpu.CompilerParams(
            collective_id=0, has_side_effects=True, vmem_limit_bytes=60 * 1024 * 1024
        ),
    )(counts, re, ce, rm, cm, ra, ca)
    return re - gr, ce - gc


def solution(mesh):
    return jax.shard_map(
        functools.partial(local, NZ=mesh.shape["col"] // 4, XN=mesh.shape["row"] // 2),
        mesh=mesh,
        in_specs=(
            P(None, "row", "col"),
            P(None, ("row", "col"), None),
            P(None, ("col", "row"), None),
            P(None, ("row", "col")),
            P(None, ("col", "row")),
            P(None, ("row", "col"), None),
            P(None, ("col", "row"), None),
        ),
        out_specs=(P(None, ("row", "col"), None), P(None, ("col", "row"), None)),
        check_vma=False,
    )
```

```python
import functools

import jax
import jax.numpy as jnp
from jax import lax
from jax.experimental import pallas as pl
from jax.experimental.pallas import tpu as pltpu
from jax.sharding import PartitionSpec as P

MESH = pl.DeviceIdType.MESH
F32 = jnp.float32
BF16 = jnp.bfloat16
NT = (((1,), (1,)), ((), ()))
NN = (((1,), (0,)), ((), ()))
TN = (((0,), (0,)), ((), ()))


def dot(a, b, dims):
    return lax.dot_general(a, b, dims, preferred_element_type=F32)


def adagrad(w, a, g):
    return w - g / jnp.sqrt(a + g * g)


def kernel(
    NZ, XN, B, D, CN,
    counts, re_h, ce_h, rm_h, cm_h, nr, nc,
    re, ce, rm, cm,
    cnt, rows, cols, colsT, colsC, LRB, LC, RP, CPT, CP,
    CS, CR, RSp, RSm, RRp, RRm, YS, YR, VR, Q1s, Q1r, Q2s, Q2r, Q3s, Q3r, VC, gr, gc,
    s_in, s_cnt, s_all, s_out, r_row, r_core, r_col, r_cr, r_rp, r_rm, r_y, r_q,
):
    H = NZ // 2
    NS = 2
    row = lax.axis_index("row")
    col = lax.axis_index("col")
    x = lax.rem(row, XN)
    yl = row // XN
    z = col // 4
    yh = lax.rem(col // 2, 2)
    c = lax.rem(col, 2)
    oc = 1 - c
    xp = lax.rem(x + 1, XN)
    xm = lax.rem(x + XN - 1, XN)
    x2 = lax.rem(x + 2, XN)
    zp = lax.rem(z + 1, NZ)
    zm = lax.rem(z + NZ - 1, NZ)
    to_core = (row, col + 1 - 2 * c)
    to_yh = (row, col + 2 - 4 * yh)
    to_zp = (row, zp * 4 + yh * 2 + c)
    to_zm = (row, zm * 4 + yh * 2 + c)
    to_yl = ((1 - yl) * XN + x, col)
    to_xp = (yl * XN + xp, col)
    to_xm = (yl * XN + xm, col)
    r_own = yl * XN + x
    r_oth = (1 - yl) * XN + x

    def place(r):
        return 0 if r == 0 else 2 * r - 1 if r > 0 or r == -H else -2 * r

    def place_of(r):
        return place(H) if r == -H else place(r)

    def span(d):
        return (2 * d - 1, 2) if 0 < d < H else (place_of(d), 1)

    rel = [0]
    for d in range(1, H):
        rel += [d, -d]
    rel += [H]

    total = [0]

    def send(src, dst, rsem, dev, kind, count=1):
        pltpu.make_async_remote_copy(
            src_ref=src, dst_ref=dst, send_sem=s_all, recv_sem=rsem, device_id=dev, device_id_type=MESH
        ).start()
        total[0] += count * (B + 16 if kind == 0 else B)

    def arrive(dst, rsem):
        pltpu.make_async_copy(dst, dst, rsem).wait()

    own_in = [
        pltpu.make_async_copy(src, dst, s_in.at[i])
        for i, (src, dst) in enumerate(((rm_h, rm), (cm_h, cm), (re_h, re), (ce_h, ce)))
    ]
    for copy in own_in:
        copy.start()

    barrier = pltpu.get_barrier_semaphore()
    partners = [to_core, to_yh, to_zp, to_zm, to_yl, to_xp, to_xm]
    for dev in partners:
        pl.semaphore_signal(barrier, inc=1, device_id=dev, device_id_type=MESH)

    def turn_of(i):
        first, second, late = (i + 7) // 8, (i + 6) // 8, (i + 3) // 8
        return late + first - second, (1 - late) * (i - first) + late * (8 - i)

    def in_turn(u):
        s, j = turn_of(u // 2)
        return s * NZ + 2 * j + lax.rem(u, 2)

    def count_copy(u):
        q = in_turn(u)
        p = lax.rem(q, NZ)
        d = (p + 1) // 2
        zc = lax.rem(z + NZ + d * (2 * lax.rem(p, 2) - 1), NZ)
        at = pl.ds(pl.multiple_of(q * 4 * B, 4 * B), 4 * B)
        return pltpu.make_async_copy(counts.at[q // NZ, zc], cnt.at[at], s_cnt.at[q])

    def counts_out(lo, hi):
        for u in range(lo, hi):
            count_copy(u).start()

    counts_out(0, 3)

    for copy in own_in:
        copy.wait()

    def own_block(embed, margs, shift):
        line = jnp.concatenate([margs[0:1, :], margs[1:2, :]], axis=1).astype(F32)
        line = 0.5 * (jnp.log(line) - shift)
        hi = line.astype(BF16).astype(F32)
        mid = (line - hi).astype(BF16).astype(F32)
        upper = jnp.concatenate([hi, mid], axis=1)
        lower = jnp.concatenate([line - hi - mid, jnp.zeros_like(line)], axis=1)
        which = lax.broadcasted_iota(jnp.int32, (16, 4 * B), 0)
        tail = jnp.where(which == 0, upper, jnp.where(which == 1, lower, 0.0)).astype(BF16)
        return embed[0].astype(BF16), embed[1].astype(BF16), tail

    for ref, parts in ((rows.at[0, yh, c], own_block(re, rm, 20.0)), (cols.at[yl, x], own_block(ce, cm, 0.0))):
        ref[0:B] = parts[0]
        ref[B : B + 16] = parts[2]
        ref[B + 16 :] = parts[1]

    def line_of(tail):
        tail = tail.astype(F32)
        return tail[0:1, : 2 * B] + tail[0:1, 2 * B :] + tail[1:2, : 2 * B]

    pl.semaphore_wait(barrier, len(partners))

    def part(s):
        return pl.ds(0, B + 16) if s == 0 else pl.ds(B + 16, B)

    def row_block(s, p, y):
        return rows.at[p, 1 - yh if y else yh, c, part(s)]

    def send_row(s, y, r, up):
        to = place_of(r - 1 if up else r + 1)
        send(row_block(s, place(r), y), row_block(s, to, y), r_row.at[s, to, y], to_zp if up else to_zm, s)

    def row_here(s, y, r):
        arrive(row_block(s, place_of(r), y), r_row.at[s, place_of(r), y])

    def row_step(s, y, d):
        for sign in (-1, 1):
            row_here(s, y, sign * d)
            if d < H - 1 or (y == 0 and sign < 0):
                send_row(s, y, sign * d, sign < 0)

    def row_y(s):
        row_here(s, 1, 0)
        send_row(s, 1, 0, True)
        send_row(s, 1, 0, False)

    def far_out(s):
        row_here(s, 0, H)
        send(row_block(s, NZ - 1, 0), row_block(s, NZ - 1, 0), r_row.at[s, NZ - 1, 1], to_yh, s)

    def row_core(s, j):
        ref = rows.at[pl.ds(2 * j, 2), :, c, part(s)]
        send(ref, ref, r_core.at[s, j], to_core, s, 4)

    def core_here(s, j):
        arrive(rows.at[pl.ds(2 * j, 2), :, oc, part(s)], r_core.at[s, j])

    def col_block(s, y, at):
        return cols.at[y, at, part(s)]

    def col_pair(s, at):
        return cols.at[:, at, part(s)]

    def col_y(s):
        arrive(col_block(s, 1 - yl, x), r_col.at[s, 0])
        send(col_pair(s, x), col_pair(s, x), r_col.at[s, 1], to_xp, s, 2)
        send(col_pair(s, x), col_pair(s, x), r_col.at[s, 2], to_xm, s, 2)

    def col_x(s):
        arrive(col_pair(s, xp), r_col.at[s, 2])
        send(col_block(s, yl, xp), col_block(s, yl, xp), r_col.at[s, 3], to_xm, s)
        arrive(col_pair(s, xm), r_col.at[s, 1])
        send(col_block(s, 1 - yl, xm), col_block(s, 1 - yl, xm), r_col.at[s, 4], to_xp, s)

    def all_cols(s):
        arrive(col_block(s, yl, x2), r_col.at[s, 3])
        arrive(col_block(s, 1 - yl, x2), r_col.at[s, 4])

    def halves(s, a, b):
        return jnp.concatenate([a[:, s * B : (s + 1) * B], b[:, s * B : (s + 1) * B]], axis=1)

    def col_lines():
        lines = [line_of(cols[r // XN, r % XN, B : B + 16]) for r in range(2 * XN)]
        for s in range(NS):
            for j in range(CN // 128):
                LC[s, :, j * 128 : (j + 1) * 128] = halves(s, lines[2 * j], lines[2 * j + 1])

    def lift(p):
        lines = [line_of(rows[p + q, y, k, B : B + 16]) for q in range(2) for y in range(2) for k in range(2)]
        wide = jnp.concatenate(lines, axis=0).T
        for i in range(8):
            for s in range(NS):
                column = wide[s * B : (s + 1) * B, i : i + 1]
                LRB[s, p + i // 4, i % 4 * B : (i % 4 + 1) * B, :] = jnp.broadcast_to(column, (B, 128))

    def turn(s):
        own = cols[:, :, s * (B + 16) : s * (B + 16) + B, :].reshape(CN, D)
        colsC[s] = own
        colsT[s] = (own * 0.5).T
        CPT[s] = jnp.zeros_like(CPT[s])

    def unit(s, p):
        pair = pl.ds(p, 2)
        left = rows[pair, :, :, pl.ds(pl.multiple_of(s * (B + 16), 16), B), :].reshape(8 * B, D)
        lr = LRB[s, pair].reshape(8 * B, 128)
        t = dot(left, colsT[s], NN) + jnp.concatenate([lr] * (CN // 128), axis=1) + LC[s]
        n = cnt[pl.ds(pl.multiple_of((s * NZ + p) * 4 * B, 8 * B), 8 * B), :].astype(F32)
        m = jnp.maximum(n, 1.0)
        there = (0.4 + m * lax.rsqrt(m)) * (t - 0.5 * jnp.log(m))
        g = jnp.where(n > 0, there, jnp.tanh(t) + 1.0).astype(BF16)
        RP[s, pair] = dot(g, colsC[s], NN).reshape(2, 2, 2, B, D)
        CS[s, pair] = RP[s, pair, :, oc].astype(BF16)
        CPT[s] += dot(left.T, g, NN)

    def sums_here(s, j):
        arrive(CR.at[s, pl.ds(2 * j, 2)], r_cr.at[s, j])

    def chip_sum(s, r):
        return RP[s, place(r), :, c] + CR[s, place(r)].astype(F32)

    def half_sum(s, r, y):
        return RP[s, place(r), y, c] + CR[s, place(r), y].astype(F32)

    halves_in_turn = (1 - yh, yh)

    def ring(s, d):
        if d > 0:
            sums_here(s, d - 1)
        lanes_of = ((RSp, RRp, r_rp, to_zp, 1), (RSm, RRm, r_rm, to_zm, -1))
        if d == H:
            v = chip_sum(s, H)
            for half, (RS, RR, rr, dev, _) in enumerate(lanes_of):
                RS[s, H - 1, half] = v[half].astype(BF16)
                send(RS.at[s, H - 1, half], RR.at[s, H - 1, half], rr.at[s, H - 1, 0], dev, 1, 1)
        elif d == H - 1:
            for half, (RS, RR, rr, dev, sign) in enumerate(lanes_of):
                v = chip_sum(s, sign * d)
                arrive(RR.at[s, d, half], rr.at[s, d, 0])
                RS[s, d - 1, half] = (v[half] + RR[s, d, half].astype(F32)).astype(BF16)
                RS[s, d - 1, 1 - half] = v[1 - half].astype(BF16)
                send(RS.at[s, d - 1], RR.at[s, d - 1], rr.at[s, d - 1, 0], dev, 1, 2)
        elif d > 0 and s == 0:
            for RS, RR, rr, dev, sign in lanes_of:
                v = chip_sum(s, sign * d)
                arrive(RR.at[s, d], rr.at[s, d, 0])
                RS[s, d - 1] = (v + RR[s, d].astype(F32)).astype(BF16)
                send(RS.at[s, d - 1], RR.at[s, d - 1], rr.at[s, d - 1, 0], dev, 1, 2)
        elif d > 0:
            for k, y in enumerate(halves_in_turn):
                for RS, RR, rr, dev, sign in lanes_of:
                    if d < H - 2:
                        arrive(RR.at[s, d, y], rr.at[s, d, k])
                    elif k == 0:
                        arrive(RR.at[s, d], rr.at[s, d, 0])
                    RS[s, d - 1, y] = (half_sum(s, sign * d, y) + RR[s, d, y].astype(F32)).astype(BF16)
                    send(RS.at[s, d - 1, y], RR.at[s, d - 1, y], rr.at[s, d - 1, k], dev, 1, 1)
        else:
            for k, y in enumerate(halves_in_turn):
                for _, RR, rr, _, _ in lanes_of:
                    if s == 1:
                        arrive(RR.at[s, 0, y], rr.at[s, 0, k])
                    elif k == 0:
                        arrive(RR.at[s, 0], rr.at[s, 0, 0])
                v = half_sum(s, 0, y) + RRp[s, 0, y].astype(F32) + RRm[s, 0, y].astype(F32)
                if k == 0:
                    YS[s] = v.astype(BF16)
                    send(YS.at[s], YR.at[s], r_y.at[s], to_yh, 1, 1)
                else:
                    VR[s] = v

    def out_copy(k, s):
        src, dst = ((gr, nr), (gc, nc))[k]
        return pltpu.make_async_copy(src.at[s], dst.at[s], s_out.at[k, s])

    def rows_out(s):
        arrive(YR.at[s], r_y.at[s])
        gr[s] = 0.5 * (VR[s] + YR[s].astype(F32))
        out_copy(0, s).start()

    def col_far(s):
        CP[s] = CPT[s].T.reshape(2 * XN, B, D)
        Q1s[s, 0] = CP[s, yl * XN + x2].astype(BF16)
        send(Q1s.at[s, 0], Q1r.at[s, 0], r_q.at[s, 0], to_xp, 1, 1)
        Q1s[s, 1] = CP[s, (1 - yl) * XN + x2].astype(BF16)
        send(Q1s.at[s, 1], Q1r.at[s, 1], r_q.at[s, 1], to_xm, 1, 1)

    def col_near(s):
        arrive(Q1r.at[s, 0], r_q.at[s, 0])
        Q2s[s, 0, 0] = (CP[s, yl * XN + xp] + Q1r[s, 0].astype(F32)).astype(BF16)
        Q2s[s, 0, 1] = CP[s, (1 - yl) * XN + xp].astype(BF16)
        send(Q2s.at[s, 0], Q2r.at[s, 0], r_q.at[s, 2], to_xp, 1, 2)
        arrive(Q1r.at[s, 1], r_q.at[s, 1])
        Q2s[s, 1, 0] = CP[s, yl * XN + xm].astype(BF16)
        Q2s[s, 1, 1] = (CP[s, (1 - yl) * XN + xm] + Q1r[s, 1].astype(F32)).astype(BF16)
        send(Q2s.at[s, 1], Q2r.at[s, 1], r_q.at[s, 3], to_xm, 1, 2)

    def col_own(s):
        arrive(Q2r.at[s, 0], r_q.at[s, 2])
        arrive(Q2r.at[s, 1], r_q.at[s, 3])
        Q3s[s] = (CP[s, r_oth] + Q2r[s, 0, 1].astype(F32) + Q2r[s, 1, 1].astype(F32)).astype(BF16)
        send(Q3s.at[s], Q3r.at[s], r_q.at[s, 4], to_yl, 1, 1)
        VC[s] = CP[s, r_own] + Q2r[s, 0, 0].astype(F32) + Q2r[s, 1, 0].astype(F32)

    def cols_out(s):
        arrive(Q3r.at[s], r_q.at[s, 4])
        gc[s] = 0.5 * (VC[s] + Q3r[s].astype(F32))
        out_copy(1, s).start()

    for s in range(NS):
        send(col_block(s, yl, x), col_block(s, yl, x), r_col.at[s, 0], to_yl, s)
        send(row_block(s, 0, 0), row_block(s, 0, 0), r_row.at[s, 0, 1], to_yh, s)
        send_row(s, 0, 0, True)
        send_row(s, 0, 0, False)
    col_y(0)
    row_step(0, 0, 1)
    row_y(0)
    row_step(1, 0, 1)
    col_y(1)
    counts_out(3, 6)
    row_step(0, 0, 2)
    col_x(0)
    row_y(1)
    row_step(1, 0, 2)
    row_step(0, 1, 1)
    row_core(0, 0)
    col_x(1)
    counts_out(6, 9)
    row_step(0, 0, 3)
    row_step(1, 1, 1)
    row_core(1, 0)
    row_step(1, 0, 3)
    all_cols(0)
    col_lines()
    turn(0)
    counts_out(9, 12)
    row_step(0, 1, 2)
    row_core(0, 1)

    def before(i):
        if i == 0:
            core_here(0, 0)
            lift(0)
        if i == 1:
            counts_out(12, 16)
            far_out(0)
            row_step(1, 1, 2)
            row_core(1, 1)
            all_cols(1)
            turn(1)
            core_here(1, 0)
        if i == 2:
            row_step(0, 1, 3)
            row_core(0, 2)
            far_out(1)
            core_here(0, 1)
            lift(2)
        if i == 3:
            row_step(1, 1, 3)
            row_core(1, 2)
            row_here(0, 1, H)
            row_core(0, 3)
            core_here(0, 2)
            lift(4)
        if i == 4:
            row_here(1, 1, H)
            row_core(1, 3)
            core_here(0, 3)
            lift(6)
        if i == 5:
            core_here(1, 3)
        if i == 6:
            ring(0, H)
            core_here(1, 2)
        if i == 7:
            ring(1, H)
            col_far(0)
            ring(0, 3)
            core_here(1, 1)

    def step(i, carry):
        for k in range(2 * H):
            pl.when(i == k)(functools.partial(before, k))
        s, j = turn_of(i)
        p = 2 * j
        count_copy(2 * i).wait()
        count_copy(2 * i + 1).wait()
        unit(s, p)
        part = pl.ds(p, 2)
        send(CS.at[s, part], CR.at[s, part], r_cr.at[s, j], to_core, 1, 4 * 2 * H)
        return carry

    lax.fori_loop(0, 2 * H, step, 0)
    ring(1, 3)
    col_near(0)
    ring(0, 2)
    col_far(1)
    ring(1, 2)
    col_own(0)
    ring(0, 1)
    col_near(1)
    ring(1, 1)
    cols_out(0)
    ring(0, 0)
    col_own(1)
    ring(1, 0)
    rows_out(0)
    cols_out(1)
    rows_out(1)
    for k in range(2):
        for s in range(NS):
            out_copy(k, s).wait()
    arrive(cnt.at[pl.ds(0, total[0] * D * 2 // (CN * 4))], s_all)


def local(counts, re, ce, rm, cm, ra, ca, *, NZ, XN):
    S, B, D = re.shape
    CB = counts.shape[2]
    H = NZ // 2
    R = 2 * XN
    counts = counts.reshape(S, NZ, 4 * B, CB)
    sem = pltpu.SemaphoreType.DMA
    v = pltpu.VMEM
    scratch = [
        v((S, B, D), F32),
        v((S, B, D), F32),
        v((S, B), jnp.int32),
        v((S, B), jnp.int32),
        v((S * NZ * 4 * B, CB), jnp.int32),
        v((NZ, 2, 2, 2 * B + 16, D), BF16),
        v((2, XN, 2 * B + 16, D), BF16),
        v((S, D, CB), BF16),
        v((S, CB, D), BF16),
        v((S, NZ, 4 * B, 128), F32),
        v((S, 1, CB), F32),
        v((S, NZ, 2, 2, B, D), F32),
        v((S, D, CB), F32),
        v((S, R, B, D), F32),
        v((S, NZ, 2, B, D), BF16),
        v((S, NZ, 2, B, D), BF16),
        v((S, H, 2, B, D), BF16),
        v((S, H, 2, B, D), BF16),
        v((S, H, 2, B, D), BF16),
        v((S, H, 2, B, D), BF16),
        v((S, B, D), BF16),
        v((S, B, D), BF16),
        v((S, B, D), F32),
        v((S, 2, B, D), BF16),
        v((S, 2, B, D), BF16),
        v((S, 2, 2, B, D), BF16),
        v((S, 2, 2, B, D), BF16),
        v((S, B, D), BF16),
        v((S, B, D), BF16),
        v((S, B, D), F32),
        v((S, B, D), F32),
        v((S, B, D), F32),
        sem((4,)),
        sem((S * NZ,)),
        sem(()),
        sem((2, S)),
        sem((S, NZ, 2)),
        sem((S, H)),
        sem((S, 5)),
        sem((S, H)),
        sem((S, H, 2)),
        sem((S, H, 2)),
        sem((S,)),
        sem((S, 5)),
    ]
    gr, gc = pl.pallas_call(
        functools.partial(kernel, NZ, XN, B, D, CB),
        out_shape=(jax.ShapeDtypeStruct((S, B, D), F32), jax.ShapeDtypeStruct((S, B, D), F32)),
        in_specs=[pl.BlockSpec(memory_space=pltpu.HBM)] * 5,
        out_specs=(pl.BlockSpec(memory_space=pltpu.HBM),) * 2,
        scratch_shapes=scratch,
        compiler_params=pltpu.CompilerParams(
            collective_id=0, has_side_effects=True, vmem_limit_bytes=60 * 1024 * 1024
        ),
    )(counts, re, ce, rm, cm)
    return adagrad(re, ra, gr), adagrad(ce, ca, gc)


def solution(mesh):
    return jax.shard_map(
        functools.partial(local, NZ=mesh.shape["col"] // 4, XN=mesh.shape["row"] // 2),
        mesh=mesh,
        in_specs=(
            P(None, "row", "col"),
            P(None, ("row", "col"), None),
            P(None, ("col", "row"), None),
            P(None, ("row", "col")),
            P(None, ("col", "row")),
            P(None, ("row", "col"), None),
            P(None, ("col", "row"), None),
        ),
        out_specs=(P(None, ("row", "col"), None), P(None, ("col", "row"), None)),
        check_vma=False,
    )
```

```python
import functools

import jax
import jax.numpy as jnp
from jax import lax
from jax.experimental import pallas as pl
from jax.experimental.pallas import tpu as pltpu
from jax.sharding import PartitionSpec as P

MESH = pl.DeviceIdType.MESH
F32 = jnp.float32
BF16 = jnp.bfloat16
NT = (((1,), (1,)), ((), ()))
NN = (((1,), (0,)), ((), ()))
TN = (((0,), (0,)), ((), ()))


def dot(a, b, dims):
    return lax.dot_general(a, b, dims, preferred_element_type=F32)


def adagrad(w, a, g):
    return w - g / jnp.sqrt(a + g * g)


def kernel(
    NZ, XN, B, D, CN,
    counts, re_h, ce_h, rm_h, cm_h, nr, nc,
    re, ce, rm, cm,
    cnt, rows, cols, colsT, colsC, LRB, LC, RP, CPT, CP,
    CS, CR, RSp, RSm, RRp, RRm, YS, YR, VR, Q1s, Q1r, Q2s, Q2r, Q3s, Q3r, VC, gr, gc,
    s_in, s_cnt, s_all, s_out, r_row, r_core, r_col, r_cr, r_rp, r_rm, r_y, r_q,
):
    H = NZ // 2
    NS = 2
    row = lax.axis_index("row")
    col = lax.axis_index("col")
    x = lax.rem(row, XN)
    yl = row // XN
    z = col // 4
    yh = lax.rem(col // 2, 2)
    c = lax.rem(col, 2)
    oc = 1 - c
    xp = lax.rem(x + 1, XN)
    xm = lax.rem(x + XN - 1, XN)
    x2 = lax.rem(x + 2, XN)
    zp = lax.rem(z + 1, NZ)
    zm = lax.rem(z + NZ - 1, NZ)
    to_core = (row, col + 1 - 2 * c)
    to_yh = (row, col + 2 - 4 * yh)
    to_zp = (row, zp * 4 + yh * 2 + c)
    to_zm = (row, zm * 4 + yh * 2 + c)
    to_yl = ((1 - yl) * XN + x, col)
    to_xp = (yl * XN + xp, col)
    to_xm = (yl * XN + xm, col)
    r_own = yl * XN + x
    r_oth = (1 - yl) * XN + x

    def place(r):
        return 0 if r == 0 else 2 * r - 1 if r > 0 or r == -H else -2 * r

    def place_of(r):
        return place(H) if r == -H else place(r)

    def span(d):
        return (2 * d - 1, 2) if 0 < d < H else (place_of(d), 1)

    rel = [0]
    for d in range(1, H):
        rel += [d, -d]
    rel += [H]

    total = [0]

    def send(src, dst, rsem, dev, kind, count=1):
        pltpu.make_async_remote_copy(
            src_ref=src, dst_ref=dst, send_sem=s_all, recv_sem=rsem, device_id=dev, device_id_type=MESH
        ).start()
        total[0] += count * (B + 16 if kind == 0 else B)

    def arrive(dst, rsem):
        pltpu.make_async_copy(dst, dst, rsem).wait()

    own_in = [
        pltpu.make_async_copy(src, dst, s_in.at[i])
        for i, (src, dst) in enumerate(((rm_h, rm), (cm_h, cm), (re_h, re), (ce_h, ce)))
    ]
    for copy in own_in:
        copy.start()

    barrier = pltpu.get_barrier_semaphore()
    partners = [to_core, to_yh, to_zp, to_zm, to_yl, to_xp, to_xm]
    for dev in partners:
        pl.semaphore_signal(barrier, inc=1, device_id=dev, device_id_type=MESH)

    def turn_of(i):
        s = i // H
        return s, i * (1 - s) + (2 * H - 1 - i) * s

    def in_turn(u):
        s, j = turn_of(u // 2)
        return s * NZ + 2 * j + lax.rem(u, 2)

    def count_copy(u):
        q = in_turn(u)
        p = lax.rem(q, NZ)
        d = (p + 1) // 2
        zc = lax.rem(z + NZ + d * (2 * lax.rem(p, 2) - 1), NZ)
        at = pl.ds(pl.multiple_of(q * 4 * B, 4 * B), 4 * B)
        return pltpu.make_async_copy(counts.at[q // NZ, zc], cnt.at[at], s_cnt.at[q])

    def counts_out(lo, hi):
        for u in range(lo, hi):
            count_copy(u).start()

    counts_out(0, 3)

    for copy in own_in:
        copy.wait()

    def own_block(embed, margs, shift):
        line = jnp.concatenate([margs[0:1, :], margs[1:2, :]], axis=1).astype(F32)
        line = 0.5 * (jnp.log(line) - shift)
        hi = line.astype(BF16).astype(F32)
        mid = (line - hi).astype(BF16).astype(F32)
        upper = jnp.concatenate([hi, mid], axis=1)
        lower = jnp.concatenate([line - hi - mid, jnp.zeros_like(line)], axis=1)
        which = lax.broadcasted_iota(jnp.int32, (16, 4 * B), 0)
        tail = jnp.where(which == 0, upper, jnp.where(which == 1, lower, 0.0)).astype(BF16)
        return embed[0].astype(BF16), embed[1].astype(BF16), tail

    for ref, parts in ((rows.at[0, yh, c], own_block(re, rm, 20.0)), (cols.at[yl, x], own_block(ce, cm, 0.0))):
        ref[0:B] = parts[0]
        ref[B : B + 16] = parts[2]
        ref[B + 16 :] = parts[1]

    def line_of(tail):
        tail = tail.astype(F32)
        return tail[0:1, : 2 * B] + tail[0:1, 2 * B :] + tail[1:2, : 2 * B]

    pl.semaphore_wait(barrier, len(partners))

    def part(s):
        return pl.ds(0, B + 16) if s == 0 else pl.ds(B + 16, B)

    def row_block(s, p, y):
        return rows.at[p, 1 - yh if y else yh, c, part(s)]

    def send_row(s, y, r, up):
        to = place_of(r - 1 if up else r + 1)
        send(row_block(s, place(r), y), row_block(s, to, y), r_row.at[s, to, y], to_zp if up else to_zm, s)

    def row_here(s, y, r):
        arrive(row_block(s, place_of(r), y), r_row.at[s, place_of(r), y])

    def row_step(s, y, d):
        for sign in (-1, 1):
            row_here(s, y, sign * d)
            if d < H - 1 or (y == 0 and sign < 0):
                send_row(s, y, sign * d, sign < 0)

    def row_y(s):
        row_here(s, 1, 0)
        send_row(s, 1, 0, True)
        send_row(s, 1, 0, False)

    def far_out(s):
        row_here(s, 0, H)
        send(row_block(s, NZ - 1, 0), row_block(s, NZ - 1, 0), r_row.at[s, NZ - 1, 1], to_yh, s)

    def row_core(s, j):
        ref = rows.at[pl.ds(2 * j, 2), :, c, part(s)]
        send(ref, ref, r_core.at[s, j], to_core, s, 4)

    def core_here(s, j):
        arrive(rows.at[pl.ds(2 * j, 2), :, oc, part(s)], r_core.at[s, j])

    def col_block(s, y, at):
        return cols.at[y, at, part(s)]

    def col_pair(s, at):
        return cols.at[:, at, part(s)]

    def col_y(s):
        arrive(col_block(s, 1 - yl, x), r_col.at[s, 0])
        send(col_pair(s, x), col_pair(s, x), r_col.at[s, 1], to_xp, s, 2)
        send(col_pair(s, x), col_pair(s, x), r_col.at[s, 2], to_xm, s, 2)

    def col_x(s):
        arrive(col_pair(s, xp), r_col.at[s, 2])
        send(col_block(s, yl, xp), col_block(s, yl, xp), r_col.at[s, 3], to_xm, s)
        arrive(col_pair(s, xm), r_col.at[s, 1])
        send(col_block(s, 1 - yl, xm), col_block(s, 1 - yl, xm), r_col.at[s, 4], to_xp, s)

    def all_cols(s):
        arrive(col_block(s, yl, x2), r_col.at[s, 3])
        arrive(col_block(s, 1 - yl, x2), r_col.at[s, 4])

    def halves(s, a, b):
        return jnp.concatenate([a[:, s * B : (s + 1) * B], b[:, s * B : (s + 1) * B]], axis=1)

    def col_lines():
        lines = [line_of(cols[r // XN, r % XN, B : B + 16]) for r in range(2 * XN)]
        for s in range(NS):
            for j in range(CN // 128):
                LC[s, :, j * 128 : (j + 1) * 128] = halves(s, lines[2 * j], lines[2 * j + 1])

    def lift(p):
        lines = [line_of(rows[p + q, y, k, B : B + 16]) for q in range(2) for y in range(2) for k in range(2)]
        wide = jnp.concatenate(lines, axis=0).T
        for i in range(8):
            for s in range(NS):
                column = wide[s * B : (s + 1) * B, i : i + 1]
                LRB[s, p + i // 4, i % 4 * B : (i % 4 + 1) * B, :] = jnp.broadcast_to(column, (B, 128))

    def turn(s):
        own = cols[:, :, s * (B + 16) : s * (B + 16) + B, :].reshape(CN, D)
        colsC[s] = own
        colsT[s] = (own * 0.5).T
        CPT[s] = jnp.zeros_like(CPT[s])

    def unit(s, p):
        pair = pl.ds(p, 2)
        left = rows[pair, :, :, pl.ds(pl.multiple_of(s * (B + 16), 16), B), :].reshape(8 * B, D)
        lr = LRB[s, pair].reshape(8 * B, 128)
        t = dot(left, colsT[s], NN) + jnp.concatenate([lr] * (CN // 128), axis=1) + LC[s]
        n = cnt[pl.ds(pl.multiple_of((s * NZ + p) * 4 * B, 8 * B), 8 * B), :].astype(F32)
        m = jnp.maximum(n, 1.0)
        root = m * lax.rsqrt(m)
        there = (0.4 + root) * (t - jnp.log(root))
        g = jnp.where(n > 0, there, jnp.tanh(t) + 1.0).astype(BF16)
        RP[s, pair] = dot(g, colsC[s], NN).reshape(2, 2, 2, B, D)
        CS[s, pair] = RP[s, pair, :, oc].astype(BF16)
        CPT[s] += dot(left.T, g, NN)

    def sums_here(s, j):
        arrive(CR.at[s, pl.ds(2 * j, 2)], r_cr.at[s, j])

    def chip_sum(s, r):
        return RP[s, place(r), :, c] + CR[s, place(r)].astype(F32)

    def half_sum(s, r, y):
        return RP[s, place(r), y, c] + CR[s, place(r), y].astype(F32)

    halves_in_turn = (1 - yh, yh)

    def ring(s, d):
        if d > 0:
            sums_here(s, d - 1)
        lanes_of = ((RSp, RRp, r_rp, to_zp, 1), (RSm, RRm, r_rm, to_zm, -1))
        if d == H:
            v = chip_sum(s, H)
            for half, (RS, RR, rr, dev, _) in enumerate(lanes_of):
                RS[s, H - 1, half] = v[half].astype(BF16)
                send(RS.at[s, H - 1, half], RR.at[s, H - 1, half], rr.at[s, H - 1, 0], dev, 1, 1)
        elif d == H - 1:
            for half, (RS, RR, rr, dev, sign) in enumerate(lanes_of):
                v = chip_sum(s, sign * d)
                arrive(RR.at[s, d, half], rr.at[s, d, 0])
                RS[s, d - 1, half] = (v[half] + RR[s, d, half].astype(F32)).astype(BF16)
                RS[s, d - 1, 1 - half] = v[1 - half].astype(BF16)
                send(RS.at[s, d - 1], RR.at[s, d - 1], rr.at[s, d - 1, 0], dev, 1, 2)
        elif d > 0 and s == 0:
            for RS, RR, rr, dev, sign in lanes_of:
                v = chip_sum(s, sign * d)
                arrive(RR.at[s, d], rr.at[s, d, 0])
                RS[s, d - 1] = (v + RR[s, d].astype(F32)).astype(BF16)
                send(RS.at[s, d - 1], RR.at[s, d - 1], rr.at[s, d - 1, 0], dev, 1, 2)
        elif d > 0:
            for k, y in enumerate(halves_in_turn):
                for RS, RR, rr, dev, sign in lanes_of:
                    if d < H - 2:
                        arrive(RR.at[s, d, y], rr.at[s, d, k])
                    elif k == 0:
                        arrive(RR.at[s, d], rr.at[s, d, 0])
                    RS[s, d - 1, y] = (half_sum(s, sign * d, y) + RR[s, d, y].astype(F32)).astype(BF16)
                    send(RS.at[s, d - 1, y], RR.at[s, d - 1, y], rr.at[s, d - 1, k], dev, 1, 1)
        else:
            for k, y in enumerate(halves_in_turn):
                for _, RR, rr, _, _ in lanes_of:
                    if s == 1:
                        arrive(RR.at[s, 0, y], rr.at[s, 0, k])
                    elif k == 0:
                        arrive(RR.at[s, 0], rr.at[s, 0, 0])
                v = half_sum(s, 0, y) + RRp[s, 0, y].astype(F32) + RRm[s, 0, y].astype(F32)
                if k == 0:
                    YS[s] = v.astype(BF16)
                    send(YS.at[s], YR.at[s], r_y.at[s], to_yh, 1, 1)
                else:
                    VR[s] = v

    def out_copy(k, s):
        src, dst = ((gr, nr), (gc, nc))[k]
        return pltpu.make_async_copy(src.at[s], dst.at[s], s_out.at[k, s])

    def rows_out(s):
        arrive(YR.at[s], r_y.at[s])
        gr[s] = 0.5 * (VR[s] + YR[s].astype(F32))
        out_copy(0, s).start()

    def col_far(s):
        CP[s] = CPT[s].T.reshape(2 * XN, B, D)
        Q1s[s, 0] = CP[s, yl * XN + x2].astype(BF16)
        send(Q1s.at[s, 0], Q1r.at[s, 0], r_q.at[s, 0], to_xp, 1, 1)
        Q1s[s, 1] = CP[s, (1 - yl) * XN + x2].astype(BF16)
        send(Q1s.at[s, 1], Q1r.at[s, 1], r_q.at[s, 1], to_xm, 1, 1)

    def col_near(s):
        arrive(Q1r.at[s, 0], r_q.at[s, 0])
        Q2s[s, 0, 0] = (CP[s, yl * XN + xp] + Q1r[s, 0].astype(F32)).astype(BF16)
        Q2s[s, 0, 1] = CP[s, (1 - yl) * XN + xp].astype(BF16)
        send(Q2s.at[s, 0], Q2r.at[s, 0], r_q.at[s, 2], to_xp, 1, 2)
        arrive(Q1r.at[s, 1], r_q.at[s, 1])
        Q2s[s, 1, 0] = CP[s, yl * XN + xm].astype(BF16)
        Q2s[s, 1, 1] = (CP[s, (1 - yl) * XN + xm] + Q1r[s, 1].astype(F32)).astype(BF16)
        send(Q2s.at[s, 1], Q2r.at[s, 1], r_q.at[s, 3], to_xm, 1, 2)

    def col_own(s):
        arrive(Q2r.at[s, 0], r_q.at[s, 2])
        arrive(Q2r.at[s, 1], r_q.at[s, 3])
        Q3s[s] = (CP[s, r_oth] + Q2r[s, 0, 1].astype(F32) + Q2r[s, 1, 1].astype(F32)).astype(BF16)
        send(Q3s.at[s], Q3r.at[s], r_q.at[s, 4], to_yl, 1, 1)
        VC[s] = CP[s, r_own] + Q2r[s, 0, 0].astype(F32) + Q2r[s, 1, 0].astype(F32)

    def cols_out(s):
        arrive(Q3r.at[s], r_q.at[s, 4])
        gc[s] = 0.5 * (VC[s] + Q3r[s].astype(F32))
        out_copy(1, s).start()

    for s in range(NS):
        send(col_block(s, yl, x), col_block(s, yl, x), r_col.at[s, 0], to_yl, s)
        send(row_block(s, 0, 0), row_block(s, 0, 0), r_row.at[s, 0, 1], to_yh, s)
        send_row(s, 0, 0, True)
        send_row(s, 0, 0, False)
    col_y(0)
    row_step(0, 0, 1)
    row_y(0)
    row_step(1, 0, 1)
    col_y(1)
    counts_out(3, 6)
    row_step(0, 0, 2)
    col_x(0)
    row_y(1)
    row_step(1, 0, 2)
    row_step(0, 1, 1)
    row_core(0, 0)
    col_x(1)
    counts_out(6, 9)
    row_step(0, 0, 3)
    row_step(1, 1, 1)
    row_core(1, 0)
    row_step(1, 0, 3)
    all_cols(0)
    col_lines()
    turn(0)
    counts_out(9, 12)
    row_step(0, 1, 2)
    row_core(0, 1)

    def before(i):
        if i == 0:
            core_here(0, 0)
            lift(0)
        if i == 1:
            counts_out(12, 16)
            far_out(0)
            row_step(1, 1, 2)
            row_core(1, 1)
            row_step(0, 1, 3)
            row_core(0, 2)
            far_out(1)
            core_here(0, 1)
            lift(2)
        if i == 2:
            row_here(0, 1, H)
            row_core(0, 3)
            row_step(1, 1, 3)
            row_core(1, 2)
            core_here(0, 2)
            lift(4)
        if i == 3:
            row_here(1, 1, H)
            row_core(1, 3)
            core_here(0, 3)
            lift(6)
        if i == 4:
            all_cols(1)
            turn(1)
            core_here(1, 3)
        if i == 5:
            ring(0, H)
            core_here(1, 2)
        if i == 6:
            ring(1, H)
            col_far(0)
            ring(0, 3)
            core_here(1, 1)
        if i == 7:
            ring(1, 3)
            col_near(0)
            ring(0, 2)
            core_here(1, 0)

    def step(i, carry):
        for k in range(2 * H):
            pl.when(i == k)(functools.partial(before, k))
        s, j = turn_of(i)
        p = 2 * j
        count_copy(2 * i).wait()
        count_copy(2 * i + 1).wait()
        unit(s, p)
        part = pl.ds(p, 2)
        send(CS.at[s, part], CR.at[s, part], r_cr.at[s, j], to_core, 1, 4 * 2 * H)
        return carry

    lax.fori_loop(0, 2 * H, step, 0)
    col_far(1)
    ring(1, 2)
    col_own(0)
    ring(0, 1)
    ring(1, 1)
    col_near(1)
    cols_out(0)
    ring(0, 0)
    ring(1, 0)
    col_own(1)
    rows_out(0)
    cols_out(1)
    rows_out(1)
    for k in range(2):
        for s in range(NS):
            out_copy(k, s).wait()
    arrive(cnt.at[pl.ds(0, total[0] * D * 2 // (CN * 4))], s_all)


def local(counts, re, ce, rm, cm, ra, ca, *, NZ, XN):
    S, B, D = re.shape
    CB = counts.shape[2]
    H = NZ // 2
    R = 2 * XN
    counts = counts.reshape(S, NZ, 4 * B, CB)
    sem = pltpu.SemaphoreType.DMA
    v = pltpu.VMEM
    scratch = [
        v((S, B, D), F32),
        v((S, B, D), F32),
        v((S, B), jnp.int32),
        v((S, B), jnp.int32),
        v((S * NZ * 4 * B, CB), jnp.int32),
        v((NZ, 2, 2, 2 * B + 16, D), BF16),
        v((2, XN, 2 * B + 16, D), BF16),
        v((S, D, CB), BF16),
        v((S, CB, D), BF16),
        v((S, NZ, 4 * B, 128), F32),
        v((S, 1, CB), F32),
        v((S, NZ, 2, 2, B, D), F32),
        v((S, D, CB), F32),
        v((S, R, B, D), F32),
        v((S, NZ, 2, B, D), BF16),
        v((S, NZ, 2, B, D), BF16),
        v((S, H, 2, B, D), BF16),
        v((S, H, 2, B, D), BF16),
        v((S, H, 2, B, D), BF16),
        v((S, H, 2, B, D), BF16),
        v((S, B, D), BF16),
        v((S, B, D), BF16),
        v((S, B, D), F32),
        v((S, 2, B, D), BF16),
        v((S, 2, B, D), BF16),
        v((S, 2, 2, B, D), BF16),
        v((S, 2, 2, B, D), BF16),
        v((S, B, D), BF16),
        v((S, B, D), BF16),
        v((S, B, D), F32),
        v((S, B, D), F32),
        v((S, B, D), F32),
        sem((4,)),
        sem((S * NZ,)),
        sem(()),
        sem((2, S)),
        sem((S, NZ, 2)),
        sem((S, H)),
        sem((S, 5)),
        sem((S, H)),
        sem((S, H, 2)),
        sem((S, H, 2)),
        sem((S,)),
        sem((S, 5)),
    ]
    gr, gc = pl.pallas_call(
        functools.partial(kernel, NZ, XN, B, D, CB),
        out_shape=(jax.ShapeDtypeStruct((S, B, D), F32), jax.ShapeDtypeStruct((S, B, D), F32)),
        in_specs=[pl.BlockSpec(memory_space=pltpu.HBM)] * 5,
        out_specs=(pl.BlockSpec(memory_space=pltpu.HBM),) * 2,
        scratch_shapes=scratch,
        compiler_params=pltpu.CompilerParams(
            collective_id=0, has_side_effects=True, vmem_limit_bytes=60 * 1024 * 1024
        ),
    )(counts, re, ce, rm, cm)
    return adagrad(re, ra, gr), adagrad(ce, ca, gc)


def solution(mesh):
    return jax.shard_map(
        functools.partial(local, NZ=mesh.shape["col"] // 4, XN=mesh.shape["row"] // 2),
        mesh=mesh,
        in_specs=(
            P(None, "row", "col"),
            P(None, ("row", "col"), None),
            P(None, ("col", "row"), None),
            P(None, ("row", "col")),
            P(None, ("col", "row")),
            P(None, ("row", "col"), None),
            P(None, ("col", "row"), None),
        ),
        out_specs=(P(None, ("row", "col"), None), P(None, ("col", "row"), None)),
        check_vma=False,
    )
```

```python
import functools

import jax
import jax.numpy as jnp
from jax import lax
from jax.experimental import pallas as pl
from jax.experimental.pallas import tpu as pltpu
from jax.sharding import PartitionSpec as P

MESH = pl.DeviceIdType.MESH
F32 = jnp.float32
BF16 = jnp.bfloat16
NT = (((1,), (1,)), ((), ()))
NN = (((1,), (0,)), ((), ()))
TN = (((0,), (0,)), ((), ()))


def dot(a, b, dims):
    return lax.dot_general(a, b, dims, preferred_element_type=F32)


def adagrad(w, a, g):
    return w - g / jnp.sqrt(a + g * g)


def kernel(
    NZ, XN, B, D, CN,
    counts, re_h, ce_h, rm_h, cm_h, nr, nc,
    re, ce, rm, cm,
    cnt, rows, cols, colsT, colsC, LRB, LC, RP, CPT, CP,
    CS, CR, RSp, RSm, RRp, RRm, YS, YR, VR, Q1s, Q1r, Q2s, Q2r, Q3s, Q3r, VC, gr, gc,
    s_in, s_cnt, s_all, s_out, r_row, r_core, r_col, r_cr, r_rp, r_rm, r_y, r_q,
):
    H = NZ // 2
    NS = 2
    row = lax.axis_index("row")
    col = lax.axis_index("col")
    x = lax.rem(row, XN)
    yl = row // XN
    z = col // 4
    yh = lax.rem(col // 2, 2)
    c = lax.rem(col, 2)
    oc = 1 - c
    xp = lax.rem(x + 1, XN)
    xm = lax.rem(x + XN - 1, XN)
    x2 = lax.rem(x + 2, XN)
    zp = lax.rem(z + 1, NZ)
    zm = lax.rem(z + NZ - 1, NZ)
    to_core = (row, col + 1 - 2 * c)
    to_yh = (row, col + 2 - 4 * yh)
    to_zp = (row, zp * 4 + yh * 2 + c)
    to_zm = (row, zm * 4 + yh * 2 + c)
    to_yl = ((1 - yl) * XN + x, col)
    to_xp = (yl * XN + xp, col)
    to_xm = (yl * XN + xm, col)
    r_own = yl * XN + x
    r_oth = (1 - yl) * XN + x

    def place(r):
        return 0 if r == 0 else 2 * r - 1 if r > 0 or r == -H else -2 * r

    def place_of(r):
        return place(H) if r == -H else place(r)

    def span(d):
        return (2 * d - 1, 2) if 0 < d < H else (place_of(d), 1)

    rel = [0]
    for d in range(1, H):
        rel += [d, -d]
    rel += [H]

    total = [0]

    def send(src, dst, rsem, dev, kind, count=1):
        pltpu.make_async_remote_copy(
            src_ref=src, dst_ref=dst, send_sem=s_all, recv_sem=rsem, device_id=dev, device_id_type=MESH
        ).start()
        total[0] += count * (B + 16 if kind == 0 else B)

    def arrive(dst, rsem):
        pltpu.make_async_copy(dst, dst, rsem).wait()

    own_in = [
        pltpu.make_async_copy(src, dst, s_in.at[i])
        for i, (src, dst) in enumerate(((rm_h, rm), (cm_h, cm), (re_h, re), (ce_h, ce)))
    ]
    for copy in own_in:
        copy.start()

    barrier = pltpu.get_barrier_semaphore()
    partners = [to_core, to_yh, to_zp, to_zm, to_yl, to_xp, to_xm]
    for dev in partners:
        pl.semaphore_signal(barrier, inc=1, device_id=dev, device_id_type=MESH)

    def turn_of(i):
        first, second, late = (i + 7) // 8, (i + 6) // 8, (i + 3) // 8
        return late + first - second, (1 - late) * (i - first) + late * (8 - i)

    def in_turn(u):
        s, j = turn_of(u // 2)
        return s * NZ + 2 * j + lax.rem(u, 2)

    def count_copy(u):
        q = in_turn(u)
        p = lax.rem(q, NZ)
        d = (p + 1) // 2
        zc = lax.rem(z + NZ + d * (2 * lax.rem(p, 2) - 1), NZ)
        at = pl.ds(pl.multiple_of(q * 4 * B, 4 * B), 4 * B)
        return pltpu.make_async_copy(counts.at[q // NZ, zc], cnt.at[at], s_cnt.at[q])

    def counts_out(lo, hi):
        for u in range(lo, hi):
            count_copy(u).start()

    counts_out(0, 3)

    for copy in own_in:
        copy.wait()

    def own_block(embed, margs, shift):
        line = jnp.concatenate([margs[0:1, :], margs[1:2, :]], axis=1).astype(F32)
        line = 0.5 * (jnp.log(line) - shift)
        hi = line.astype(BF16).astype(F32)
        mid = (line - hi).astype(BF16).astype(F32)
        upper = jnp.concatenate([hi, mid], axis=1)
        lower = jnp.concatenate([line - hi - mid, jnp.zeros_like(line)], axis=1)
        which = lax.broadcasted_iota(jnp.int32, (16, 4 * B), 0)
        tail = jnp.where(which == 0, upper, jnp.where(which == 1, lower, 0.0)).astype(BF16)
        return embed[0].astype(BF16), embed[1].astype(BF16), tail

    for ref, parts in ((rows.at[0, yh, c], own_block(re, rm, 20.0)), (cols.at[yl, x], own_block(ce, cm, 0.0))):
        ref[0:B] = parts[0]
        ref[B : B + 16] = parts[2]
        ref[B + 16 :] = parts[1]

    def line_of(tail):
        tail = tail.astype(F32)
        return tail[0:1, : 2 * B] + tail[0:1, 2 * B :] + tail[1:2, : 2 * B]

    pl.semaphore_wait(barrier, len(partners))

    def part(s):
        return pl.ds(0, B + 16) if s == 0 else pl.ds(B + 16, B)

    def row_block(s, p, y):
        return rows.at[p, 1 - yh if y else yh, c, part(s)]

    def send_row(s, y, r, up):
        to = place_of(r - 1 if up else r + 1)
        send(row_block(s, place(r), y), row_block(s, to, y), r_row.at[s, to, y], to_zp if up else to_zm, s)

    def row_here(s, y, r):
        arrive(row_block(s, place_of(r), y), r_row.at[s, place_of(r), y])

    def row_step(s, y, d):
        for sign in (-1, 1):
            row_here(s, y, sign * d)
            if d < H - 1 or (y == 0 and sign < 0):
                send_row(s, y, sign * d, sign < 0)

    def row_y(s):
        row_here(s, 1, 0)
        send_row(s, 1, 0, True)
        send_row(s, 1, 0, False)

    def far_out(s):
        row_here(s, 0, H)
        send(row_block(s, NZ - 1, 0), row_block(s, NZ - 1, 0), r_row.at[s, NZ - 1, 1], to_yh, s)

    def row_core(s, j):
        ref = rows.at[pl.ds(2 * j, 2), :, c, part(s)]
        send(ref, ref, r_core.at[s, j], to_core, s, 4)

    def core_here(s, j):
        arrive(rows.at[pl.ds(2 * j, 2), :, oc, part(s)], r_core.at[s, j])

    def col_block(s, y, at):
        return cols.at[y, at, part(s)]

    def col_pair(s, at):
        return cols.at[:, at, part(s)]

    def col_y(s):
        arrive(col_block(s, 1 - yl, x), r_col.at[s, 0])
        send(col_pair(s, x), col_pair(s, x), r_col.at[s, 1], to_xp, s, 2)
        send(col_pair(s, x), col_pair(s, x), r_col.at[s, 2], to_xm, s, 2)

    def col_x(s):
        arrive(col_pair(s, xp), r_col.at[s, 2])
        send(col_block(s, yl, xp), col_block(s, yl, xp), r_col.at[s, 3], to_xm, s)
        arrive(col_pair(s, xm), r_col.at[s, 1])
        send(col_block(s, 1 - yl, xm), col_block(s, 1 - yl, xm), r_col.at[s, 4], to_xp, s)

    def all_cols(s):
        arrive(col_block(s, yl, x2), r_col.at[s, 3])
        arrive(col_block(s, 1 - yl, x2), r_col.at[s, 4])

    def halves(s, a, b):
        return jnp.concatenate([a[:, s * B : (s + 1) * B], b[:, s * B : (s + 1) * B]], axis=1)

    def col_lines():
        lines = [line_of(cols[r // XN, r % XN, B : B + 16]) for r in range(2 * XN)]
        for s in range(NS):
            for j in range(CN // 128):
                LC[s, :, j * 128 : (j + 1) * 128] = halves(s, lines[2 * j], lines[2 * j + 1])

    def lift(p):
        lines = [line_of(rows[p + q, y, k, B : B + 16]) for q in range(2) for y in range(2) for k in range(2)]
        wide = jnp.concatenate(lines, axis=0).T
        for i in range(8):
            for s in range(NS):
                column = wide[s * B : (s + 1) * B, i : i + 1]
                LRB[s, p + i // 4, i % 4 * B : (i % 4 + 1) * B, :] = jnp.broadcast_to(column, (B, 128))

    def turn(s):
        own = cols[:, :, s * (B + 16) : s * (B + 16) + B, :].reshape(CN, D)
        colsC[s] = own
        colsT[s] = (own * 0.5).T
        CPT[s] = jnp.zeros_like(CPT[s])

    def unit(s, p):
        lefts, grads = [], []
        for q in range(2):
            left = rows[p + q, :, :, pl.ds(pl.multiple_of(s * (B + 16), 16), B), :].reshape(4 * B, D)
            t = dot(left, colsT[s], NN) + jnp.concatenate([LRB[s, p + q]] * (CN // 128), axis=1) + LC[s]
            n = cnt[pl.ds(pl.multiple_of((s * NZ + p + q) * 4 * B, 4 * B), 4 * B), :].astype(F32)
            m = jnp.maximum(n, 1.0)
            root = m * lax.rsqrt(m)
            there = (0.4 + root) * (t - jnp.log(root))
            g = jnp.where(n > 0, there, jnp.tanh(t) + 1.0).astype(BF16)
            RP[s, p + q] = dot(g, colsC[s], NN).reshape(2, 2, B, D)
            CS[s, p + q] = RP[s, p + q, :, oc].astype(BF16)
            lefts.append(left)
            grads.append(g)
        CPT[s] += dot(jnp.concatenate(lefts, axis=0).T, jnp.concatenate(grads, axis=0), NN)

    def sums_here(s, j):
        arrive(CR.at[s, pl.ds(2 * j, 2)], r_cr.at[s, j])

    def chip_sum(s, r):
        return RP[s, place(r), :, c] + CR[s, place(r)].astype(F32)

    def half_sum(s, r, y):
        return RP[s, place(r), y, c] + CR[s, place(r), y].astype(F32)

    halves_in_turn = (1 - yh, yh)

    def ring(s, d):
        if d > 0:
            sums_here(s, d - 1)
        lanes_of = ((RSp, RRp, r_rp, to_zp, 1), (RSm, RRm, r_rm, to_zm, -1))
        if d == H:
            v = chip_sum(s, H)
            for half, (RS, RR, rr, dev, _) in enumerate(lanes_of):
                RS[s, H - 1, half] = v[half].astype(BF16)
                send(RS.at[s, H - 1, half], RR.at[s, H - 1, half], rr.at[s, H - 1, 0], dev, 1, 1)
        elif d == H - 1:
            for half, (RS, RR, rr, dev, sign) in enumerate(lanes_of):
                v = chip_sum(s, sign * d)
                arrive(RR.at[s, d, half], rr.at[s, d, 0])
                RS[s, d - 1, half] = (v[half] + RR[s, d, half].astype(F32)).astype(BF16)
                RS[s, d - 1, 1 - half] = v[1 - half].astype(BF16)
                send(RS.at[s, d - 1], RR.at[s, d - 1], rr.at[s, d - 1, 0], dev, 1, 2)
        elif d > 0 and s == 0:
            for RS, RR, rr, dev, sign in lanes_of:
                v = chip_sum(s, sign * d)
                arrive(RR.at[s, d], rr.at[s, d, 0])
                RS[s, d - 1] = (v + RR[s, d].astype(F32)).astype(BF16)
                send(RS.at[s, d - 1], RR.at[s, d - 1], rr.at[s, d - 1, 0], dev, 1, 2)
        elif d > 0:
            for k, y in enumerate(halves_in_turn):
                for RS, RR, rr, dev, sign in lanes_of:
                    if d < H - 2:
                        arrive(RR.at[s, d, y], rr.at[s, d, k])
                    elif k == 0:
                        arrive(RR.at[s, d], rr.at[s, d, 0])
                    RS[s, d - 1, y] = (half_sum(s, sign * d, y) + RR[s, d, y].astype(F32)).astype(BF16)
                    send(RS.at[s, d - 1, y], RR.at[s, d - 1, y], rr.at[s, d - 1, k], dev, 1, 1)
        else:
            for k, y in enumerate(halves_in_turn):
                for _, RR, rr, _, _ in lanes_of:
                    if s == 1:
                        arrive(RR.at[s, 0, y], rr.at[s, 0, k])
                    elif k == 0:
                        arrive(RR.at[s, 0], rr.at[s, 0, 0])
                v = half_sum(s, 0, y) + RRp[s, 0, y].astype(F32) + RRm[s, 0, y].astype(F32)
                if k == 0:
                    YS[s] = v.astype(BF16)
                    send(YS.at[s], YR.at[s], r_y.at[s], to_yh, 1, 1)
                else:
                    VR[s] = v

    def out_copy(k, s):
        src, dst = ((gr, nr), (gc, nc))[k]
        return pltpu.make_async_copy(src.at[s], dst.at[s], s_out.at[k, s])

    def rows_out(s):
        arrive(YR.at[s], r_y.at[s])
        gr[s] = 0.5 * (VR[s] + YR[s].astype(F32))
        out_copy(0, s).start()

    def col_far(s):
        CP[s] = CPT[s].T.reshape(2 * XN, B, D)
        Q1s[s, 0] = CP[s, yl * XN + x2].astype(BF16)
        send(Q1s.at[s, 0], Q1r.at[s, 0], r_q.at[s, 0], to_xp, 1, 1)
        Q1s[s, 1] = CP[s, (1 - yl) * XN + x2].astype(BF16)
        send(Q1s.at[s, 1], Q1r.at[s, 1], r_q.at[s, 1], to_xm, 1, 1)

    def col_near(s):
        arrive(Q1r.at[s, 0], r_q.at[s, 0])
        Q2s[s, 0, 0] = (CP[s, yl * XN + xp] + Q1r[s, 0].astype(F32)).astype(BF16)
        Q2s[s, 0, 1] = CP[s, (1 - yl) * XN + xp].astype(BF16)
        send(Q2s.at[s, 0], Q2r.at[s, 0], r_q.at[s, 2], to_xp, 1, 2)
        arrive(Q1r.at[s, 1], r_q.at[s, 1])
        Q2s[s, 1, 0] = CP[s, yl * XN + xm].astype(BF16)
        Q2s[s, 1, 1] = (CP[s, (1 - yl) * XN + xm] + Q1r[s, 1].astype(F32)).astype(BF16)
        send(Q2s.at[s, 1], Q2r.at[s, 1], r_q.at[s, 3], to_xm, 1, 2)

    def col_own(s):
        arrive(Q2r.at[s, 0], r_q.at[s, 2])
        arrive(Q2r.at[s, 1], r_q.at[s, 3])
        Q3s[s] = (CP[s, r_oth] + Q2r[s, 0, 1].astype(F32) + Q2r[s, 1, 1].astype(F32)).astype(BF16)
        send(Q3s.at[s], Q3r.at[s], r_q.at[s, 4], to_yl, 1, 1)
        VC[s] = CP[s, r_own] + Q2r[s, 0, 0].astype(F32) + Q2r[s, 1, 0].astype(F32)

    def cols_out(s):
        arrive(Q3r.at[s], r_q.at[s, 4])
        gc[s] = 0.5 * (VC[s] + Q3r[s].astype(F32))
        out_copy(1, s).start()

    for s in range(NS):
        send(col_block(s, yl, x), col_block(s, yl, x), r_col.at[s, 0], to_yl, s)
        send(row_block(s, 0, 0), row_block(s, 0, 0), r_row.at[s, 0, 1], to_yh, s)
        send_row(s, 0, 0, True)
        send_row(s, 0, 0, False)
    col_y(0)
    row_step(0, 0, 1)
    row_y(0)
    row_step(1, 0, 1)
    col_y(1)
    counts_out(3, 6)
    row_step(0, 0, 2)
    col_x(0)
    row_y(1)
    row_step(1, 0, 2)
    row_step(0, 1, 1)
    row_core(0, 0)
    col_x(1)
    counts_out(6, 9)
    row_step(0, 0, 3)
    row_step(1, 1, 1)
    row_core(1, 0)
    row_step(1, 0, 3)
    all_cols(0)
    col_lines()
    turn(0)
    counts_out(9, 12)
    row_step(0, 1, 2)
    row_core(0, 1)

    def before(i):
        if i == 0:
            core_here(0, 0)
            lift(0)
        if i == 1:
            counts_out(12, 16)
            far_out(0)
            row_step(1, 1, 2)
            row_core(1, 1)
            all_cols(1)
            turn(1)
            core_here(1, 0)
        if i == 2:
            row_step(0, 1, 3)
            row_core(0, 2)
            far_out(1)
            core_here(0, 1)
            lift(2)
        if i == 3:
            row_step(1, 1, 3)
            row_core(1, 2)
            row_here(0, 1, H)
            row_core(0, 3)
            core_here(0, 2)
            lift(4)
        if i == 4:
            row_here(1, 1, H)
            row_core(1, 3)
            core_here(0, 3)
            lift(6)
        if i == 5:
            core_here(1, 3)
        if i == 6:
            ring(0, H)
            core_here(1, 2)
        if i == 7:
            ring(1, H)
            col_far(0)
            ring(0, 3)
            core_here(1, 1)

    def step(i, carry):
        for k in range(2 * H):
            pl.when(i == k)(functools.partial(before, k))
        s, j = turn_of(i)
        p = 2 * j
        count_copy(2 * i).wait()
        count_copy(2 * i + 1).wait()
        unit(s, p)
        part = pl.ds(p, 2)
        send(CS.at[s, part], CR.at[s, part], r_cr.at[s, j], to_core, 1, 4 * 2 * H)
        return carry

    lax.fori_loop(0, 2 * H, step, 0)
    ring(1, 3)
    col_near(0)
    ring(0, 2)
    col_far(1)
    ring(1, 2)
    col_own(0)
    ring(0, 1)
    col_near(1)
    ring(1, 1)
    cols_out(0)
    ring(0, 0)
    col_own(1)
    ring(1, 0)
    rows_out(0)
    cols_out(1)
    rows_out(1)
    for k in range(2):
        for s in range(NS):
            out_copy(k, s).wait()
    arrive(cnt.at[pl.ds(0, total[0] * D * 2 // (CN * 4))], s_all)


def local(counts, re, ce, rm, cm, ra, ca, *, NZ, XN):
    S, B, D = re.shape
    CB = counts.shape[2]
    H = NZ // 2
    R = 2 * XN
    counts = counts.reshape(S, NZ, 4 * B, CB)
    sem = pltpu.SemaphoreType.DMA
    v = pltpu.VMEM
    scratch = [
        v((S, B, D), F32),
        v((S, B, D), F32),
        v((S, B), jnp.int32),
        v((S, B), jnp.int32),
        v((S * NZ * 4 * B, CB), jnp.int32),
        v((NZ, 2, 2, 2 * B + 16, D), BF16),
        v((2, XN, 2 * B + 16, D), BF16),
        v((S, D, CB), BF16),
        v((S, CB, D), BF16),
        v((S, NZ, 4 * B, 128), F32),
        v((S, 1, CB), F32),
        v((S, NZ, 2, 2, B, D), F32),
        v((S, D, CB), F32),
        v((S, R, B, D), F32),
        v((S, NZ, 2, B, D), BF16),
        v((S, NZ, 2, B, D), BF16),
        v((S, H, 2, B, D), BF16),
        v((S, H, 2, B, D), BF16),
        v((S, H, 2, B, D), BF16),
        v((S, H, 2, B, D), BF16),
        v((S, B, D), BF16),
        v((S, B, D), BF16),
        v((S, B, D), F32),
        v((S, 2, B, D), BF16),
        v((S, 2, B, D), BF16),
        v((S, 2, 2, B, D), BF16),
        v((S, 2, 2, B, D), BF16),
        v((S, B, D), BF16),
        v((S, B, D), BF16),
        v((S, B, D), F32),
        v((S, B, D), F32),
        v((S, B, D), F32),
        sem((4,)),
        sem((S * NZ,)),
        sem(()),
        sem((2, S)),
        sem((S, NZ, 2)),
        sem((S, H)),
        sem((S, 5)),
        sem((S, H)),
        sem((S, H, 2)),
        sem((S, H, 2)),
        sem((S,)),
        sem((S, 5)),
    ]
    gr, gc = pl.pallas_call(
        functools.partial(kernel, NZ, XN, B, D, CB),
        out_shape=(jax.ShapeDtypeStruct((S, B, D), F32), jax.ShapeDtypeStruct((S, B, D), F32)),
        in_specs=[pl.BlockSpec(memory_space=pltpu.HBM)] * 5,
        out_specs=(pl.BlockSpec(memory_space=pltpu.HBM),) * 2,
        scratch_shapes=scratch,
        compiler_params=pltpu.CompilerParams(
            collective_id=0, has_side_effects=True, vmem_limit_bytes=60 * 1024 * 1024
        ),
    )(counts, re, ce, rm, cm)
    return adagrad(re, ra, gr), adagrad(ce, ca, gc)


def solution(mesh):
    return jax.shard_map(
        functools.partial(local, NZ=mesh.shape["col"] // 4, XN=mesh.shape["row"] // 2),
        mesh=mesh,
        in_specs=(
            P(None, "row", "col"),
            P(None, ("row", "col"), None),
            P(None, ("col", "row"), None),
            P(None, ("row", "col")),
            P(None, ("col", "row")),
            P(None, ("row", "col"), None),
            P(None, ("col", "row"), None),
        ),
        out_specs=(P(None, ("row", "col"), None), P(None, ("col", "row"), None)),
        check_vma=False,
    )
```

```python
import functools

import jax
import jax.numpy as jnp
from jax import lax
from jax.experimental import pallas as pl
from jax.experimental.pallas import tpu as pltpu
from jax.sharding import PartitionSpec as P

MESH = pl.DeviceIdType.MESH
F32 = jnp.float32
BF16 = jnp.bfloat16
NT = (((1,), (1,)), ((), ()))
NN = (((1,), (0,)), ((), ()))
TN = (((0,), (0,)), ((), ()))


def dot(a, b, dims):
    return lax.dot_general(a, b, dims, preferred_element_type=F32)


def adagrad(w, a, g):
    return w - g / jnp.sqrt(a + g * g)


def kernel(
    NZ, XN, B, D, CN,
    counts, re_h, ce_h, rm_h, cm_h, nr, nc,
    re, ce, rm, cm,
    cnt, rows, cols, colsT, colsC, LRB, LC, RP, CPT, CP,
    CS, CR, RSp, RSm, RRp, RRm, YS, YR, VR, Q1s, Q1r, Q2s, Q2r, Q3s, Q3r, VC, gr, gc,
    s_in, s_cnt, s_all, s_out, r_row, r_core, r_col, r_cr, r_rp, r_rm, r_y, r_q,
):
    H = NZ // 2
    NS = 2
    row = lax.axis_index("row")
    col = lax.axis_index("col")
    x = lax.rem(row, XN)
    yl = row // XN
    z = col // 4
    yh = lax.rem(col // 2, 2)
    c = lax.rem(col, 2)
    oc = 1 - c
    xp = lax.rem(x + 1, XN)
    xm = lax.rem(x + XN - 1, XN)
    x2 = lax.rem(x + 2, XN)
    zp = lax.rem(z + 1, NZ)
    zm = lax.rem(z + NZ - 1, NZ)
    to_core = (row, col + 1 - 2 * c)
    to_yh = (row, col + 2 - 4 * yh)
    to_zp = (row, zp * 4 + yh * 2 + c)
    to_zm = (row, zm * 4 + yh * 2 + c)
    to_yl = ((1 - yl) * XN + x, col)
    to_xp = (yl * XN + xp, col)
    to_xm = (yl * XN + xm, col)
    r_own = yl * XN + x
    r_oth = (1 - yl) * XN + x

    def place(r):
        return 0 if r == 0 else 2 * r - 1 if r > 0 or r == -H else -2 * r

    def place_of(r):
        return place(H) if r == -H else place(r)

    def span(d):
        return (2 * d - 1, 2) if 0 < d < H else (place_of(d), 1)

    rel = [0]
    for d in range(1, H):
        rel += [d, -d]
    rel += [H]

    total = [0]

    def send(src, dst, rsem, dev, kind, count=1):
        pltpu.make_async_remote_copy(
            src_ref=src, dst_ref=dst, send_sem=s_all, recv_sem=rsem, device_id=dev, device_id_type=MESH
        ).start()
        total[0] += count * (B + 16 if kind == 0 else B)

    def arrive(dst, rsem):
        pltpu.make_async_copy(dst, dst, rsem).wait()

    own_in = [
        pltpu.make_async_copy(src, dst, s_in.at[i])
        for i, (src, dst) in enumerate(((rm_h, rm), (cm_h, cm), (re_h, re), (ce_h, ce)))
    ]
    for copy in own_in:
        copy.start()

    barrier = pltpu.get_barrier_semaphore()
    partners = [to_core, to_yh, to_zp, to_zm, to_yl, to_xp, to_xm]
    for dev in partners:
        pl.semaphore_signal(barrier, inc=1, device_id=dev, device_id_type=MESH)

    def turn_of(i):
        s = i // H
        return s, i * (1 - s) + (2 * H - 1 - i) * s

    def in_turn(u):
        s, j = turn_of(u // 2)
        return s * NZ + 2 * j + lax.rem(u, 2)

    def count_copy(u):
        q = in_turn(u)
        p = lax.rem(q, NZ)
        d = (p + 1) // 2
        zc = lax.rem(z + NZ + d * (2 * lax.rem(p, 2) - 1), NZ)
        at = pl.ds(pl.multiple_of(q * 4 * B, 4 * B), 4 * B)
        return pltpu.make_async_copy(counts.at[q // NZ, zc], cnt.at[at], s_cnt.at[q])

    def counts_out(lo, hi):
        for u in range(lo, hi):
            count_copy(u).start()

    counts_out(0, 4)

    for copy in own_in:
        copy.wait()

    def own_block(embed, margs, shift):
        line = jnp.concatenate([margs[0:1, :], margs[1:2, :]], axis=1).astype(F32)
        line = 0.5 * (jnp.log(line) - shift)
        hi = line.astype(BF16).astype(F32)
        mid = (line - hi).astype(BF16).astype(F32)
        upper = jnp.concatenate([hi, mid], axis=1)
        lower = jnp.concatenate([line - hi - mid, jnp.zeros_like(line)], axis=1)
        which = lax.broadcasted_iota(jnp.int32, (16, 4 * B), 0)
        tail = jnp.where(which == 0, upper, jnp.where(which == 1, lower, 0.0)).astype(BF16)
        return embed[0].astype(BF16), embed[1].astype(BF16), tail

    for ref, parts in ((rows.at[0, yh, c], own_block(re, rm, 20.0)), (cols.at[yl, x], own_block(ce, cm, 0.0))):
        ref[0:B] = parts[0]
        ref[B : B + 16] = parts[2]
        ref[B + 16 :] = parts[1]

    def line_of(tail):
        tail = tail.astype(F32)
        return tail[0:1, : 2 * B] + tail[0:1, 2 * B :] + tail[1:2, : 2 * B]

    pl.semaphore_wait(barrier, len(partners))

    def part(s):
        return pl.ds(0, B + 16) if s == 0 else pl.ds(B + 16, B)

    def row_block(s, p, y):
        return rows.at[p, 1 - yh if y else yh, c, part(s)]

    def send_row(s, y, r, up):
        to = place_of(r - 1 if up else r + 1)
        send(row_block(s, place(r), y), row_block(s, to, y), r_row.at[s, to, y], to_zp if up else to_zm, s)

    def row_here(s, y, r):
        arrive(row_block(s, place_of(r), y), r_row.at[s, place_of(r), y])

    def row_step(s, y, d):
        for sign in (-1, 1):
            row_here(s, y, sign * d)
            if d < H - 1 or (y == 0 and sign < 0):
                send_row(s, y, sign * d, sign < 0)

    def row_y(s):
        row_here(s, 1, 0)
        send_row(s, 1, 0, True)
        send_row(s, 1, 0, False)

    def far_out(s):
        row_here(s, 0, H)
        send(row_block(s, NZ - 1, 0), row_block(s, NZ - 1, 0), r_row.at[s, NZ - 1, 1], to_yh, s)

    def row_core(s, j):
        ref = rows.at[pl.ds(2 * j, 2), :, c, part(s)]
        send(ref, ref, r_core.at[s, j], to_core, s, 4)

    def core_here(s, j):
        arrive(rows.at[pl.ds(2 * j, 2), :, oc, part(s)], r_core.at[s, j])

    def col_block(s, y, at):
        return cols.at[y, at, part(s)]

    def col_pair(s, at):
        return cols.at[:, at, part(s)]

    def col_y(s):
        arrive(col_block(s, 1 - yl, x), r_col.at[s, 0])
        send(col_pair(s, x), col_pair(s, x), r_col.at[s, 1], to_xp, s, 2)
        send(col_pair(s, x), col_pair(s, x), r_col.at[s, 2], to_xm, s, 2)

    def col_x(s):
        arrive(col_pair(s, xp), r_col.at[s, 2])
        send(col_block(s, yl, xp), col_block(s, yl, xp), r_col.at[s, 3], to_xm, s)
        arrive(col_pair(s, xm), r_col.at[s, 1])
        send(col_block(s, 1 - yl, xm), col_block(s, 1 - yl, xm), r_col.at[s, 4], to_xp, s)

    def all_cols(s):
        arrive(col_block(s, yl, x2), r_col.at[s, 3])
        arrive(col_block(s, 1 - yl, x2), r_col.at[s, 4])

    def halves(s, a, b):
        return jnp.concatenate([a[:, s * B : (s + 1) * B], b[:, s * B : (s + 1) * B]], axis=1)

    def col_lines():
        lines = [line_of(cols[r // XN, r % XN, B : B + 16]) for r in range(2 * XN)]
        for s in range(NS):
            for j in range(CN // 128):
                LC[s, :, j * 128 : (j + 1) * 128] = halves(s, lines[2 * j], lines[2 * j + 1])

    def lift(p):
        lines = [line_of(rows[p + q, y, k, B : B + 16]) for q in range(2) for y in range(2) for k in range(2)]
        wide = jnp.concatenate(lines, axis=0).T
        for i in range(8):
            for s in range(NS):
                column = wide[s * B : (s + 1) * B, i : i + 1]
                LRB[s, p + i // 4, i % 4 * B : (i % 4 + 1) * B, :] = jnp.broadcast_to(column, (B, 128))

    def turn(s):
        own = cols[:, :, s * (B + 16) : s * (B + 16) + B, :].reshape(CN, D)
        colsC[s] = own
        colsT[s] = (own * 0.5).T
        CPT[s] = jnp.zeros_like(CPT[s])

    def unit(s, p):
        pair = pl.ds(p, 2)
        left = rows[pair, :, :, pl.ds(pl.multiple_of(s * (B + 16), 16), B), :].reshape(8 * B, D)
        lr = LRB[s, pair].reshape(8 * B, 128)
        t = dot(left, colsT[s], NN) + jnp.concatenate([lr] * (CN // 128), axis=1) + LC[s]
        n = cnt[pl.ds(pl.multiple_of((s * NZ + p) * 4 * B, 8 * B), 8 * B), :].astype(F32)
        m = jnp.maximum(n, 1.0)
        root = m * lax.rsqrt(m)
        there = (0.4 + root) * (t - jnp.log(root))
        g = jnp.where(n > 0, there, jnp.tanh(t) + 1.0).astype(BF16)
        RP[s, pair] = dot(g, colsC[s], NN).reshape(2, 2, 2, B, D)
        CS[s, pair] = RP[s, pair, :, oc].astype(BF16)
        CPT[s] += dot(left.T, g, NN)

    def sums_here(s, j):
        arrive(CR.at[s, pl.ds(2 * j, 2)], r_cr.at[s, j])

    def chip_sum(s, r):
        return RP[s, place(r), :, c] + CR[s, place(r)].astype(F32)

    def half_sum(s, r, y):
        return RP[s, place(r), y, c] + CR[s, place(r), y].astype(F32)

    halves_in_turn = (1 - yh, yh)

    def ring(s, d):
        if d > 0:
            sums_here(s, d - 1)
        lanes_of = ((RSp, RRp, r_rp, to_zp, 1), (RSm, RRm, r_rm, to_zm, -1))
        if d == H:
            v = chip_sum(s, H)
            for half, (RS, RR, rr, dev, _) in enumerate(lanes_of):
                RS[s, H - 1, half] = v[half].astype(BF16)
                send(RS.at[s, H - 1, half], RR.at[s, H - 1, half], rr.at[s, H - 1, 0], dev, 1, 1)
        elif d == H - 1:
            for half, (RS, RR, rr, dev, sign) in enumerate(lanes_of):
                v = chip_sum(s, sign * d)
                arrive(RR.at[s, d, half], rr.at[s, d, 0])
                RS[s, d - 1, half] = (v[half] + RR[s, d, half].astype(F32)).astype(BF16)
                RS[s, d - 1, 1 - half] = v[1 - half].astype(BF16)
                send(RS.at[s, d - 1], RR.at[s, d - 1], rr.at[s, d - 1, 0], dev, 1, 2)
        elif d > 0 and s == 0:
            for RS, RR, rr, dev, sign in lanes_of:
                v = chip_sum(s, sign * d)
                arrive(RR.at[s, d], rr.at[s, d, 0])
                RS[s, d - 1] = (v + RR[s, d].astype(F32)).astype(BF16)
                send(RS.at[s, d - 1], RR.at[s, d - 1], rr.at[s, d - 1, 0], dev, 1, 2)
        elif d > 0:
            for k, y in enumerate(halves_in_turn):
                for RS, RR, rr, dev, sign in lanes_of:
                    if d < H - 2:
                        arrive(RR.at[s, d, y], rr.at[s, d, k])
                    elif k == 0:
                        arrive(RR.at[s, d], rr.at[s, d, 0])
                    RS[s, d - 1, y] = (half_sum(s, sign * d, y) + RR[s, d, y].astype(F32)).astype(BF16)
                    send(RS.at[s, d - 1, y], RR.at[s, d - 1, y], rr.at[s, d - 1, k], dev, 1, 1)
        else:
            for k, y in enumerate(halves_in_turn):
                for _, RR, rr, _, _ in lanes_of:
                    if s == 1:
                        arrive(RR.at[s, 0, y], rr.at[s, 0, k])
                    elif k == 0:
                        arrive(RR.at[s, 0], rr.at[s, 0, 0])
                v = half_sum(s, 0, y) + RRp[s, 0, y].astype(F32) + RRm[s, 0, y].astype(F32)
                if k == 0:
                    YS[s] = v.astype(BF16)
                    send(YS.at[s], YR.at[s], r_y.at[s], to_yh, 1, 1)
                else:
                    VR[s] = v

    def out_copy(k, s):
        src, dst = ((gr, nr), (gc, nc))[k]
        return pltpu.make_async_copy(src.at[s], dst.at[s], s_out.at[k, s])

    def rows_out(s):
        arrive(YR.at[s], r_y.at[s])
        gr[s] = 0.5 * (VR[s] + YR[s].astype(F32))
        out_copy(0, s).start()

    def col_far(s):
        CP[s] = CPT[s].T.reshape(2 * XN, B, D)
        Q1s[s, 0] = CP[s, yl * XN + x2].astype(BF16)
        send(Q1s.at[s, 0], Q1r.at[s, 0], r_q.at[s, 0], to_xp, 1, 1)
        Q1s[s, 1] = CP[s, (1 - yl) * XN + x2].astype(BF16)
        send(Q1s.at[s, 1], Q1r.at[s, 1], r_q.at[s, 1], to_xm, 1, 1)

    def col_near(s):
        arrive(Q1r.at[s, 0], r_q.at[s, 0])
        Q2s[s, 0, 0] = (CP[s, yl * XN + xp] + Q1r[s, 0].astype(F32)).astype(BF16)
        Q2s[s, 0, 1] = CP[s, (1 - yl) * XN + xp].astype(BF16)
        send(Q2s.at[s, 0], Q2r.at[s, 0], r_q.at[s, 2], to_xp, 1, 2)
        arrive(Q1r.at[s, 1], r_q.at[s, 1])
        Q2s[s, 1, 0] = CP[s, yl * XN + xm].astype(BF16)
        Q2s[s, 1, 1] = (CP[s, (1 - yl) * XN + xm] + Q1r[s, 1].astype(F32)).astype(BF16)
        send(Q2s.at[s, 1], Q2r.at[s, 1], r_q.at[s, 3], to_xm, 1, 2)

    def col_own(s):
        arrive(Q2r.at[s, 0], r_q.at[s, 2])
        arrive(Q2r.at[s, 1], r_q.at[s, 3])
        Q3s[s] = (CP[s, r_oth] + Q2r[s, 0, 1].astype(F32) + Q2r[s, 1, 1].astype(F32)).astype(BF16)
        send(Q3s.at[s], Q3r.at[s], r_q.at[s, 4], to_yl, 1, 1)
        VC[s] = CP[s, r_own] + Q2r[s, 0, 0].astype(F32) + Q2r[s, 1, 0].astype(F32)

    def cols_out(s):
        arrive(Q3r.at[s], r_q.at[s, 4])
        gc[s] = 0.5 * (VC[s] + Q3r[s].astype(F32))
        out_copy(1, s).start()

    for s in range(NS):
        send(col_block(s, yl, x), col_block(s, yl, x), r_col.at[s, 0], to_yl, s)
        send(row_block(s, 0, 0), row_block(s, 0, 0), r_row.at[s, 0, 1], to_yh, s)
        send_row(s, 0, 0, True)
        send_row(s, 0, 0, False)
    col_y(0)
    row_step(0, 0, 1)
    row_y(0)
    row_step(1, 0, 1)
    col_y(1)
    row_step(0, 0, 2)
    col_x(0)
    row_y(1)
    row_step(1, 0, 2)
    row_step(0, 1, 1)
    row_core(0, 0)
    col_x(1)
    row_step(0, 0, 3)
    row_step(1, 1, 1)
    row_core(1, 0)
    row_step(1, 0, 3)
    all_cols(0)
    col_lines()
    turn(0)
    row_step(0, 1, 2)
    row_core(0, 1)
    far_out(0)

    def before(i):
        if i > 0:
            counts_out(2 * i + 2, min(2 * i + 4, NS * NZ))
        if i == 0:
            core_here(0, 0)
            lift(0)
        if i == 1:
            row_step(1, 1, 2)
            row_core(1, 1)
            far_out(1)
            row_step(0, 1, 3)
            row_core(0, 2)
            core_here(0, 1)
            lift(2)
        if i == 2:
            row_here(0, 1, H)
            row_core(0, 3)
            row_step(1, 1, 3)
            row_core(1, 2)
            core_here(0, 2)
            lift(4)
        if i == 3:
            row_here(1, 1, H)
            row_core(1, 3)
            core_here(0, 3)
            lift(6)
        if i == 4:
            all_cols(1)
            turn(1)
            core_here(1, 3)
        if i == 5:
            ring(0, H)
            core_here(1, 2)
        if i == 6:
            ring(1, H)
            col_far(0)
            ring(0, 3)
            core_here(1, 1)
        if i == 7:
            ring(1, 3)
            col_near(0)
            ring(0, 2)
            core_here(1, 0)

    def step(i, carry):
        for k in range(2 * H):
            pl.when(i == k)(functools.partial(before, k))
        s, j = turn_of(i)
        p = 2 * j
        count_copy(2 * i).wait()
        count_copy(2 * i + 1).wait()
        unit(s, p)
        part = pl.ds(p, 2)
        send(CS.at[s, part], CR.at[s, part], r_cr.at[s, j], to_core, 1, 4 * 2 * H)
        return carry

    lax.fori_loop(0, 2 * H, step, 0)
    col_far(1)
    ring(1, 2)
    col_own(0)
    ring(0, 1)
    ring(1, 1)
    col_near(1)
    cols_out(0)
    ring(0, 0)
    ring(1, 0)
    col_own(1)
    rows_out(0)
    cols_out(1)
    rows_out(1)
    for k in range(2):
        for s in range(NS):
            out_copy(k, s).wait()
    arrive(cnt.at[pl.ds(0, total[0] * D * 2 // (CN * 4))], s_all)


def local(counts, re, ce, rm, cm, ra, ca, *, NZ, XN):
    S, B, D = re.shape
    CB = counts.shape[2]
    H = NZ // 2
    R = 2 * XN
    counts = counts.reshape(S, NZ, 4 * B, CB)
    sem = pltpu.SemaphoreType.DMA
    v = pltpu.VMEM
    scratch = [
        v((S, B, D), F32),
        v((S, B, D), F32),
        v((S, B), jnp.int32),
        v((S, B), jnp.int32),
        v((S * NZ * 4 * B, CB), jnp.int32),
        v((NZ, 2, 2, 2 * B + 16, D), BF16),
        v((2, XN, 2 * B + 16, D), BF16),
        v((S, D, CB), BF16),
        v((S, CB, D), BF16),
        v((S, NZ, 4 * B, 128), F32),
        v((S, 1, CB), F32),
        v((S, NZ, 2, 2, B, D), F32),
        v((S, D, CB), F32),
        v((S, R, B, D), F32),
        v((S, NZ, 2, B, D), BF16),
        v((S, NZ, 2, B, D), BF16),
        v((S, H, 2, B, D), BF16),
        v((S, H, 2, B, D), BF16),
        v((S, H, 2, B, D), BF16),
        v((S, H, 2, B, D), BF16),
        v((S, B, D), BF16),
        v((S, B, D), BF16),
        v((S, B, D), F32),
        v((S, 2, B, D), BF16),
        v((S, 2, B, D), BF16),
        v((S, 2, 2, B, D), BF16),
        v((S, 2, 2, B, D), BF16),
        v((S, B, D), BF16),
        v((S, B, D), BF16),
        v((S, B, D), F32),
        v((S, B, D), F32),
        v((S, B, D), F32),
        sem((4,)),
        sem((S * NZ,)),
        sem(()),
        sem((2, S)),
        sem((S, NZ, 2)),
        sem((S, H)),
        sem((S, 5)),
        sem((S, H)),
        sem((S, H, 2)),
        sem((S, H, 2)),
        sem((S,)),
        sem((S, 5)),
    ]
    gr, gc = pl.pallas_call(
        functools.partial(kernel, NZ, XN, B, D, CB),
        out_shape=(jax.ShapeDtypeStruct((S, B, D), F32), jax.ShapeDtypeStruct((S, B, D), F32)),
        in_specs=[pl.BlockSpec(memory_space=pltpu.HBM)] * 5,
        out_specs=(pl.BlockSpec(memory_space=pltpu.HBM),) * 2,
        scratch_shapes=scratch,
        compiler_params=pltpu.CompilerParams(
            collective_id=0, has_side_effects=True, vmem_limit_bytes=60 * 1024 * 1024
        ),
    )(counts, re, ce, rm, cm)
    return adagrad(re, ra, gr), adagrad(ce, ca, gc)


def solution(mesh):
    return jax.shard_map(
        functools.partial(local, NZ=mesh.shape["col"] // 4, XN=mesh.shape["row"] // 2),
        mesh=mesh,
        in_specs=(
            P(None, "row", "col"),
            P(None, ("row", "col"), None),
            P(None, ("col", "row"), None),
            P(None, ("row", "col")),
            P(None, ("col", "row")),
            P(None, ("row", "col"), None),
            P(None, ("col", "row"), None),
        ),
        out_specs=(P(None, ("row", "col"), None), P(None, ("col", "row"), None)),
        check_vma=False,
    )
```

```python
import functools

import jax
import jax.numpy as jnp
from jax import lax
from jax.experimental import pallas as pl
from jax.experimental.pallas import tpu as pltpu
from jax.sharding import PartitionSpec as P

MESH = pl.DeviceIdType.MESH
F32 = jnp.float32
BF16 = jnp.bfloat16
NT = (((1,), (1,)), ((), ()))
NN = (((1,), (0,)), ((), ()))
TN = (((0,), (0,)), ((), ()))


def dot(a, b, dims):
    return lax.dot_general(a, b, dims, preferred_element_type=F32)


def adagrad(w, a, g):
    return w - g / jnp.sqrt(a + g * g)


def kernel(
    NZ, XN, B, D, CN,
    counts, re_h, ce_h, rm_h, cm_h, nr, nc,
    re, ce, rm, cm,
    cnt, rows, cols, colsT, colsC, LRB, LC, RP, CPT, CP,
    CS, CR, RSp, RSm, RRp, RRm, YS, YR, VR, Q1s, Q1r, Q2s, Q2r, Q3s, Q3r, VC, gr, gc,
    s_in, s_cnt, s_all, s_out, r_row, r_core, r_col, r_cr, r_rp, r_rm, r_y, r_q,
):
    H = NZ // 2
    NS = 2
    row = lax.axis_index("row")
    col = lax.axis_index("col")
    x = lax.rem(row, XN)
    yl = row // XN
    z = col // 4
    yh = lax.rem(col // 2, 2)
    c = lax.rem(col, 2)
    oc = 1 - c
    xp = lax.rem(x + 1, XN)
    xm = lax.rem(x + XN - 1, XN)
    x2 = lax.rem(x + 2, XN)
    zp = lax.rem(z + 1, NZ)
    zm = lax.rem(z + NZ - 1, NZ)
    to_core = (row, col + 1 - 2 * c)
    to_yh = (row, col + 2 - 4 * yh)
    to_zp = (row, zp * 4 + yh * 2 + c)
    to_zm = (row, zm * 4 + yh * 2 + c)
    to_yl = ((1 - yl) * XN + x, col)
    to_xp = (yl * XN + xp, col)
    to_xm = (yl * XN + xm, col)
    r_own = yl * XN + x
    r_oth = (1 - yl) * XN + x

    def place(r):
        return 0 if r == 0 else 2 * r - 1 if r > 0 or r == -H else -2 * r

    def place_of(r):
        return place(H) if r == -H else place(r)

    def span(d):
        return (2 * d - 1, 2) if 0 < d < H else (place_of(d), 1)

    rel = [0]
    for d in range(1, H):
        rel += [d, -d]
    rel += [H]

    total = [0]

    def send(src, dst, rsem, dev, kind, count=1):
        pltpu.make_async_remote_copy(
            src_ref=src, dst_ref=dst, send_sem=s_all, recv_sem=rsem, device_id=dev, device_id_type=MESH
        ).start()
        total[0] += count * (B + 16 if kind == 0 else B)

    def arrive(dst, rsem):
        pltpu.make_async_copy(dst, dst, rsem).wait()

    own_in = [
        pltpu.make_async_copy(src, dst, s_in.at[i])
        for i, (src, dst) in enumerate(((rm_h, rm), (cm_h, cm), (re_h, re), (ce_h, ce)))
    ]
    for copy in own_in:
        copy.start()

    barrier = pltpu.get_barrier_semaphore()
    partners = [to_core, to_yh, to_zp, to_zm, to_yl, to_xp, to_xm]
    for dev in partners:
        pl.semaphore_signal(barrier, inc=1, device_id=dev, device_id_type=MESH)

    def turn_of(i):
        first, second, late = (i + 7) // 8, (i + 6) // 8, (i + 3) // 8
        return late + first - second, (1 - late) * (i - first) + late * (8 - i)

    def in_turn(u):
        s, j = turn_of(u // 2)
        return s * NZ + 2 * j + lax.rem(u, 2)

    def count_copy(u):
        q = in_turn(u)
        p = lax.rem(q, NZ)
        d = (p + 1) // 2
        zc = lax.rem(z + NZ + d * (2 * lax.rem(p, 2) - 1), NZ)
        at = pl.ds(pl.multiple_of(q * 4 * B, 4 * B), 4 * B)
        return pltpu.make_async_copy(counts.at[q // NZ, zc], cnt.at[at], s_cnt.at[q])

    def counts_out(lo, hi):
        for u in range(lo, hi):
            count_copy(u).start()

    counts_out(0, 3)

    for copy in own_in:
        copy.wait()

    def own_block(embed, margs, shift):
        line = jnp.concatenate([margs[0:1, :], margs[1:2, :]], axis=1).astype(F32)
        line = 0.5 * (jnp.log(line) - shift)
        hi = line.astype(BF16).astype(F32)
        mid = (line - hi).astype(BF16).astype(F32)
        upper = jnp.concatenate([hi, mid], axis=1)
        lower = jnp.concatenate([line - hi - mid, jnp.zeros_like(line)], axis=1)
        which = lax.broadcasted_iota(jnp.int32, (16, 4 * B), 0)
        tail = jnp.where(which == 0, upper, jnp.where(which == 1, lower, 0.0)).astype(BF16)
        return embed[0].astype(BF16), embed[1].astype(BF16), tail

    for ref, parts in ((rows.at[0, yh, c], own_block(re, rm, 20.0)), (cols.at[yl, x], own_block(ce, cm, 0.0))):
        ref[0:B] = parts[0]
        ref[B : B + 16] = parts[2]
        ref[B + 16 :] = parts[1]

    def line_of(tail):
        tail = tail.astype(F32)
        return tail[0:1, : 2 * B] + tail[0:1, 2 * B :] + tail[1:2, : 2 * B]

    pl.semaphore_wait(barrier, len(partners))

    def part(s):
        return pl.ds(0, B + 16) if s == 0 else pl.ds(B + 16, B)

    def row_block(s, p, y):
        return rows.at[p, 1 - yh if y else yh, c, part(s)]

    def send_row(s, y, r, up):
        to = place_of(r - 1 if up else r + 1)
        send(row_block(s, place(r), y), row_block(s, to, y), r_row.at[s, to, y], to_zp if up else to_zm, s)

    def row_here(s, y, r):
        arrive(row_block(s, place_of(r), y), r_row.at[s, place_of(r), y])

    def row_step(s, y, d):
        for sign in (-1, 1):
            row_here(s, y, sign * d)
            if d < H - 1 or (y == 0 and sign < 0):
                send_row(s, y, sign * d, sign < 0)

    def row_y(s):
        row_here(s, 1, 0)
        send_row(s, 1, 0, True)
        send_row(s, 1, 0, False)

    def far_out(s):
        row_here(s, 0, H)
        send(row_block(s, NZ - 1, 0), row_block(s, NZ - 1, 0), r_row.at[s, NZ - 1, 1], to_yh, s)

    def row_core(s, j):
        ref = rows.at[pl.ds(2 * j, 2), :, c, part(s)]
        send(ref, ref, r_core.at[s, j], to_core, s, 4)

    def core_here(s, j):
        arrive(rows.at[pl.ds(2 * j, 2), :, oc, part(s)], r_core.at[s, j])

    def col_block(s, y, at):
        return cols.at[y, at, part(s)]

    def col_pair(s, at):
        return cols.at[:, at, part(s)]

    def col_y(s):
        arrive(col_block(s, 1 - yl, x), r_col.at[s, 0])
        send(col_pair(s, x), col_pair(s, x), r_col.at[s, 1], to_xp, s, 2)
        send(col_pair(s, x), col_pair(s, x), r_col.at[s, 2], to_xm, s, 2)

    def col_x(s):
        arrive(col_pair(s, xp), r_col.at[s, 2])
        send(col_block(s, yl, xp), col_block(s, yl, xp), r_col.at[s, 3], to_xm, s)
        arrive(col_pair(s, xm), r_col.at[s, 1])
        send(col_block(s, 1 - yl, xm), col_block(s, 1 - yl, xm), r_col.at[s, 4], to_xp, s)

    def all_cols(s):
        arrive(col_block(s, yl, x2), r_col.at[s, 3])
        arrive(col_block(s, 1 - yl, x2), r_col.at[s, 4])

    def halves(s, a, b):
        return jnp.concatenate([a[:, s * B : (s + 1) * B], b[:, s * B : (s + 1) * B]], axis=1)

    def col_lines():
        lines = [line_of(cols[r // XN, r % XN, B : B + 16]) for r in range(2 * XN)]
        for s in range(NS):
            for j in range(CN // 128):
                LC[s, :, j * 128 : (j + 1) * 128] = halves(s, lines[2 * j], lines[2 * j + 1])

    def lift(p):
        lines = [line_of(rows[p + q, y, k, B : B + 16]) for q in range(2) for y in range(2) for k in range(2)]
        wide = jnp.concatenate(lines, axis=0).T
        for i in range(8):
            for s in range(NS):
                column = wide[s * B : (s + 1) * B, i : i + 1]
                LRB[s, p + i // 4, i % 4 * B : (i % 4 + 1) * B, :] = jnp.broadcast_to(column, (B, 128))

    def turn(s):
        own = cols[:, :, s * (B + 16) : s * (B + 16) + B, :].reshape(CN, D)
        colsC[s] = own
        colsT[s] = (own * 0.5).T
        CPT[s] = jnp.zeros_like(CPT[s])

    def unit(s, p):
        pair = pl.ds(p, 2)
        left = rows[pair, :, :, pl.ds(pl.multiple_of(s * (B + 16), 16), B), :].reshape(8 * B, D)
        lr = LRB[s, pair].reshape(8 * B, 128)
        t = dot(left, colsT[s], NN) + jnp.concatenate([lr] * (CN // 128), axis=1) + LC[s]
        n = cnt[pl.ds(pl.multiple_of((s * NZ + p) * 4 * B, 8 * B), 8 * B), :].astype(F32)
        m = jnp.maximum(n, 1.0)
        root = m * lax.rsqrt(m)
        there = (0.4 + root) * (t - jnp.log(root))
        g = jnp.where(n > 0, there, jnp.tanh(t) + 1.0).astype(BF16)
        RP[s, pair] = dot(g, colsC[s], NN).reshape(2, 2, 2, B, D)
        CS[s, pair] = RP[s, pair, :, oc].astype(BF16)
        CPT[s] += dot(left.T, g, NN)

    def sums_here(s, j):
        arrive(CR.at[s, pl.ds(2 * j, 2)], r_cr.at[s, j])

    def chip_sum(s, r):
        return RP[s, place(r), :, c] + CR[s, place(r)].astype(F32)

    def half_sum(s, r, y):
        return RP[s, place(r), y, c] + CR[s, place(r), y].astype(F32)

    halves_in_turn = (1 - yh, yh)

    def ring(s, d):
        if d > 0:
            sums_here(s, d - 1)
        lanes_of = ((RSp, RRp, r_rp, to_zp, 1), (RSm, RRm, r_rm, to_zm, -1))
        if d == H:
            v = chip_sum(s, H)
            for half, (RS, RR, rr, dev, _) in enumerate(lanes_of):
                RS[s, H - 1, half] = v[half].astype(BF16)
                send(RS.at[s, H - 1, half], RR.at[s, H - 1, half], rr.at[s, H - 1, 0], dev, 1, 1)
        elif d == H - 1:
            for half, (RS, RR, rr, dev, sign) in enumerate(lanes_of):
                v = chip_sum(s, sign * d)
                arrive(RR.at[s, d, half], rr.at[s, d, 0])
                RS[s, d - 1, half] = (v[half] + RR[s, d, half].astype(F32)).astype(BF16)
                RS[s, d - 1, 1 - half] = v[1 - half].astype(BF16)
                send(RS.at[s, d - 1], RR.at[s, d - 1], rr.at[s, d - 1, 0], dev, 1, 2)
        elif d > 0 and s == 0:
            for RS, RR, rr, dev, sign in lanes_of:
                v = chip_sum(s, sign * d)
                arrive(RR.at[s, d], rr.at[s, d, 0])
                RS[s, d - 1] = (v + RR[s, d].astype(F32)).astype(BF16)
                send(RS.at[s, d - 1], RR.at[s, d - 1], rr.at[s, d - 1, 0], dev, 1, 2)
        elif d > 0:
            for k, y in enumerate(halves_in_turn):
                for RS, RR, rr, dev, sign in lanes_of:
                    if d < H - 2:
                        arrive(RR.at[s, d, y], rr.at[s, d, k])
                    elif k == 0:
                        arrive(RR.at[s, d], rr.at[s, d, 0])
                    RS[s, d - 1, y] = (half_sum(s, sign * d, y) + RR[s, d, y].astype(F32)).astype(BF16)
                    send(RS.at[s, d - 1, y], RR.at[s, d - 1, y], rr.at[s, d - 1, k], dev, 1, 1)
        else:
            for k, y in enumerate(halves_in_turn):
                for _, RR, rr, _, _ in lanes_of:
                    if s == 1:
                        arrive(RR.at[s, 0, y], rr.at[s, 0, k])
                    elif k == 0:
                        arrive(RR.at[s, 0], rr.at[s, 0, 0])
                v = half_sum(s, 0, y) + RRp[s, 0, y].astype(F32) + RRm[s, 0, y].astype(F32)
                if k == 0:
                    YS[s] = v.astype(BF16)
                    send(YS.at[s], YR.at[s], r_y.at[s], to_yh, 1, 1)
                else:
                    VR[s] = v

    def out_copy(k, s):
        src, dst = ((gr, nr), (gc, nc))[k]
        return pltpu.make_async_copy(src.at[s], dst.at[s], s_out.at[k, s])

    def rows_out(s):
        arrive(YR.at[s], r_y.at[s])
        gr[s] = 0.5 * (VR[s] + YR[s].astype(F32))
        out_copy(0, s).start()

    def col_far(s):
        CP[s] = CPT[s].T.reshape(2 * XN, B, D)
        Q1s[s, 0] = CP[s, yl * XN + x2].astype(BF16)
        send(Q1s.at[s, 0], Q1r.at[s, 0], r_q.at[s, 0], to_xp, 1, 1)
        Q1s[s, 1] = CP[s, (1 - yl) * XN + x2].astype(BF16)
        send(Q1s.at[s, 1], Q1r.at[s, 1], r_q.at[s, 1], to_xm, 1, 1)

    def col_near(s):
        arrive(Q1r.at[s, 0], r_q.at[s, 0])
        Q2s[s, 0, 0] = (CP[s, yl * XN + xp] + Q1r[s, 0].astype(F32)).astype(BF16)
        Q2s[s, 0, 1] = CP[s, (1 - yl) * XN + xp].astype(BF16)
        send(Q2s.at[s, 0], Q2r.at[s, 0], r_q.at[s, 2], to_xp, 1, 2)
        arrive(Q1r.at[s, 1], r_q.at[s, 1])
        Q2s[s, 1, 0] = CP[s, yl * XN + xm].astype(BF16)
        Q2s[s, 1, 1] = (CP[s, (1 - yl) * XN + xm] + Q1r[s, 1].astype(F32)).astype(BF16)
        send(Q2s.at[s, 1], Q2r.at[s, 1], r_q.at[s, 3], to_xm, 1, 2)

    def col_own(s):
        arrive(Q2r.at[s, 0], r_q.at[s, 2])
        arrive(Q2r.at[s, 1], r_q.at[s, 3])
        Q3s[s] = (CP[s, r_oth] + Q2r[s, 0, 1].astype(F32) + Q2r[s, 1, 1].astype(F32)).astype(BF16)
        send(Q3s.at[s], Q3r.at[s], r_q.at[s, 4], to_yl, 1, 1)
        VC[s] = CP[s, r_own] + Q2r[s, 0, 0].astype(F32) + Q2r[s, 1, 0].astype(F32)

    def cols_out(s):
        arrive(Q3r.at[s], r_q.at[s, 4])
        gc[s] = 0.5 * (VC[s] + Q3r[s].astype(F32))
        out_copy(1, s).start()

    for s in range(NS):
        send(col_block(s, yl, x), col_block(s, yl, x), r_col.at[s, 0], to_yl, s)
        send(row_block(s, 0, 0), row_block(s, 0, 0), r_row.at[s, 0, 1], to_yh, s)
        send_row(s, 0, 0, True)
        send_row(s, 0, 0, False)
    row_step(0, 0, 1)
    col_y(0)
    row_y(0)
    row_step(1, 0, 1)
    col_y(1)
    counts_out(3, 6)
    row_step(0, 0, 2)
    row_y(1)
    row_step(1, 0, 2)
    row_step(0, 1, 1)
    row_core(0, 0)
    col_x(0)
    counts_out(6, 9)
    row_step(0, 0, 3)
    row_step(1, 1, 1)
    row_core(1, 0)
    col_x(1)
    row_step(1, 0, 3)
    row_step(0, 1, 2)
    row_core(0, 1)
    counts_out(9, 12)
    far_out(0)
    row_step(1, 1, 2)
    row_core(1, 1)
    all_cols(0)
    col_lines()
    turn(0)

    def before(i):
        if i == 0:
            core_here(0, 0)
            lift(0)
        if i == 1:
            counts_out(12, 16)
            far_out(1)
            all_cols(1)
            turn(1)
            core_here(1, 0)
        if i == 2:
            row_step(0, 1, 3)
            row_core(0, 2)
            core_here(0, 1)
            lift(2)
        if i == 3:
            row_step(1, 1, 3)
            row_core(1, 2)
            row_here(0, 1, H)
            row_core(0, 3)
            core_here(0, 2)
            lift(4)
        if i == 4:
            row_here(1, 1, H)
            row_core(1, 3)
            core_here(0, 3)
            lift(6)
        if i == 5:
            core_here(1, 3)
        if i == 6:
            ring(0, H)
            core_here(1, 2)
        if i == 7:
            ring(1, H)
            col_far(0)
            ring(0, 3)
            core_here(1, 1)

    def step(i, carry):
        for k in range(2 * H):
            pl.when(i == k)(functools.partial(before, k))
        s, j = turn_of(i)
        p = 2 * j
        count_copy(2 * i).wait()
        count_copy(2 * i + 1).wait()
        unit(s, p)
        part = pl.ds(p, 2)
        send(CS.at[s, part], CR.at[s, part], r_cr.at[s, j], to_core, 1, 4 * 2 * H)
        return carry

    lax.fori_loop(0, 2 * H, step, 0)
    ring(1, 3)
    col_near(0)
    ring(0, 2)
    col_far(1)
    ring(1, 2)
    col_own(0)
    ring(0, 1)
    col_near(1)
    ring(1, 1)
    cols_out(0)
    ring(0, 0)
    col_own(1)
    ring(1, 0)
    rows_out(0)
    cols_out(1)
    rows_out(1)
    for k in range(2):
        for s in range(NS):
            out_copy(k, s).wait()
    arrive(cnt.at[pl.ds(0, total[0] * D * 2 // (CN * 4))], s_all)


def local(counts, re, ce, rm, cm, ra, ca, *, NZ, XN):
    S, B, D = re.shape
    CB = counts.shape[2]
    H = NZ // 2
    R = 2 * XN
    counts = counts.reshape(S, NZ, 4 * B, CB)
    sem = pltpu.SemaphoreType.DMA
    v = pltpu.VMEM
    scratch = [
        v((S, B, D), F32),
        v((S, B, D), F32),
        v((S, B), jnp.int32),
        v((S, B), jnp.int32),
        v((S * NZ * 4 * B, CB), jnp.int32),
        v((NZ, 2, 2, 2 * B + 16, D), BF16),
        v((2, XN, 2 * B + 16, D), BF16),
        v((S, D, CB), BF16),
        v((S, CB, D), BF16),
        v((S, NZ, 4 * B, 128), F32),
        v((S, 1, CB), F32),
        v((S, NZ, 2, 2, B, D), F32),
        v((S, D, CB), F32),
        v((S, R, B, D), F32),
        v((S, NZ, 2, B, D), BF16),
        v((S, NZ, 2, B, D), BF16),
        v((S, H, 2, B, D), BF16),
        v((S, H, 2, B, D), BF16),
        v((S, H, 2, B, D), BF16),
        v((S, H, 2, B, D), BF16),
        v((S, B, D), BF16),
        v((S, B, D), BF16),
        v((S, B, D), F32),
        v((S, 2, B, D), BF16),
        v((S, 2, B, D), BF16),
        v((S, 2, 2, B, D), BF16),
        v((S, 2, 2, B, D), BF16),
        v((S, B, D), BF16),
        v((S, B, D), BF16),
        v((S, B, D), F32),
        v((S, B, D), F32),
        v((S, B, D), F32),
        sem((4,)),
        sem((S * NZ,)),
        sem(()),
        sem((2, S)),
        sem((S, NZ, 2)),
        sem((S, H)),
        sem((S, 5)),
        sem((S, H)),
        sem((S, H, 2)),
        sem((S, H, 2)),
        sem((S,)),
        sem((S, 5)),
    ]
    gr, gc = pl.pallas_call(
        functools.partial(kernel, NZ, XN, B, D, CB),
        out_shape=(jax.ShapeDtypeStruct((S, B, D), F32), jax.ShapeDtypeStruct((S, B, D), F32)),
        in_specs=[pl.BlockSpec(memory_space=pltpu.HBM)] * 5,
        out_specs=(pl.BlockSpec(memory_space=pltpu.HBM),) * 2,
        scratch_shapes=scratch,
        compiler_params=pltpu.CompilerParams(
            collective_id=0, has_side_effects=True, vmem_limit_bytes=60 * 1024 * 1024
        ),
    )(counts, re, ce, rm, cm)
    return adagrad(re, ra, gr), adagrad(ce, ca, gc)


def solution(mesh):
    return jax.shard_map(
        functools.partial(local, NZ=mesh.shape["col"] // 4, XN=mesh.shape["row"] // 2),
        mesh=mesh,
        in_specs=(
            P(None, "row", "col"),
            P(None, ("row", "col"), None),
            P(None, ("col", "row"), None),
            P(None, ("row", "col")),
            P(None, ("col", "row")),
            P(None, ("row", "col"), None),
            P(None, ("col", "row"), None),
        ),
        out_specs=(P(None, ("row", "col"), None), P(None, ("col", "row"), None)),
        check_vma=False,
    )
```

```python
import functools

import jax
import jax.numpy as jnp
from jax import lax
from jax.experimental import pallas as pl
from jax.experimental.pallas import tpu as pltpu
from jax.sharding import PartitionSpec as P

MESH = pl.DeviceIdType.MESH
F32 = jnp.float32
BF16 = jnp.bfloat16
NT = (((1,), (1,)), ((), ()))
NN = (((1,), (0,)), ((), ()))
TN = (((0,), (0,)), ((), ()))


def dot(a, b, dims):
    return lax.dot_general(a, b, dims, preferred_element_type=F32)


def adagrad(w, a, g):
    return w - g / jnp.sqrt(a + g * g)


def kernel(
    NZ, XN, B, D, CN,
    counts, re_h, ce_h, rm_h, cm_h, nr, nc,
    re, ce, rm, cm,
    cnt, rows, cols, colsT, colsC, LRB, LC, RP, CPT, CP,
    CS, CR, RSp, RSm, RRp, RRm, YS, YR, VR, Q1s, Q1r, Q2s, Q2r, Q3s, Q3r, VC, gr, gc,
    s_in, s_cnt, s_all, s_out, r_row, r_core, r_col, r_cr, r_rp, r_rm, r_y, r_q,
):
    H = NZ // 2
    NS = 2
    row = lax.axis_index("row")
    col = lax.axis_index("col")
    x = lax.rem(row, XN)
    yl = row // XN
    z = col // 4
    yh = lax.rem(col // 2, 2)
    c = lax.rem(col, 2)
    oc = 1 - c
    xp = lax.rem(x + 1, XN)
    xm = lax.rem(x + XN - 1, XN)
    x2 = lax.rem(x + 2, XN)
    zp = lax.rem(z + 1, NZ)
    zm = lax.rem(z + NZ - 1, NZ)
    to_core = (row, col + 1 - 2 * c)
    to_yh = (row, col + 2 - 4 * yh)
    to_zp = (row, zp * 4 + yh * 2 + c)
    to_zm = (row, zm * 4 + yh * 2 + c)
    to_yl = ((1 - yl) * XN + x, col)
    to_xp = (yl * XN + xp, col)
    to_xm = (yl * XN + xm, col)
    r_own = yl * XN + x
    r_oth = (1 - yl) * XN + x

    def place(r):
        return 0 if r == 0 else 2 * r - 1 if r > 0 or r == -H else -2 * r

    def place_of(r):
        return place(H) if r == -H else place(r)

    def span(d):
        return (2 * d - 1, 2) if 0 < d < H else (place_of(d), 1)

    rel = [0]
    for d in range(1, H):
        rel += [d, -d]
    rel += [H]

    total = [0]

    def send(src, dst, rsem, dev, kind, count=1):
        pltpu.make_async_remote_copy(
            src_ref=src, dst_ref=dst, send_sem=s_all, recv_sem=rsem, device_id=dev, device_id_type=MESH
        ).start()
        total[0] += count * (B + 16 if kind == 0 else B)

    def arrive(dst, rsem):
        pltpu.make_async_copy(dst, dst, rsem).wait()

    own_in = [
        pltpu.make_async_copy(src, dst, s_in.at[i])
        for i, (src, dst) in enumerate(((rm_h, rm), (cm_h, cm), (re_h, re), (ce_h, ce)))
    ]
    for copy in own_in:
        copy.start()

    barrier = pltpu.get_barrier_semaphore()
    partners = [to_core, to_yh, to_zp, to_zm, to_yl, to_xp, to_xm]
    for dev in partners:
        pl.semaphore_signal(barrier, inc=1, device_id=dev, device_id_type=MESH)

    def turn_of(i):
        first, second, late = (i + 7) // 8, (i + 6) // 8, (i + 3) // 8
        return late + first - second, (1 - late) * (i - first) + late * (8 - i)

    def in_turn(u):
        s, j = turn_of(u // 2)
        return s * NZ + 2 * j + lax.rem(u, 2)

    def count_copy(u):
        q = in_turn(u)
        p = lax.rem(q, NZ)
        d = (p + 1) // 2
        zc = lax.rem(z + NZ + d * (2 * lax.rem(p, 2) - 1), NZ)
        at = pl.ds(pl.multiple_of(q * 4 * B, 4 * B), 4 * B)
        return pltpu.make_async_copy(counts.at[q // NZ, zc], cnt.at[at], s_cnt.at[q])

    def counts_out(lo, hi):
        for u in range(lo, hi):
            count_copy(u).start()

    counts_out(0, 3)

    for copy in own_in:
        copy.wait()

    def own_block(embed, margs, shift):
        line = jnp.concatenate([margs[0:1, :], margs[1:2, :]], axis=1).astype(F32)
        line = 0.5 * (jnp.log(line) - shift)
        hi = line.astype(BF16).astype(F32)
        mid = (line - hi).astype(BF16).astype(F32)
        upper = jnp.concatenate([hi, mid], axis=1)
        lower = jnp.concatenate([line - hi - mid, jnp.zeros_like(line)], axis=1)
        which = lax.broadcasted_iota(jnp.int32, (16, 4 * B), 0)
        tail = jnp.where(which == 0, upper, jnp.where(which == 1, lower, 0.0)).astype(BF16)
        return embed[0].astype(BF16), embed[1].astype(BF16), tail

    for ref, parts in ((rows.at[0, yh, c], own_block(re, rm, 20.0)), (cols.at[yl, x], own_block(ce, cm, 0.0))):
        ref[0:B] = parts[0]
        ref[B : B + 16] = parts[2]
        ref[B + 16 :] = parts[1]

    def line_of(tail):
        tail = tail.astype(F32)
        return tail[0:1, : 2 * B] + tail[0:1, 2 * B :] + tail[1:2, : 2 * B]

    pl.semaphore_wait(barrier, len(partners))

    def part(s):
        return pl.ds(0, B + 16) if s == 0 else pl.ds(B + 16, B)

    def row_block(s, p, y):
        return rows.at[p, 1 - yh if y else yh, c, part(s)]

    def send_row(s, y, r, up):
        to = place_of(r - 1 if up else r + 1)
        send(row_block(s, place(r), y), row_block(s, to, y), r_row.at[s, to, y], to_zp if up else to_zm, s)

    def row_here(s, y, r):
        arrive(row_block(s, place_of(r), y), r_row.at[s, place_of(r), y])

    def row_step(s, y, d):
        for sign in (-1, 1):
            row_here(s, y, sign * d)
            if d < H - 1 or (y == 0 and sign < 0):
                send_row(s, y, sign * d, sign < 0)

    def row_y(s):
        row_here(s, 1, 0)
        send_row(s, 1, 0, True)
        send_row(s, 1, 0, False)

    def far_out(s):
        row_here(s, 0, H)
        send(row_block(s, NZ - 1, 0), row_block(s, NZ - 1, 0), r_row.at[s, NZ - 1, 1], to_yh, s)

    def row_core(s, j):
        ref = rows.at[pl.ds(2 * j, 2), :, c, part(s)]
        send(ref, ref, r_core.at[s, j], to_core, s, 4)

    def core_here(s, j):
        arrive(rows.at[pl.ds(2 * j, 2), :, oc, part(s)], r_core.at[s, j])

    def col_block(s, y, at):
        return cols.at[y, at, part(s)]

    def col_pair(s, at):
        return cols.at[:, at, part(s)]

    def col_y(s):
        arrive(col_block(s, 1 - yl, x), r_col.at[s, 0])
        send(col_pair(s, x), col_pair(s, x), r_col.at[s, 1], to_xp, s, 2)
        send(col_pair(s, x), col_pair(s, x), r_col.at[s, 2], to_xm, s, 2)

    def col_x(s):
        arrive(col_pair(s, xp), r_col.at[s, 2])
        send(col_block(s, yl, xp), col_block(s, yl, xp), r_col.at[s, 3], to_xm, s)
        arrive(col_pair(s, xm), r_col.at[s, 1])
        send(col_block(s, 1 - yl, xm), col_block(s, 1 - yl, xm), r_col.at[s, 4], to_xp, s)

    def all_cols(s):
        arrive(col_block(s, yl, x2), r_col.at[s, 3])
        arrive(col_block(s, 1 - yl, x2), r_col.at[s, 4])

    def halves(s, a, b):
        return jnp.concatenate([a[:, s * B : (s + 1) * B], b[:, s * B : (s + 1) * B]], axis=1)

    def col_lines():
        lines = [line_of(cols[r // XN, r % XN, B : B + 16]) for r in range(2 * XN)]
        for s in range(NS):
            for j in range(CN // 128):
                LC[s, :, j * 128 : (j + 1) * 128] = halves(s, lines[2 * j], lines[2 * j + 1])

    def lift(p):
        lines = [line_of(rows[p + q, y, k, B : B + 16]) for q in range(2) for y in range(2) for k in range(2)]
        wide = jnp.concatenate(lines, axis=0).T
        for i in range(8):
            for s in range(NS):
                column = wide[s * B : (s + 1) * B, i : i + 1]
                LRB[s, p + i // 4, i % 4 * B : (i % 4 + 1) * B, :] = jnp.broadcast_to(column, (B, 128))

    def turn(s):
        own = cols[:, :, s * (B + 16) : s * (B + 16) + B, :].reshape(CN, D)
        colsC[s] = own
        colsT[s] = (own * 0.5).T
        CPT[s] = jnp.zeros_like(CPT[s])

    def unit(s, p):
        pair = pl.ds(p, 2)
        left = rows[pair, :, :, pl.ds(pl.multiple_of(s * (B + 16), 16), B), :].reshape(8 * B, D)
        lr = LRB[s, pair].reshape(8 * B, 128)
        t = dot(left, colsT[s], NN) + jnp.concatenate([lr] * (CN // 128), axis=1) + LC[s]
        n = cnt[pl.ds(pl.multiple_of((s * NZ + p) * 4 * B, 8 * B), 8 * B), :].astype(F32)
        m = jnp.maximum(n, 1.0)
        root = m * lax.rsqrt(m)
        there = (0.4 + root) * (t - jnp.log(root))
        g = jnp.where(n > 0, there, jnp.tanh(t) + 1.0).astype(BF16)
        RP[s, pair] = dot(g, colsC[s], NN).reshape(2, 2, 2, B, D)
        CS[s, pair] = RP[s, pair, :, oc].astype(BF16)
        CPT[s] += dot(left.T, g, NN)

    def sums_here(s, j):
        arrive(CR.at[s, pl.ds(2 * j, 2)], r_cr.at[s, j])

    def chip_sum(s, r):
        return RP[s, place(r), :, c] + CR[s, place(r)].astype(F32)

    def half_sum(s, r, y):
        return RP[s, place(r), y, c] + CR[s, place(r), y].astype(F32)

    halves_in_turn = (1 - yh, yh)

    def ring(s, d):
        if d > 0:
            sums_here(s, d - 1)
        lanes_of = ((RSp, RRp, r_rp, to_zp, 1), (RSm, RRm, r_rm, to_zm, -1))
        if d == H:
            v = chip_sum(s, H)
            for half, (RS, RR, rr, dev, _) in enumerate(lanes_of):
                RS[s, H - 1, half] = v[half].astype(BF16)
                send(RS.at[s, H - 1, half], RR.at[s, H - 1, half], rr.at[s, H - 1, 0], dev, 1, 1)
        elif d == H - 1:
            for half, (RS, RR, rr, dev, sign) in enumerate(lanes_of):
                v = chip_sum(s, sign * d)
                arrive(RR.at[s, d, half], rr.at[s, d, 0])
                RS[s, d - 1, half] = (v[half] + RR[s, d, half].astype(F32)).astype(BF16)
                RS[s, d - 1, 1 - half] = v[1 - half].astype(BF16)
                send(RS.at[s, d - 1], RR.at[s, d - 1], rr.at[s, d - 1, 0], dev, 1, 2)
        elif d > 0 and s == 0:
            for RS, RR, rr, dev, sign in lanes_of:
                v = chip_sum(s, sign * d)
                arrive(RR.at[s, d], rr.at[s, d, 0])
                RS[s, d - 1] = (v + RR[s, d].astype(F32)).astype(BF16)
                send(RS.at[s, d - 1], RR.at[s, d - 1], rr.at[s, d - 1, 0], dev, 1, 2)
        elif d > 0:
            for k, y in enumerate(halves_in_turn):
                for RS, RR, rr, dev, sign in lanes_of:
                    if d < H - 2:
                        arrive(RR.at[s, d, y], rr.at[s, d, k])
                    elif k == 0:
                        arrive(RR.at[s, d], rr.at[s, d, 0])
                    RS[s, d - 1, y] = (half_sum(s, sign * d, y) + RR[s, d, y].astype(F32)).astype(BF16)
                    send(RS.at[s, d - 1, y], RR.at[s, d - 1, y], rr.at[s, d - 1, k], dev, 1, 1)
        else:
            for k, y in enumerate(halves_in_turn):
                for _, RR, rr, _, _ in lanes_of:
                    if s == 1:
                        arrive(RR.at[s, 0, y], rr.at[s, 0, k])
                    elif k == 0:
                        arrive(RR.at[s, 0], rr.at[s, 0, 0])
                v = half_sum(s, 0, y) + RRp[s, 0, y].astype(F32) + RRm[s, 0, y].astype(F32)
                if k == 0:
                    YS[s] = v.astype(BF16)
                    send(YS.at[s], YR.at[s], r_y.at[s], to_yh, 1, 1)
                else:
                    VR[s] = v

    def out_copy(k, s):
        src, dst = ((gr, nr), (gc, nc))[k]
        return pltpu.make_async_copy(src.at[s], dst.at[s], s_out.at[k, s])

    def rows_out(s):
        arrive(YR.at[s], r_y.at[s])
        gr[s] = 0.5 * (VR[s] + YR[s].astype(F32))
        out_copy(0, s).start()

    def col_far(s):
        CP[s] = CPT[s].T.reshape(2 * XN, B, D)
        Q1s[s, 0] = CP[s, yl * XN + x2].astype(BF16)
        send(Q1s.at[s, 0], Q1r.at[s, 0], r_q.at[s, 0], to_xp, 1, 1)
        Q1s[s, 1] = CP[s, (1 - yl) * XN + x2].astype(BF16)
        send(Q1s.at[s, 1], Q1r.at[s, 1], r_q.at[s, 1], to_xm, 1, 1)

    def col_near(s):
        arrive(Q1r.at[s, 0], r_q.at[s, 0])
        Q2s[s, 0, 0] = (CP[s, yl * XN + xp] + Q1r[s, 0].astype(F32)).astype(BF16)
        Q2s[s, 0, 1] = CP[s, (1 - yl) * XN + xp].astype(BF16)
        send(Q2s.at[s, 0], Q2r.at[s, 0], r_q.at[s, 2], to_xp, 1, 2)
        arrive(Q1r.at[s, 1], r_q.at[s, 1])
        Q2s[s, 1, 0] = CP[s, yl * XN + xm].astype(BF16)
        Q2s[s, 1, 1] = (CP[s, (1 - yl) * XN + xm] + Q1r[s, 1].astype(F32)).astype(BF16)
        send(Q2s.at[s, 1], Q2r.at[s, 1], r_q.at[s, 3], to_xm, 1, 2)

    def col_own(s):
        arrive(Q2r.at[s, 0], r_q.at[s, 2])
        arrive(Q2r.at[s, 1], r_q.at[s, 3])
        Q3s[s] = (CP[s, r_oth] + Q2r[s, 0, 1].astype(F32) + Q2r[s, 1, 1].astype(F32)).astype(BF16)
        send(Q3s.at[s], Q3r.at[s], r_q.at[s, 4], to_yl, 1, 1)
        VC[s] = CP[s, r_own] + Q2r[s, 0, 0].astype(F32) + Q2r[s, 1, 0].astype(F32)

    def cols_out(s):
        arrive(Q3r.at[s], r_q.at[s, 4])
        gc[s] = 0.5 * (VC[s] + Q3r[s].astype(F32))
        out_copy(1, s).start()

    for s in range(NS):
        send(col_block(s, yl, x), col_block(s, yl, x), r_col.at[s, 0], to_yl, s)
        send(row_block(s, 0, 0), row_block(s, 0, 0), r_row.at[s, 0, 1], to_yh, s)
        send_row(s, 0, 0, True)
        send_row(s, 0, 0, False)
    row_step(0, 0, 1)
    col_y(0)
    row_y(0)
    row_step(1, 0, 1)
    col_y(1)
    counts_out(3, 6)
    row_step(0, 0, 2)
    row_y(1)
    row_step(1, 0, 2)
    row_step(0, 1, 1)
    row_core(0, 0)
    col_x(0)
    counts_out(6, 9)
    row_step(0, 0, 3)
    row_step(1, 1, 1)
    row_core(1, 0)
    col_x(1)
    row_step(1, 0, 3)
    row_step(0, 1, 2)
    row_core(0, 1)
    counts_out(9, 12)
    far_out(0)
    row_step(1, 1, 2)
    row_core(1, 1)
    all_cols(0)
    col_lines()
    turn(0)

    def before(i):
        if i == 0:
            core_here(0, 0)
            lift(0)
        if i == 1:
            counts_out(12, 16)
            far_out(1)
            all_cols(1)
            turn(1)
            core_here(1, 0)
        if i == 2:
            row_step(0, 1, 3)
            row_core(0, 2)
            core_here(0, 1)
            lift(2)
        if i == 3:
            row_step(1, 1, 3)
            row_core(1, 2)
            row_here(0, 1, H)
            row_core(0, 3)
            core_here(0, 2)
            lift(4)
        if i == 4:
            row_here(1, 1, H)
            row_core(1, 3)
            core_here(0, 3)
            lift(6)
        if i == 5:
            core_here(1, 3)
        if i == 6:
            ring(0, H)
            core_here(1, 2)
        if i == 7:
            ring(1, H)
            col_far(0)
            ring(0, 3)
            core_here(1, 1)

    def step(i, carry):
        for k in range(2 * H):
            pl.when(i == k)(functools.partial(before, k))
        s, j = turn_of(i)
        p = 2 * j
        count_copy(2 * i).wait()
        count_copy(2 * i + 1).wait()
        unit(s, p)
        part = pl.ds(p, 2)
        send(CS.at[s, part], CR.at[s, part], r_cr.at[s, j], to_core, 1, 4 * 2 * H)
        return carry

    lax.fori_loop(0, 2 * H, step, 0)
    ring(1, 3)
    ring(0, 2)
    col_near(0)
    col_far(1)
    ring(1, 2)
    ring(0, 1)
    col_own(0)
    col_near(1)
    ring(1, 1)
    ring(0, 0)
    ring(1, 0)
    cols_out(0)
    col_own(1)
    rows_out(0)
    cols_out(1)
    rows_out(1)
    for k in range(2):
        for s in range(NS):
            out_copy(k, s).wait()
    arrive(cnt.at[pl.ds(0, total[0] * D * 2 // (CN * 4))], s_all)


def local(counts, re, ce, rm, cm, ra, ca, *, NZ, XN):
    S, B, D = re.shape
    CB = counts.shape[2]
    H = NZ // 2
    R = 2 * XN
    counts = counts.reshape(S, NZ, 4 * B, CB)
    sem = pltpu.SemaphoreType.DMA
    v = pltpu.VMEM
    scratch = [
        v((S, B, D), F32),
        v((S, B, D), F32),
        v((S, B), jnp.int32),
        v((S, B), jnp.int32),
        v((S * NZ * 4 * B, CB), jnp.int32),
        v((NZ, 2, 2, 2 * B + 16, D), BF16),
        v((2, XN, 2 * B + 16, D), BF16),
        v((S, D, CB), BF16),
        v((S, CB, D), BF16),
        v((S, NZ, 4 * B, 128), F32),
        v((S, 1, CB), F32),
        v((S, NZ, 2, 2, B, D), F32),
        v((S, D, CB), F32),
        v((S, R, B, D), F32),
        v((S, NZ, 2, B, D), BF16),
        v((S, NZ, 2, B, D), BF16),
        v((S, H, 2, B, D), BF16),
        v((S, H, 2, B, D), BF16),
        v((S, H, 2, B, D), BF16),
        v((S, H, 2, B, D), BF16),
        v((S, B, D), BF16),
        v((S, B, D), BF16),
        v((S, B, D), F32),
        v((S, 2, B, D), BF16),
        v((S, 2, B, D), BF16),
        v((S, 2, 2, B, D), BF16),
        v((S, 2, 2, B, D), BF16),
        v((S, B, D), BF16),
        v((S, B, D), BF16),
        v((S, B, D), F32),
        v((S, B, D), F32),
        v((S, B, D), F32),
        sem((4,)),
        sem((S * NZ,)),
        sem(()),
        sem((2, S)),
        sem((S, NZ, 2)),
        sem((S, H)),
        sem((S, 5)),
        sem((S, H)),
        sem((S, H, 2)),
        sem((S, H, 2)),
        sem((S,)),
        sem((S, 5)),
    ]
    gr, gc = pl.pallas_call(
        functools.partial(kernel, NZ, XN, B, D, CB),
        out_shape=(jax.ShapeDtypeStruct((S, B, D), F32), jax.ShapeDtypeStruct((S, B, D), F32)),
        in_specs=[pl.BlockSpec(memory_space=pltpu.HBM)] * 5,
        out_specs=(pl.BlockSpec(memory_space=pltpu.HBM),) * 2,
        scratch_shapes=scratch,
        compiler_params=pltpu.CompilerParams(
            collective_id=0, has_side_effects=True, vmem_limit_bytes=60 * 1024 * 1024
        ),
    )(counts, re, ce, rm, cm)
    return adagrad(re, ra, gr), adagrad(ce, ca, gc)


def solution(mesh):
    return jax.shard_map(
        functools.partial(local, NZ=mesh.shape["col"] // 4, XN=mesh.shape["row"] // 2),
        mesh=mesh,
        in_specs=(
            P(None, "row", "col"),
            P(None, ("row", "col"), None),
            P(None, ("col", "row"), None),
            P(None, ("row", "col")),
            P(None, ("col", "row")),
            P(None, ("row", "col"), None),
            P(None, ("col", "row"), None),
        ),
        out_specs=(P(None, ("row", "col"), None), P(None, ("col", "row"), None)),
        check_vma=False,
    )
```

```python
import functools

import jax
import jax.numpy as jnp
from jax import lax
from jax.experimental import pallas as pl
from jax.experimental.pallas import tpu as pltpu
from jax.sharding import PartitionSpec as P

MESH = pl.DeviceIdType.MESH
F32 = jnp.float32
BF16 = jnp.bfloat16
NT = (((1,), (1,)), ((), ()))
NN = (((1,), (0,)), ((), ()))
TN = (((0,), (0,)), ((), ()))


def dot(a, b, dims):
    return lax.dot_general(a, b, dims, preferred_element_type=F32)


def adagrad(w, a, g):
    return w - g / jnp.sqrt(a + g * g)


def kernel(
    NZ, XN, B, D, CN,
    counts, re_h, ce_h, rm_h, cm_h, nr, nc,
    re, ce, rm, cm,
    cnt, rows, cols, colsT, colsC, LRB, LC, RP, CPT, CP,
    CS, CR, RSp, RSm, RRp, RRm, YS, YR, VR, Q1s, Q1r, Q2s, Q2r, Q3s, Q3r, VC, gr, gc,
    s_in, s_cnt, s_all, s_out, r_row, r_core, r_col, r_cr, r_rp, r_rm, r_y, r_q,
):
    H = NZ // 2
    NS = 2
    row = lax.axis_index("row")
    col = lax.axis_index("col")
    x = lax.rem(row, XN)
    yl = row // XN
    z = col // 4
    yh = lax.rem(col // 2, 2)
    c = lax.rem(col, 2)
    oc = 1 - c
    xp = lax.rem(x + 1, XN)
    xm = lax.rem(x + XN - 1, XN)
    x2 = lax.rem(x + 2, XN)
    zp = lax.rem(z + 1, NZ)
    zm = lax.rem(z + NZ - 1, NZ)
    to_core = (row, col + 1 - 2 * c)
    to_yh = (row, col + 2 - 4 * yh)
    to_zp = (row, zp * 4 + yh * 2 + c)
    to_zm = (row, zm * 4 + yh * 2 + c)
    to_yl = ((1 - yl) * XN + x, col)
    to_xp = (yl * XN + xp, col)
    to_xm = (yl * XN + xm, col)
    r_own = yl * XN + x
    r_oth = (1 - yl) * XN + x

    def place(r):
        return 0 if r == 0 else 2 * r - 1 if r > 0 or r == -H else -2 * r

    def place_of(r):
        return place(H) if r == -H else place(r)

    def span(d):
        return (2 * d - 1, 2) if 0 < d < H else (place_of(d), 1)

    rel = [0]
    for d in range(1, H):
        rel += [d, -d]
    rel += [H]

    total = [0]

    def send(src, dst, rsem, dev, kind, count=1):
        pltpu.make_async_remote_copy(
            src_ref=src, dst_ref=dst, send_sem=s_all, recv_sem=rsem, device_id=dev, device_id_type=MESH
        ).start()
        total[0] += count * (B + 16 if kind == 0 else B)

    def arrive(dst, rsem):
        pltpu.make_async_copy(dst, dst, rsem).wait()

    own_in = [
        pltpu.make_async_copy(src, dst, s_in.at[i])
        for i, (src, dst) in enumerate(((rm_h, rm), (cm_h, cm), (re_h, re), (ce_h, ce)))
    ]
    for copy in own_in:
        copy.start()

    barrier = pltpu.get_barrier_semaphore()
    partners = [to_core, to_yh, to_zp, to_zm, to_yl, to_xp, to_xm]
    for dev in partners:
        pl.semaphore_signal(barrier, inc=1, device_id=dev, device_id_type=MESH)

    def turn_of(i):
        first, second, late = (i + 7) // 8, (i + 6) // 8, (i + 3) // 8
        return late + first - second, (1 - late) * (i - first) + late * (8 - i)

    def in_turn(u):
        s, j = turn_of(u // 2)
        return s * NZ + 2 * j + lax.rem(u, 2)

    def count_copy(u):
        q = in_turn(u)
        p = lax.rem(q, NZ)
        d = (p + 1) // 2
        zc = lax.rem(z + NZ + d * (2 * lax.rem(p, 2) - 1), NZ)
        at = pl.ds(pl.multiple_of(q * 4 * B, 4 * B), 4 * B)
        return pltpu.make_async_copy(counts.at[q // NZ, zc], cnt.at[at], s_cnt.at[q])

    def counts_out(lo, hi):
        for u in range(lo, hi):
            count_copy(u).start()

    counts_out(0, 3)

    for copy in own_in:
        copy.wait()

    def own_block(embed, margs, shift):
        line = jnp.concatenate([margs[0:1, :], margs[1:2, :]], axis=1).astype(F32)
        line = 0.5 * (jnp.log(line) - shift)
        hi = line.astype(BF16).astype(F32)
        mid = (line - hi).astype(BF16).astype(F32)
        upper = jnp.concatenate([hi, mid], axis=1)
        lower = jnp.concatenate([line - hi - mid, jnp.zeros_like(line)], axis=1)
        which = lax.broadcasted_iota(jnp.int32, (16, 4 * B), 0)
        tail = jnp.where(which == 0, upper, jnp.where(which == 1, lower, 0.0)).astype(BF16)
        return embed[0].astype(BF16), embed[1].astype(BF16), tail

    def store_block(ref, parts):
        ref[0:B] = parts[0]
        ref[B : B + 16] = parts[2]
        ref[B + 16 :] = parts[1]

    store_block(rows.at[0, yh, c], own_block(re, rm, 20.0))

    def line_of(tail):
        tail = tail.astype(F32)
        return tail[0:1, : 2 * B] + tail[0:1, 2 * B :] + tail[1:2, : 2 * B]

    pl.semaphore_wait(barrier, len(partners))

    def part(s):
        return pl.ds(0, B + 16) if s == 0 else pl.ds(B + 16, B)

    def row_block(s, p, y):
        return rows.at[p, 1 - yh if y else yh, c, part(s)]

    def send_row(s, y, r, up):
        to = place_of(r - 1 if up else r + 1)
        send(row_block(s, place(r), y), row_block(s, to, y), r_row.at[s, to, y], to_zp if up else to_zm, s)

    def row_here(s, y, r):
        arrive(row_block(s, place_of(r), y), r_row.at[s, place_of(r), y])

    def row_step(s, y, d):
        for sign in (-1, 1):
            row_here(s, y, sign * d)
            if d < H - 1 or (y == 0 and sign < 0):
                send_row(s, y, sign * d, sign < 0)

    def row_y(s):
        row_here(s, 1, 0)
        send_row(s, 1, 0, True)
        send_row(s, 1, 0, False)

    def far_out(s):
        row_here(s, 0, H)
        send(row_block(s, NZ - 1, 0), row_block(s, NZ - 1, 0), r_row.at[s, NZ - 1, 1], to_yh, s)

    def row_core(s, j):
        ref = rows.at[pl.ds(2 * j, 2), :, c, part(s)]
        send(ref, ref, r_core.at[s, j], to_core, s, 4)

    def core_here(s, j):
        arrive(rows.at[pl.ds(2 * j, 2), :, oc, part(s)], r_core.at[s, j])

    def col_block(s, y, at):
        return cols.at[y, at, part(s)]

    def col_pair(s, at):
        return cols.at[:, at, part(s)]

    def col_y(s):
        arrive(col_block(s, 1 - yl, x), r_col.at[s, 0])
        send(col_pair(s, x), col_pair(s, x), r_col.at[s, 1], to_xp, s, 2)
        send(col_pair(s, x), col_pair(s, x), r_col.at[s, 2], to_xm, s, 2)

    def col_x(s):
        arrive(col_pair(s, xp), r_col.at[s, 2])
        send(col_block(s, yl, xp), col_block(s, yl, xp), r_col.at[s, 3], to_xm, s)
        arrive(col_pair(s, xm), r_col.at[s, 1])
        send(col_block(s, 1 - yl, xm), col_block(s, 1 - yl, xm), r_col.at[s, 4], to_xp, s)

    def all_cols(s):
        arrive(col_block(s, yl, x2), r_col.at[s, 3])
        arrive(col_block(s, 1 - yl, x2), r_col.at[s, 4])

    def halves(s, a, b):
        return jnp.concatenate([a[:, s * B : (s + 1) * B], b[:, s * B : (s + 1) * B]], axis=1)

    def col_lines():
        lines = [line_of(cols[r // XN, r % XN, B : B + 16]) for r in range(2 * XN)]
        for s in range(NS):
            for j in range(CN // 128):
                LC[s, :, j * 128 : (j + 1) * 128] = halves(s, lines[2 * j], lines[2 * j + 1])

    def lift(p):
        lines = [line_of(rows[p + q, y, k, B : B + 16]) for q in range(2) for y in range(2) for k in range(2)]
        wide = jnp.concatenate(lines, axis=0).T
        for i in range(8):
            for s in range(NS):
                column = wide[s * B : (s + 1) * B, i : i + 1]
                LRB[s, p + i // 4, i % 4 * B : (i % 4 + 1) * B, :] = jnp.broadcast_to(column, (B, 128))

    def turn(s):
        own = cols[:, :, s * (B + 16) : s * (B + 16) + B, :].reshape(CN, D)
        colsC[s] = own
        colsT[s] = (own * 0.5).T
        CPT[s] = jnp.zeros_like(CPT[s])

    def unit(s, p):
        pair = pl.ds(p, 2)
        left = rows[pair, :, :, pl.ds(pl.multiple_of(s * (B + 16), 16), B), :].reshape(8 * B, D)
        lr = LRB[s, pair].reshape(8 * B, 128)
        t = dot(left, colsT[s], NN) + jnp.concatenate([lr] * (CN // 128), axis=1) + LC[s]
        n = cnt[pl.ds(pl.multiple_of((s * NZ + p) * 4 * B, 8 * B), 8 * B), :].astype(F32)
        m = jnp.maximum(n, 1.0)
        root = m * lax.rsqrt(m)
        there = (0.4 + root) * (t - jnp.log(root))
        g = jnp.where(n > 0, there, jnp.tanh(t) + 1.0).astype(BF16)
        RP[s, pair] = dot(g, colsC[s], NN).reshape(2, 2, 2, B, D)
        CS[s, pair] = RP[s, pair, :, oc].astype(BF16)
        CPT[s] += dot(left.T, g, NN)

    def sums_here(s, j):
        arrive(CR.at[s, pl.ds(2 * j, 2)], r_cr.at[s, j])

    def chip_sum(s, r):
        return RP[s, place(r), :, c] + CR[s, place(r)].astype(F32)

    def half_sum(s, r, y):
        return RP[s, place(r), y, c] + CR[s, place(r), y].astype(F32)

    halves_in_turn = (1 - yh, yh)

    def ring(s, d):
        if d > 0:
            sums_here(s, d - 1)
        lanes_of = ((RSp, RRp, r_rp, to_zp, 1), (RSm, RRm, r_rm, to_zm, -1))
        if d == H:
            v = chip_sum(s, H)
            for half, (RS, RR, rr, dev, _) in enumerate(lanes_of):
                RS[s, H - 1, half] = v[half].astype(BF16)
                send(RS.at[s, H - 1, half], RR.at[s, H - 1, half], rr.at[s, H - 1, 0], dev, 1, 1)
        elif d == H - 1:
            for half, (RS, RR, rr, dev, sign) in enumerate(lanes_of):
                v = chip_sum(s, sign * d)
                arrive(RR.at[s, d, half], rr.at[s, d, 0])
                RS[s, d - 1, half] = (v[half] + RR[s, d, half].astype(F32)).astype(BF16)
                RS[s, d - 1, 1 - half] = v[1 - half].astype(BF16)
                send(RS.at[s, d - 1], RR.at[s, d - 1], rr.at[s, d - 1, 0], dev, 1, 2)
        elif d > 0 and s == 0:
            for RS, RR, rr, dev, sign in lanes_of:
                v = chip_sum(s, sign * d)
                arrive(RR.at[s, d], rr.at[s, d, 0])
                RS[s, d - 1] = (v + RR[s, d].astype(F32)).astype(BF16)
                send(RS.at[s, d - 1], RR.at[s, d - 1], rr.at[s, d - 1, 0], dev, 1, 2)
        elif d > 0:
            for k, y in enumerate(halves_in_turn):
                for RS, RR, rr, dev, sign in lanes_of:
                    if d < H - 2:
                        arrive(RR.at[s, d, y], rr.at[s, d, k])
                    elif k == 0:
                        arrive(RR.at[s, d], rr.at[s, d, 0])
                    RS[s, d - 1, y] = (half_sum(s, sign * d, y) + RR[s, d, y].astype(F32)).astype(BF16)
                    send(RS.at[s, d - 1, y], RR.at[s, d - 1, y], rr.at[s, d - 1, k], dev, 1, 1)
        else:
            for k, y in enumerate(halves_in_turn):
                for _, RR, rr, _, _ in lanes_of:
                    if s == 1:
                        arrive(RR.at[s, 0, y], rr.at[s, 0, k])
                    elif k == 0:
                        arrive(RR.at[s, 0], rr.at[s, 0, 0])
                v = half_sum(s, 0, y) + RRp[s, 0, y].astype(F32) + RRm[s, 0, y].astype(F32)
                if k == 0:
                    YS[s] = v.astype(BF16)
                    send(YS.at[s], YR.at[s], r_y.at[s], to_yh, 1, 1)
                else:
                    VR[s] = v

    def out_copy(k, s):
        src, dst = ((gr, nr), (gc, nc))[k]
        return pltpu.make_async_copy(src.at[s], dst.at[s], s_out.at[k, s])

    def rows_out(s):
        arrive(YR.at[s], r_y.at[s])
        gr[s] = 0.5 * (VR[s] + YR[s].astype(F32))
        out_copy(0, s).start()

    def col_far(s):
        CP[s] = CPT[s].T.reshape(2 * XN, B, D)
        Q1s[s, 0] = CP[s, yl * XN + x2].astype(BF16)
        send(Q1s.at[s, 0], Q1r.at[s, 0], r_q.at[s, 0], to_xp, 1, 1)
        Q1s[s, 1] = CP[s, (1 - yl) * XN + x2].astype(BF16)
        send(Q1s.at[s, 1], Q1r.at[s, 1], r_q.at[s, 1], to_xm, 1, 1)

    def col_near(s):
        arrive(Q1r.at[s, 0], r_q.at[s, 0])
        Q2s[s, 0, 0] = (CP[s, yl * XN + xp] + Q1r[s, 0].astype(F32)).astype(BF16)
        Q2s[s, 0, 1] = CP[s, (1 - yl) * XN + xp].astype(BF16)
        send(Q2s.at[s, 0], Q2r.at[s, 0], r_q.at[s, 2], to_xp, 1, 2)
        arrive(Q1r.at[s, 1], r_q.at[s, 1])
        Q2s[s, 1, 0] = CP[s, yl * XN + xm].astype(BF16)
        Q2s[s, 1, 1] = (CP[s, (1 - yl) * XN + xm] + Q1r[s, 1].astype(F32)).astype(BF16)
        send(Q2s.at[s, 1], Q2r.at[s, 1], r_q.at[s, 3], to_xm, 1, 2)

    def col_own(s):
        arrive(Q2r.at[s, 0], r_q.at[s, 2])
        arrive(Q2r.at[s, 1], r_q.at[s, 3])
        Q3s[s] = (CP[s, r_oth] + Q2r[s, 0, 1].astype(F32) + Q2r[s, 1, 1].astype(F32)).astype(BF16)
        send(Q3s.at[s], Q3r.at[s], r_q.at[s, 4], to_yl, 1, 1)
        VC[s] = CP[s, r_own] + Q2r[s, 0, 0].astype(F32) + Q2r[s, 1, 0].astype(F32)

    def cols_out(s):
        arrive(Q3r.at[s], r_q.at[s, 4])
        gc[s] = 0.5 * (VC[s] + Q3r[s].astype(F32))
        out_copy(1, s).start()

    for s in range(NS):
        send(row_block(s, 0, 0), row_block(s, 0, 0), r_row.at[s, 0, 1], to_yh, s)
        send_row(s, 0, 0, True)
        send_row(s, 0, 0, False)
        if s == 0:
            store_block(cols.at[yl, x], own_block(ce, cm, 0.0))
        send(col_block(s, yl, x), col_block(s, yl, x), r_col.at[s, 0], to_yl, s)
    row_step(0, 0, 1)
    col_y(0)
    row_y(0)
    row_step(1, 0, 1)
    col_y(1)
    counts_out(3, 6)
    row_step(0, 0, 2)
    row_y(1)
    row_step(1, 0, 2)
    row_step(0, 1, 1)
    row_core(0, 0)
    col_x(0)
    counts_out(6, 9)
    row_step(0, 0, 3)
    row_step(1, 1, 1)
    row_core(1, 0)
    col_x(1)
    row_step(1, 0, 3)
    row_step(0, 1, 2)
    row_core(0, 1)
    counts_out(9, 12)
    far_out(0)
    row_step(1, 1, 2)
    row_core(1, 1)
    all_cols(0)
    col_lines()
    turn(0)

    def before(i):
        if i == 0:
            core_here(0, 0)
            lift(0)
        if i == 1:
            counts_out(12, 16)
            far_out(1)
            all_cols(1)
            turn(1)
            core_here(1, 0)
        if i == 2:
            row_step(0, 1, 3)
            row_core(0, 2)
            core_here(0, 1)
            lift(2)
        if i == 3:
            row_step(1, 1, 3)
            row_core(1, 2)
            row_here(0, 1, H)
            row_core(0, 3)
            core_here(0, 2)
            lift(4)
        if i == 4:
            row_here(1, 1, H)
            row_core(1, 3)
            core_here(0, 3)
            lift(6)
        if i == 5:
            core_here(1, 3)
        if i == 6:
            ring(0, H)
            core_here(1, 2)
        if i == 7:
            ring(1, H)
            col_far(0)
            ring(0, 3)
            core_here(1, 1)

    def step(i, carry):
        for k in range(2 * H):
            pl.when(i == k)(functools.partial(before, k))
        s, j = turn_of(i)
        p = 2 * j
        count_copy(2 * i).wait()
        count_copy(2 * i + 1).wait()
        unit(s, p)
        part = pl.ds(p, 2)
        send(CS.at[s, part], CR.at[s, part], r_cr.at[s, j], to_core, 1, 4 * 2 * H)
        return carry

    lax.fori_loop(0, 2 * H, step, 0)
    ring(1, 3)
    col_near(0)
    ring(0, 2)
    col_far(1)
    ring(1, 2)
    col_own(0)
    ring(0, 1)
    col_near(1)
    ring(1, 1)
    cols_out(0)
    ring(0, 0)
    col_own(1)
    ring(1, 0)
    rows_out(0)
    cols_out(1)
    rows_out(1)
    for k in range(2):
        for s in range(NS):
            out_copy(k, s).wait()
    arrive(cnt.at[pl.ds(0, total[0] * D * 2 // (CN * 4))], s_all)


def local(counts, re, ce, rm, cm, ra, ca, *, NZ, XN):
    S, B, D = re.shape
    CB = counts.shape[2]
    H = NZ // 2
    R = 2 * XN
    counts = counts.reshape(S, NZ, 4 * B, CB)
    sem = pltpu.SemaphoreType.DMA
    v = pltpu.VMEM
    scratch = [
        v((S, B, D), F32),
        v((S, B, D), F32),
        v((S, B), jnp.int32),
        v((S, B), jnp.int32),
        v((S * NZ * 4 * B, CB), jnp.int32),
        v((NZ, 2, 2, 2 * B + 16, D), BF16),
        v((2, XN, 2 * B + 16, D), BF16),
        v((S, D, CB), BF16),
        v((S, CB, D), BF16),
        v((S, NZ, 4 * B, 128), F32),
        v((S, 1, CB), F32),
        v((S, NZ, 2, 2, B, D), F32),
        v((S, D, CB), F32),
        v((S, R, B, D), F32),
        v((S, NZ, 2, B, D), BF16),
        v((S, NZ, 2, B, D), BF16),
        v((S, H, 2, B, D), BF16),
        v((S, H, 2, B, D), BF16),
        v((S, H, 2, B, D), BF16),
        v((S, H, 2, B, D), BF16),
        v((S, B, D), BF16),
        v((S, B, D), BF16),
        v((S, B, D), F32),
        v((S, 2, B, D), BF16),
        v((S, 2, B, D), BF16),
        v((S, 2, 2, B, D), BF16),
        v((S, 2, 2, B, D), BF16),
        v((S, B, D), BF16),
        v((S, B, D), BF16),
        v((S, B, D), F32),
        v((S, B, D), F32),
        v((S, B, D), F32),
        sem((4,)),
        sem((S * NZ,)),
        sem(()),
        sem((2, S)),
        sem((S, NZ, 2)),
        sem((S, H)),
        sem((S, 5)),
        sem((S, H)),
        sem((S, H, 2)),
        sem((S, H, 2)),
        sem((S,)),
        sem((S, 5)),
    ]
    gr, gc = pl.pallas_call(
        functools.partial(kernel, NZ, XN, B, D, CB),
        out_shape=(jax.ShapeDtypeStruct((S, B, D), F32), jax.ShapeDtypeStruct((S, B, D), F32)),
        in_specs=[pl.BlockSpec(memory_space=pltpu.HBM)] * 5,
        out_specs=(pl.BlockSpec(memory_space=pltpu.HBM),) * 2,
        scratch_shapes=scratch,
        compiler_params=pltpu.CompilerParams(
            collective_id=0, has_side_effects=True, vmem_limit_bytes=60 * 1024 * 1024
        ),
    )(counts, re, ce, rm, cm)
    return adagrad(re, ra, gr), adagrad(ce, ca, gc)


def solution(mesh):
    return jax.shard_map(
        functools.partial(local, NZ=mesh.shape["col"] // 4, XN=mesh.shape["row"] // 2),
        mesh=mesh,
        in_specs=(
            P(None, "row", "col"),
            P(None, ("row", "col"), None),
            P(None, ("col", "row"), None),
            P(None, ("row", "col")),
            P(None, ("col", "row")),
            P(None, ("row", "col"), None),
            P(None, ("col", "row"), None),
        ),
        out_specs=(P(None, ("row", "col"), None), P(None, ("col", "row"), None)),
        check_vma=False,
    )
```
